32 devices in a mesh: crop: 2 (over x), row: 8 (over z, y), col: 2 (over core).
Axes of the slice: x: 2, y: 2, z: 4, core: 2. Of those that a mesh axis runs over, the one named last changes fastest.
Arguments:
- pair_rep: bfloat16 [96, 48, 128], P(('crop', 'row'), 'col'), parts along dimension 0, may hold values from -6 to 6
- cotangent: bfloat16 [96, 48, 128], P(('crop', 'row'), 'col'), parts along dimension 0, may hold values from -6 to 6
- norm_gain: float32 [128], replicated, may hold values from 0.5 to 1.5
- norm_bias: float32 [128], replicated, may hold values from -3 to 3
- proj_weight: bfloat16 [128, 512], replicated, may hold values from -0.5 to 0.5
- gate_weight: bfloat16 [128, 128], replicated, may hold values from -0.5 to 0.5
- tri_gain: float32 [128], replicated, may hold values from 0.5 to 1.5
- tri_bias: float32 [128], replicated, may hold values from -3 to 3
- out_weight: bfloat16 [128, 128], replicated, may hold values from -0.5 to 0.5
Outputs:
- block_out: bfloat16 [96, 48, 128], P(('crop', 'row'), 'col'), parts along dimension 0
- pair_grad: float32 [96, 48, 128], P(('crop', 'row'), 'col'), parts along dimension 0
- proj_grad: float32 [256, 512], P('crop'), parts along dimension 0
- gate_grad: float32 [256, 128], P('crop'), parts along dimension 0
- out_grad: float32 [256, 128], P('crop'), parts along dimension 0
The draws below stay inside these ranges and needn't reach their ends.
There are 2 independent parts, one for each index of `crop`. The reference program is written for one: setup_inputs(seed, part) draws one part's arguments, and reference() takes and returns one part's arrays. A program takes and returns all parts, laid end to end along the dimension named above; an argument that names none is the same for every part. Nothing has to cross between parts.
All inputs are finite; a program needn't handle non-finite values.
Results may differ from the reference program's by a relative error of at most 0.0066.
Values may be sent and summed in bfloat16 or wider, within the bound.
No kernel may reach another device: no remote copies, remote signals or barrier semaphores. Data moves between devices by JAX's collectives and lax.ppermute only.
A program may use at most 128 MiB of HBM per device.

```python
import jax
import jax.numpy as jnp
from jax import lax

C = 128
H = 128
N = 48


def block_scale(key, dims, cuts, smallest, top_value):
    def one(position, parts):
        heights = jax.random.uniform(jax.random.fold_in(jax.random.fold_in(key, 6), position), (parts,), jnp.float32, smallest / len(cuts), top_value / len(cuts))
        return jnp.repeat(jnp.exp(heights), dims[position] // parts).reshape((-1,) + (1,) * (len(dims) - position - 1))

    level = one(*cuts[0])
    for cut in cuts[1:]:
        level = level * one(*cut)
    return level


def noise(stream_key, shape, spread, most, shards=(), held_as=jnp.bfloat16):
    loudness = block_scale(stream_key, shape, shards, -0.22, 0.18) if shards else 1.0
    array = jax.random.normal(stream_key, shape, jnp.float32) * spread * loudness
    return jnp.minimum(jnp.maximum(array, -most), most).astype(held_as)


def setup_inputs(seed: int = 0, part: int = 0) -> dict:
    key_list = jax.random.split(jax.random.key(seed), 10)
    part_keys = jax.random.split(jax.random.fold_in(key_list[9], part), 10)
    pair_rep = noise(part_keys[0], (N, N, C), 1.0, 6.0, ((0, 8), (1, 2)))
    cotangent = noise(part_keys[1], (N, N, C), 1.0, 6.0, ((0, 8), (1, 2)))
    norm_gain = jnp.clip(1.0 + 0.1 * jax.random.normal(key_list[2], (C,), jnp.float32), 0.5, 1.5)
    norm_bias = noise(key_list[3], (C,), 0.5, 3.0, (), jnp.float32)
    proj_weight = noise(key_list[4], (C, 4 * H), C ** -0.5, 0.5)
    gate_weight = noise(key_list[5], (C, C), C ** -0.5, 0.5)
    tri_gain = jnp.clip(1.0 + 0.1 * jax.random.normal(key_list[6], (H,), jnp.float32), 0.5, 1.5)
    tri_bias = noise(key_list[7], (H,), 0.5, 3.0, (), jnp.float32)
    out_weight = noise(key_list[8], (H, C), H ** -0.5, 0.5)
    return dict(pair_rep=pair_rep, cotangent=cotangent, norm_gain=norm_gain, norm_bias=norm_bias, proj_weight=proj_weight, gate_weight=gate_weight, tri_gain=tri_gain, tri_bias=tri_bias, out_weight=out_weight)


def layer_norm(values, gain, bias):
    centred = values - lax.optimization_barrier(jnp.mean(values, axis=-1, keepdims=True))
    inverse = lax.rsqrt(lax.optimization_barrier(jnp.mean(centred * centred, axis=-1, keepdims=True)) + 1e-05)
    scaled = centred * inverse
    return (scaled * gain + bias, scaled, inverse)

def norm_back(grads, gain, scaled, inverse):
    weighted = grads * gain
    first = lax.optimization_barrier(jnp.mean(weighted, axis=-1, keepdims=True))
    second = lax.optimization_barrier(jnp.mean(weighted * scaled, axis=-1, keepdims=True))
    return inverse * (weighted - first - scaled * second)

def reference(pair_rep, cotangent, norm_gain, norm_bias, proj_weight, gate_weight, tri_gain, tri_bias, out_weight):
    f32 = jnp.float32
    bf16 = jnp.bfloat16
    normed_f, pair_hat, pair_inv = layer_norm(pair_rep.astype(f32), norm_gain, norm_bias)
    normed = normed_f.astype(bf16)
    flat_norm = normed.reshape(N * N, C)
    projected = jnp.dot(flat_norm, proj_weight, preferred_element_type=f32).reshape(N, N, 4 * H)
    sig_left = jax.nn.sigmoid(projected[..., 0:H])
    val_left = projected[..., H:2 * H]
    sig_right = jax.nn.sigmoid(projected[..., 2 * H:3 * H])
    val_right = projected[..., 3 * H:4 * H]
    left_edge = (sig_left * val_left).astype(bf16)
    right_edge = (sig_right * val_right).astype(bf16)
    out_gate = jax.nn.sigmoid(jnp.dot(flat_norm, gate_weight, preferred_element_type=f32).reshape(N, N, C))
    triangle = jnp.einsum('ikc,jkc->ijc', left_edge.astype(f32), right_edge.astype(f32))
    tri_f, tri_hat, tri_inv = layer_norm(triangle, tri_gain, tri_bias)
    tri_norm = tri_f.astype(bf16)
    flat_tri = tri_norm.reshape(N * N, H)
    update = jnp.dot(flat_tri, out_weight, preferred_element_type=f32).reshape(N, N, C)
    block_out = (out_gate * update).astype(bf16)
    cot = cotangent.astype(f32)
    d_update = (cot * out_gate).astype(bf16)
    d_gate = (cot * update * out_gate * (1.0 - out_gate)).astype(bf16)
    d_norm = jnp.dot(d_update.reshape(N * N, C), out_weight.T, preferred_element_type=f32).reshape(N, N, H)
    d_triangle = norm_back(d_norm, tri_gain, tri_hat, tri_inv).astype(bf16)
    d_left = jnp.einsum('ijc,jkc->ikc', d_triangle.astype(f32), right_edge.astype(f32))
    d_right = jnp.einsum('ijc,ikc->jkc', d_triangle.astype(f32), left_edge.astype(f32))
    d_proj = jnp.concatenate([d_left * val_left * sig_left * (1.0 - sig_left), d_left * sig_left, d_right * val_right * sig_right * (1.0 - sig_right), d_right * sig_right], axis=-1).astype(bf16)
    flat_dproj = d_proj.reshape(N * N, 4 * H)
    flat_dgate = d_gate.reshape(N * N, C)
    d_normed = jnp.dot(flat_dproj, proj_weight.T, preferred_element_type=f32) + jnp.dot(flat_dgate, gate_weight.T, preferred_element_type=f32)
    pair_grad = norm_back(d_normed.reshape(N, N, C), norm_gain, pair_hat, pair_inv)
    proj_grad = jnp.dot(flat_norm.T, flat_dproj, preferred_element_type=f32) / N
    gate_grad = jnp.dot(flat_norm.T, flat_dgate, preferred_element_type=f32) / N
    out_grad = jnp.dot(flat_tri.T, d_update.reshape(N * N, C), preferred_element_type=f32) / N
    return (block_out, pair_grad, proj_grad, gate_grad, out_grad)
```

```python
import functools

import jax
import jax.numpy as jnp
from jax import lax
from jax.experimental import pallas as pl
from jax.experimental.pallas import tpu as pltpu
from jax.sharding import PartitionSpec as P

F32 = jnp.float32
BF16 = jnp.bfloat16
VMEM_BUDGET = 40 * 2**20


def layer_norm(values, gain, bias):
    centred = values - jnp.mean(values, axis=-1, keepdims=True)
    inverse = lax.rsqrt(jnp.mean(centred * centred, axis=-1, keepdims=True) + 1e-05)
    scaled = centred * inverse
    return (scaled * gain + bias, scaled, inverse)


def norm_back(grads, gain, scaled, inverse):
    weighted = grads * gain
    first = jnp.mean(weighted, axis=-1, keepdims=True)
    second = jnp.mean(weighted * scaled, axis=-1, keepdims=True)
    return inverse * (weighted - first - scaled * second)


def sigmoid(values):
    return 0.5 * jnp.tanh(0.5 * values) + 0.5


def dot(a, b, contract=((1,), (0,))):
    return lax.dot_general(a, b, (contract, ((), ())), preferred_element_type=F32)


def at(index, size):
    return pl.ds(pl.multiple_of(index * size, size), size)


def forward_kernel(
    sizes,
    pair_z,
    pair_y,
    mate_z,
    mate_y,
    cot_z,
    cot_y,
    norm_gain,
    norm_bias,
    proj_weight,
    gate_weight,
    tri_gain,
    tri_bias,
    out_weight,
    block_out,
    d_tri,
    normed_out,
    d_gate_out,
    out_grad,
    left_own,
    right_own,
    left_mate,
    right_mate,
    tri,
    cot,
    tri_norm_s,
    d_update_s,
    block_s,
):
    rows, cols, groups = sizes
    total = rows * groups
    cells = rows * cols
    hidden = tri_gain.shape[-1]
    me = lax.axis_index("row")
    half = lax.axis_index("col")

    def slot_row(ref_index, slot):
        return lax.bitwise_xor(me, 2 * slot + ref_index)

    for source, is_own in ((pair_z, True), (pair_y, True), (mate_z, False), (mate_y, False)):
        parity = 0 if source is pair_z or source is mate_z else 1
        left, right = (left_own, right_own) if is_own else (left_mate, right_mate)
        values = source[...].astype(F32)
        normed = layer_norm(values, norm_gain[...], norm_bias[...])[0].astype(BF16)
        projected = dot(normed, proj_weight[...])
        left_edge = sigmoid(projected[:, :hidden]) * projected[:, hidden : 2 * hidden]
        right_edge = sigmoid(projected[:, 2 * hidden : 3 * hidden]) * projected[:, 3 * hidden :]
        left_edge = left_edge.astype(BF16).astype(F32)
        right_edge = right_edge.astype(BF16).astype(F32)
        for slot in range(groups // 2):
            place = at(slot_row(parity, slot), cells)
            part = slice(slot * cells, (slot + 1) * cells)
            left[place, :] = left_edge[part]
            right[place, :] = right_edge[part]
            if is_own:
                normed_out[place, :] = normed[part]
                cot[place, :] = (cot_z, cot_y)[parity][part, :]

    def tri_block(block, carry):
        first = block * rows

        def step(k, sums):
            new = list(sums)
            for left, right in ((left_own, right_own), (left_mate, right_mate)):
                tiles = [
                    right[pl.ds(half * cols * cols + tile * 8 * cols + k, 8, stride=cols), :]
                    for tile in range(cols // 8)
                ]
                for a in range(rows):
                    row = left[pl.ds((first + a) * cols + k, 1), :]
                    for t, tile in enumerate(tiles):
                        new[a * len(tiles) + t] += row * tile
            return tuple(new)

        zero = jnp.zeros((8, hidden), F32)
        sums = lax.fori_loop(0, cols, step, (zero,) * (rows * cols // 8), unroll=4)
        for t, value in enumerate(sums):
            tri[pl.ds(pl.multiple_of(block * cells + t * 8, 8), 8), :] = value
        return carry

    lax.fori_loop(0, groups, tri_block, 0)

    def cell_block(block, carry):
        place = at(block, 2 * cells)
        tri_f, tri_hat, tri_inv = layer_norm(tri[place, :], tri_gain[...], tri_bias[...])
        tri_norm = tri_f.astype(BF16)
        update = dot(tri_norm, out_weight[...])
        out_gate = sigmoid(dot(normed_out[place, :], gate_weight[...]))
        block_s[place, :] = (out_gate * update).astype(BF16)
        cotangent = cot[place, :].astype(F32)
        gated = cotangent * out_gate
        d_update = gated.astype(BF16)
        d_gate_out[place, :] = (gated * update * (1.0 - out_gate)).astype(BF16)
        d_norm = dot(d_update, out_weight[...], ((1,), (1,)))
        d_tri[place, :] = norm_back(d_norm, tri_gain[...], tri_hat, tri_inv).astype(BF16)
        tri_norm_s[place, :] = tri_norm
        d_update_s[place, :] = d_update
        return carry

    lax.fori_loop(0, groups // 2, cell_block, 0)
    block_out[...] = block_s[at(me, cells), :]
    out_grad[...] = dot(tri_norm_s[...], d_update_s[...], ((0,), (0,))) * (1.0 / total)


def backward_kernel(
    sizes,
    pair,
    d_tri_own,
    d_tri_mate,
    normed_ref,
    d_gate,
    out_grad,
    norm_gain,
    norm_bias,
    proj_weight,
    gate_weight,
    pair_grad,
    weight_grads,
    tri_own,
    tri_mate,
    left,
    right,
    left_gate,
    left_value,
    right_gate,
    right_value,
    d_proj_s,
):
    rows, cols, groups = sizes
    total = rows * groups
    cells = rows * cols
    channels = norm_gain.shape[-1]
    hidden = left.shape[-1]
    me = lax.axis_index("row")
    half = lax.axis_index("col")

    def project(block, carry):
        place = at(block, 2 * cells)
        projected = dot(normed_ref[place, :], proj_weight[...])
        for gate_s, value_s, edge_s, start in (
            (left_gate, left_value, left, 0),
            (right_gate, right_value, right, 2 * hidden),
        ):
            gate = sigmoid(projected[:, start : start + hidden])
            value = projected[:, start + hidden : start + 2 * hidden]
            edge = gate * value
            gate_s[place, :] = gate
            value_s[place, :] = edge * (1.0 - gate)
            edge_s[place, :] = edge.astype(BF16).astype(F32)
        tri_own[place, :] = d_tri_own[place, :].astype(F32)
        tri_mate[place, :] = d_tri_mate[place, :].astype(F32)
        return carry

    lax.fori_loop(0, groups // 2, project, 0)
    zero = jnp.zeros((8, hidden), F32)
    tiles = cols // 8

    def finish(sums, block_start, gate_s, value_s, column):
        for t, value in enumerate(sums):
            place = pl.ds(pl.multiple_of(block_start + t * 8, 8), 8)
            d_proj_s[place, column : column + hidden] = value * value_s[place, :]
            d_proj_s[place, column + hidden : column + 2 * hidden] = value * gate_s[place, :]

    def left_block(block, carry):
        first = block * rows

        def step(j, sums):
            new = list(sums)
            for source, side in ((tri_own, half), (tri_mate, 1 - half)):
                start = (side * cols + j) * cols
                operand = [
                    right[pl.ds(pl.multiple_of(start + t * 8, 8), 8), :] for t in range(tiles)
                ]
                for a in range(rows):
                    row = source[pl.ds((first + a) * cols + j, 1), :]
                    for t in range(tiles):
                        new[a * tiles + t] += row * operand[t]
            return tuple(new)

        sums = lax.fori_loop(0, cols, step, (zero,) * (rows * tiles), unroll=4)
        finish(sums, block * cells, left_gate, left_value, 0)
        return carry

    lax.fori_loop(0, groups, left_block, 0)

    for source, side in ((tri_own, half), (tri_mate, 1 - half)):

        def right_block(block, carry, source=source, side=side):
            first = block * rows

            def step(i, sums):
                new = list(sums)
                operand = [
                    left[pl.ds(pl.multiple_of(i * cols + t * 8, 8), 8), :] for t in range(tiles)
                ]
                for a in range(rows):
                    row = source[pl.ds(i * cols + first + a, 1), :]
                    for t in range(tiles):
                        new[a * tiles + t] += row * operand[t]
                return tuple(new)

            sums = lax.fori_loop(0, total, step, (zero,) * (rows * tiles), unroll=8)
            finish(
                sums, (side * cols + first) * cols, right_gate, right_value, 2 * hidden
            )
            return carry

        lax.fori_loop(0, cols // rows, right_block, 0)

    scale = 1.0 / total
    width = 4 * hidden
    weight_grads[:, :width] = (
        dot(normed_ref[...], d_proj_s[...].astype(BF16), ((0,), (0,))) * scale
    )
    weight_grads[:, width : width + channels] = (
        dot(normed_ref[...], d_gate[...], ((0,), (0,))) * scale
    )
    weight_grads[:, width + channels :] = out_grad[...]
    own = at(me, cells)
    d_normed = dot(d_proj_s[own, :].astype(BF16), proj_weight[...], ((1,), (1,))) + dot(
        d_gate[own, :], gate_weight[...], ((1,), (1,))
    )
    _, hat, inverse = layer_norm(pair[...].astype(F32), norm_gain[...], norm_bias[...])
    pair_grad[...] = norm_back(d_normed, norm_gain[...], hat, inverse)


def replicated(
    pair_rep,
    cotangent,
    norm_gain,
    norm_bias,
    proj_weight,
    gate_weight,
    tri_gain,
    tri_bias,
    out_weight,
):
    rows, cols, channels = pair_rep.shape
    hidden = tri_gain.shape[0]
    groups = lax.axis_size("row")
    cells = rows * cols
    every = cells * groups
    sizes = (rows, cols, groups)
    norm_gain, norm_bias = norm_gain[None], norm_bias[None]
    tri_gain, tri_bias = tri_gain[None], tri_bias[None]

    def across(value, mask):
        return lax.ppermute(value, "row", [(i, i ^ mask) for i in range(groups)])

    pair = pair_rep.reshape(cells, channels)
    own = jnp.stack([pair, cotangent.reshape(cells, channels)])
    got = [own] + [across(own, 2 * s) for s in range(1, groups // 2)]
    near = jnp.concatenate(got, axis=1)
    far = across(near, 1)
    pair_z, cot_z, pair_y, cot_y = near[0], near[1], far[0], far[1]
    swap = [(0, 1), (1, 0)]
    mate_z = lax.ppermute(pair_z, "col", swap)
    mate_y = lax.ppermute(pair_y, "col", swap)

    def vmem(*shape, dtype=F32):
        return pltpu.VMEM(shape, dtype)

    params = pltpu.CompilerParams(vmem_limit_bytes=VMEM_BUDGET)
    shape = jax.ShapeDtypeStruct
    block_out, d_tri, normed, d_gate, out_grad = pl.pallas_call(
        functools.partial(forward_kernel, sizes),
        out_shape=(
            shape((cells, channels), BF16),
            shape((every, hidden), BF16),
            shape((every, channels), BF16),
            shape((every, channels), BF16),
            shape((hidden, channels), F32),
        ),
        scratch_shapes=[
            vmem(every, hidden),
            vmem(every, hidden),
            vmem(every, hidden),
            vmem(every, hidden),
            vmem(every, hidden),
            vmem(every, channels, dtype=BF16),
            vmem(every, hidden, dtype=BF16),
            vmem(every, channels, dtype=BF16),
            vmem(every, channels, dtype=BF16),
        ],
        compiler_params=params,
        name="forward",
    )(
        pair_z,
        pair_y,
        mate_z,
        mate_y,
        cot_z,
        cot_y,
        norm_gain,
        norm_bias,
        proj_weight,
        gate_weight,
        tri_gain,
        tri_bias,
        out_weight,
    )
    d_tri_mate = lax.ppermute(d_tri, "col", swap)
    pair_grad, grads = pl.pallas_call(
        functools.partial(backward_kernel, sizes),
        out_shape=(
            shape((cells, channels), F32),
            shape((channels, 4 * hidden + channels + channels), F32),
        ),
        scratch_shapes=[vmem(every, hidden) for _ in range(8)] + [vmem(every, 4 * hidden)],
        compiler_params=params,
        name="backward",
    )(
        pair,
        d_tri,
        d_tri_mate,
        normed,
        d_gate,
        out_grad,
        norm_gain,
        norm_bias,
        proj_weight,
        gate_weight,
    )
    grads = grads + lax.ppermute(grads, "col", swap)
    return (
        block_out.reshape(pair_rep.shape),
        pair_grad.reshape(pair_rep.shape),
        grads[:, : 4 * hidden],
        grads[:, 4 * hidden : 4 * hidden + channels],
        grads[:, 4 * hidden + channels :],
    )


def sharded(
    pair_rep,
    cotangent,
    norm_gain,
    norm_bias,
    proj_weight,
    gate_weight,
    tri_gain,
    tri_bias,
    out_weight,
):
    f32 = jnp.float32
    bf16 = jnp.bfloat16
    hidden = tri_gain.shape[0]
    channels = norm_gain.shape[0]
    row_count = pair_rep.shape[0]
    col_count = pair_rep.shape[1]
    crop_len = row_count * lax.axis_size("row")
    normed_f, pair_hat, pair_inv = layer_norm(pair_rep.astype(f32), norm_gain, norm_bias)
    normed = normed_f.astype(bf16)
    projected = jnp.einsum("ijc,cd->ijd", normed, proj_weight, preferred_element_type=f32)
    sig_left = jax.nn.sigmoid(projected[..., 0:hidden])
    val_left = projected[..., hidden : 2 * hidden]
    sig_right = jax.nn.sigmoid(projected[..., 2 * hidden : 3 * hidden])
    val_right = projected[..., 3 * hidden : 4 * hidden]
    left_edge = (sig_left * val_left).astype(bf16)
    right_edge = (sig_right * val_right).astype(bf16)
    out_gate = jax.nn.sigmoid(
        jnp.einsum("ijc,cd->ijd", normed, gate_weight, preferred_element_type=f32)
    )
    right_all = lax.all_gather(right_edge, "row", axis=0, tiled=True)
    block = right_all
    triangle = lax.psum_scatter(
        jnp.einsum("ikc,jkc->jic", left_edge, block, preferred_element_type=f32),
        "col",
        scatter_dimension=0,
        tiled=True,
    ).transpose(1, 0, 2)
    tri_f, tri_hat, tri_inv = layer_norm(triangle, tri_gain, tri_bias)
    tri_norm = tri_f.astype(bf16)
    update = jnp.einsum("ijh,hc->ijc", tri_norm, out_weight, preferred_element_type=f32)
    block_out = (out_gate * update).astype(bf16)
    cot = cotangent.astype(f32)
    d_update = (cot * out_gate).astype(bf16)
    d_gate = (cot * update * out_gate * (1.0 - out_gate)).astype(bf16)
    d_norm = jnp.einsum("ijc,hc->ijh", d_update, out_weight, preferred_element_type=f32)
    d_triangle = norm_back(d_norm, tri_gain, tri_hat, tri_inv).astype(bf16)
    tri_rows = lax.all_gather(d_triangle, "col", axis=1, tiled=True)
    d_left = jnp.einsum("ijc,jkc->ikc", tri_rows, right_all, preferred_element_type=f32)
    tri_cols = lax.all_to_all(tri_rows, "row", split_axis=1, concat_axis=0, tiled=True)
    block = tri_cols
    d_right = jnp.einsum(
        "ijc,ikc->jkc",
        block,
        lax.all_gather(left_edge, "row", axis=0, tiled=True),
        preferred_element_type=f32,
    )
    d_proj = jnp.concatenate(
        [
            d_left * val_left * sig_left * (1.0 - sig_left),
            d_left * sig_left,
            d_right * val_right * sig_right * (1.0 - sig_right),
            d_right * sig_right,
        ],
        axis=-1,
    ).astype(bf16)
    d_normed = jnp.einsum(
        "ijd,cd->ijc", d_proj, proj_weight, preferred_element_type=f32
    ) + jnp.einsum("ijd,cd->ijc", d_gate, gate_weight, preferred_element_type=f32)
    pair_grad = norm_back(d_normed, norm_gain, pair_hat, pair_inv)
    cells = row_count * col_count
    flat_norm = normed.reshape(cells, channels)
    local_proj = (
        jnp.dot(flat_norm.T, d_proj.reshape(cells, 4 * hidden), preferred_element_type=f32)
        / crop_len
    )
    local_gate = (
        jnp.dot(flat_norm.T, d_gate.reshape(cells, channels), preferred_element_type=f32) / crop_len
    )
    local_out = (
        jnp.dot(
            tri_norm.reshape(cells, hidden).T,
            d_update.reshape(cells, channels),
            preferred_element_type=f32,
        )
        / crop_len
    )
    proj_grad, gate_grad, out_grad = lax.psum((local_proj, local_gate, local_out), ("row", "col"))
    return (block_out, pair_grad, proj_grad, gate_grad, out_grad)


def local(pair_rep, *others):
    rows, cols, channels = pair_rep.shape
    groups = lax.axis_size("row")
    every = rows * groups * cols
    fits = 16 * every * channels * 4 <= VMEM_BUDGET
    paired = lax.axis_size("col") == 2 and groups & (groups - 1) == 0 and groups >= 2
    whole_tiles = cols % 8 == 0 and cols % rows == 0 and rows * cols % 16 == 0
    plan = replicated if fits and paired and whole_tiles else sharded
    return plan(pair_rep, *others)


def solution(mesh):
    return jax.shard_map(
        local,
        mesh=mesh,
        in_specs=(
            P(("crop", "row"), "col", None),
            P(("crop", "row"), "col", None),
            P(),
            P(),
            P(),
            P(),
            P(),
            P(),
            P(),
        ),
        out_specs=(
            P(("crop", "row"), "col", None),
            P(("crop", "row"), "col", None),
            P("crop", None),
            P("crop", None),
            P("crop", None),
        ),
        check_vma=False,
    )
```

```python
import functools

import jax
import jax.numpy as jnp
from jax import lax
from jax.experimental import pallas as pl
from jax.experimental.pallas import tpu as pltpu
from jax.sharding import PartitionSpec as P

F32 = jnp.float32
BF16 = jnp.bfloat16
VMEM_BUDGET = 24 * 2**20
SWAP = ((0, 1), (1, 0))
NATIVE = ((1,), (0,))
BY_ROWS = ((0,), (0,))
TRANSPOSED = ((1,), (1,))


def layer_norm(values, gain, bias):
    centred = values - jnp.mean(values, axis=-1, keepdims=True)
    inverse = lax.rsqrt(jnp.mean(centred * centred, axis=-1, keepdims=True) + 1e-05)
    scaled = centred * inverse
    return (scaled * gain + bias, scaled, inverse)


def norm_back(grads, gain, scaled, inverse):
    weighted = grads * gain
    first = jnp.mean(weighted, axis=-1, keepdims=True)
    second = jnp.mean(weighted * scaled, axis=-1, keepdims=True)
    return inverse * (weighted - first - scaled * second)


def sigmoid(values):
    return 0.5 * jnp.tanh(0.5 * values) + 0.5


def dot(a, b, contract=NATIVE):
    return lax.dot_general(a, b, (contract, ((), ())), preferred_element_type=F32)


def at(index, size):
    return pl.ds(pl.multiple_of(index * size, size), size)


def tile(start):
    return pl.ds(pl.multiple_of(start, 8), 8)


def places(groups):
    me = lax.axis_index("row")
    return [lax.bitwise_xor(me // 2, t) for t in range(groups // 2)]


def row_block(which, b):
    me = lax.axis_index("row")
    parity = lax.rem(me, 2)
    return 2 * b + (parity if which == 0 else 1 - parity)


def edges(values, norm_gain, norm_bias, proj_weight):
    hidden = proj_weight.shape[1] // 4
    normed = layer_norm(values.astype(F32), norm_gain, norm_bias)[0].astype(BF16)
    projected = dot(normed, proj_weight)
    sides = []
    for start in (0, 2 * hidden):
        gate = sigmoid(projected[:, start : start + hidden])
        edge = gate * projected[:, start + hidden : start + 2 * hidden]
        sides.append((edge.astype(BF16).astype(F32), gate, edge * (1.0 - gate)))
    return normed, sides


def own_edges_kernel(sizes, x, gain, bias, weight, normed_out, *outs):
    rows, cols, groups = sizes
    cells = rows * cols
    normed, sides = edges(x[...], gain[...], bias[...], weight[...])
    for t, b in enumerate(places(groups)):
        part = slice(t * cells, (t + 1) * cells)
        place = at(b, cells)
        normed_out[place, :] = normed[part]
        for out, value in zip(outs, sides[0] + sides[1], strict=True):
            out[place, :] = value[part]


def mate_edges_kernel(sizes, x, gain, bias, weight, left, right):
    rows, cols, groups = sizes
    cells = rows * cols
    _, sides = edges(x[...], gain[...], bias[...], weight[...])
    for t, b in enumerate(places(groups)):
        part = slice(t * cells, (t + 1) * cells)
        left[at(b, cells), :] = sides[0][0][part]
        right[at(b, cells), :] = sides[1][0][part]


def triangle_kernel(sizes, *refs):
    rows, cols, groups = sizes
    cells = rows * cols
    lefts, rights, (tri,), picked = refs[:4], refs[4:8], refs[8:9], refs[9:]
    hidden = tri.shape[-1]
    half = lax.axis_index("col")
    zero = jnp.zeros((8, hidden), F32)
    count = cols // 8
    blocks = cols // rows
    for side in range(2):
        for which in range(2):
            for s in range(blocks // 2):
                b = half * (blocks // 2) + s
                p = row_block(which, b) - half * blocks
                picked[side][at(p, cells), :] = rights[2 * side + which][at(b, cells), :]

    for which in range(2):

        def tri_block(b, carry, which=which):
            def step(k, sums):
                new = list(sums)
                for side in range(2):
                    left = lefts[2 * side + which]
                    tiles = [
                        picked[side][pl.ds(t * 8 * cols + k, 8, stride=cols), :]
                        for t in range(count)
                    ]
                    for a in range(rows):
                        row = left[pl.ds((b * rows + a) * cols + k, 1), :]
                        for t in range(count):
                            new[a * count + t] += row * tiles[t]
                return tuple(new)

            sums = lax.fori_loop(0, cols, step, (zero,) * (rows * count), unroll=4)
            start = row_block(which, b) * cells
            for t, value in enumerate(sums):
                tri[tile(start + t * 8), :] = value
            return carry

        lax.fori_loop(0, groups // 2, tri_block, 0)


def cells_kernel(
    sizes,
    tri,
    normed_0,
    normed_1,
    cot_0,
    cot_1,
    gate_weight,
    gain,
    bias,
    out_weight,
    block_out,
    d_tri,
    d_gate,
    tri_norm_out,
    d_update_out,
):
    rows, cols, groups = sizes
    cells = rows * cols
    for which, normed, cot in ((0, normed_0, cot_0), (1, normed_1, cot_1)):
        for t, b in enumerate(places(groups)):
            place = at(row_block(which, b), cells)
            tri_f, hat, inverse = layer_norm(tri[place, :], gain[...], bias[...])
            tri_norm = tri_f.astype(BF16)
            update = dot(tri_norm, out_weight[...])
            out_gate = sigmoid(dot(normed[at(b, cells), :], gate_weight[...]))
            if which == 0 and t == 0:
                block_out[...] = (out_gate * update).astype(BF16)
            gated = cot[t * cells : (t + 1) * cells, :].astype(F32) * out_gate
            d_update = gated.astype(BF16)
            d_gate[place, :] = (gated * update * (1.0 - out_gate)).astype(BF16)
            d_norm = dot(d_update, out_weight[...], TRANSPOSED)
            d_tri[place, :] = norm_back(d_norm, gain[...], hat, inverse).astype(BF16)
            tri_norm_out[place, :] = tri_norm
            d_update_out[place, :] = d_update


def contract(rows, cols, count, unroll, start, source, row_at, operand, operand_at):
    tiles = cols // 8

    def step(term, sums):
        new = list(sums)
        loaded = [operand[tile(operand_at(term) + t * 8), :] for t in range(tiles)]
        for a in range(rows):
            row = source[pl.ds(row_at(a, term), 1), :]
            for t in range(tiles):
                new[a * tiles + t] += row * loaded[t]
        return tuple(new)

    return lax.fori_loop(0, count, step, start, unroll=unroll)


def early_kernel(
    sizes,
    d_tri_ref,
    d_gate,
    tri_norm,
    d_update,
    normed_0,
    normed_1,
    left_0,
    left_1,
    right_0,
    right_1,
    left,
    right,
    normed,
    d_left,
    d_right,
    small_grads,
    source,
):
    rows, cols, groups = sizes
    cells = rows * cols
    hidden = left.shape[-1]
    channels = normed.shape[-1]
    half = lax.axis_index("col")
    zeros = (jnp.zeros((8, hidden), F32),) * (rows * cols // 8)
    source[...] = d_tri_ref[...].astype(F32)
    for which, part_n, part_l, part_r in (
        (0, normed_0, left_0, right_0),
        (1, normed_1, left_1, right_1),
    ):
        for b in range(groups // 2):
            place, part = at(row_block(which, b), cells), slice(b * cells, (b + 1) * cells)
            normed[place, :] = part_n[part, :]
            left[place, :] = part_l[part, :]
            right[place, :] = part_r[part, :]

    def left_block(p, carry):
        sums = contract(
            rows,
            cols,
            cols,
            8,
            zeros,
            source,
            lambda a, j: (p * rows + a) * cols + j,
            right,
            lambda j: (half * cols + j) * cols,
        )
        for t, value in enumerate(sums):
            d_left[tile(p * cells + t * 8), :] = value
        return carry

    lax.fori_loop(0, groups, left_block, 0)

    def right_block(p, carry):
        sums = contract(
            rows,
            cols,
            rows * groups,
            8,
            zeros,
            source,
            lambda a, i: i * cols + p * rows + a,
            left,
            lambda i: i * cols,
        )
        for t, value in enumerate(sums):
            d_right[tile(p * cells + t * 8), :] = value
        return carry

    lax.fori_loop(0, cols // rows, right_block, 0)
    scale = 1.0 / (rows * groups)
    small_grads[:, :channels] = dot(normed[...], d_gate[...], BY_ROWS) * scale
    small_grads[:, channels:] = dot(tri_norm[...], d_update[...], BY_ROWS) * scale


def late_kernel(
    sizes,
    pair,
    d_tri_ref,
    d_gate,
    left,
    right,
    normed,
    d_left,
    d_right,
    left_gate_0,
    left_gate_1,
    left_value_0,
    left_value_1,
    right_gate_0,
    right_gate_1,
    right_value_0,
    right_value_1,
    norm_gain,
    norm_bias,
    proj_weight,
    gate_weight,
    pair_grad,
    proj_grad,
    source,
    d_right_s,
    d_proj,
):
    rows, cols, groups = sizes
    cells = rows * cols
    hidden = left.shape[-1]
    half = lax.axis_index("col")
    me = lax.axis_index("row")
    zeros = (jnp.zeros((8, hidden), F32),) * (rows * cols // 8)
    source[...] = d_tri_ref[...].astype(F32)
    d_right_s[at(half, cols * cols), :] = d_right[...]

    def right_block(p, carry):
        sums = contract(
            rows,
            cols,
            rows * groups,
            8,
            zeros,
            source,
            lambda a, i: i * cols + p * rows + a,
            left,
            lambda i: i * cols,
        )
        start = (1 - half) * cols * cols + p * cells
        for t, value in enumerate(sums):
            d_right_s[tile(start + t * 8), :] = value
        return carry

    lax.fori_loop(0, cols // rows, right_block, 0)

    for which, left_gate, left_value, right_gate, right_value in (
        (0, left_gate_0, left_value_0, right_gate_0, right_value_0),
        (1, left_gate_1, left_value_1, right_gate_1, right_value_1),
    ):

        def left_block(
            b,
            carry,
            which=which,
            left_gate=left_gate,
            left_value=left_value,
            right_gate=right_gate,
            right_value=right_value,
        ):
            p = row_block(which, b)
            start = p * cells
            sums = contract(
                rows,
                cols,
                cols,
                8,
                tuple(d_left[tile(start + t * 8), :] for t in range(cells // 8)),
                source,
                lambda a, j: (p * rows + a) * cols + j,
                right,
                lambda j: ((1 - half) * cols + j) * cols,
            )
            part, place = at(b, cells), at(p, cells)
            grads = jnp.concatenate(sums, axis=0)
            d_proj[place, :hidden] = (grads * left_value[part, :]).astype(BF16)
            d_proj[place, hidden : 2 * hidden] = (grads * left_gate[part, :]).astype(BF16)
            grads = d_right_s[place, :]
            d_proj[place, 2 * hidden : 3 * hidden] = (grads * right_value[part, :]).astype(BF16)
            d_proj[place, 3 * hidden :] = (grads * right_gate[part, :]).astype(BF16)
            return carry

        lax.fori_loop(0, groups // 2, left_block, 0)

    scale = 1.0 / (rows * groups)
    proj_grad[...] = dot(normed[...], d_proj[...], BY_ROWS) * scale
    own = at(me, cells)
    d_normed = dot(d_proj[own, :], proj_weight[...], TRANSPOSED) + dot(
        d_gate[own, :], gate_weight[...], TRANSPOSED
    )
    _, hat, inverse = layer_norm(pair[...].astype(F32), norm_gain[...], norm_bias[...])
    pair_grad[...] = norm_back(d_normed, norm_gain[...], hat, inverse)


def replicated(
    pair_rep,
    cotangent,
    norm_gain,
    norm_bias,
    proj_weight,
    gate_weight,
    tri_gain,
    tri_bias,
    out_weight,
):
    rows, cols, channels = pair_rep.shape
    hidden = tri_gain.shape[0]
    groups = lax.axis_size("row")
    cells = rows * cols
    every = cells * groups
    some = every // 2
    sizes = (rows, cols, groups)
    norm_gain, norm_bias = norm_gain[None], norm_bias[None]
    tri_gain, tri_bias = tri_gain[None], tri_bias[None]

    def call(kernel, outs, *args, scratch=(), name):
        return pl.pallas_call(
            functools.partial(kernel, sizes),
            out_shape=[jax.ShapeDtypeStruct(*out) for out in outs],
            scratch_shapes=[pltpu.VMEM(*one) for one in scratch],
            compiler_params=pltpu.CompilerParams(vmem_limit_bytes=VMEM_BUDGET),
            name=name,
        )(*args)

    def across(value, mask):
        return lax.ppermute(value, "row", [(i, i ^ mask) for i in range(groups)])

    def over(value):
        return lax.ppermute(value, "col", SWAP)

    def gather(value):
        got = [value] + [across(value, 2 * s) for s in range(1, groups // 2)]
        near = jnp.concatenate(got, axis=0)
        return near, across(near, 1)

    pair = pair_rep.reshape(cells, channels)
    pairs = gather(pair)
    cots = gather(cotangent.reshape(cells, channels))
    mates = [over(part) for part in pairs]
    weights = (norm_gain, norm_bias, proj_weight)

    full, part = (every, hidden), (some, hidden)
    own = [
        call(
            own_edges_kernel,
            [((some, channels), BF16)] + [(part, F32)] * 6,
            x,
            *weights,
            name="own_edges",
        )
        for x in pairs
    ]
    mate = [
        call(mate_edges_kernel, [(part, F32)] * 2, x, *weights, name="mate_edges") for x in mates
    ]
    normed = [o[0] for o in own]
    left, left_gate, left_value = ([o[n] for o in own] for n in (1, 2, 3))
    right, right_gate, right_value = ([o[n] for o in own] for n in (4, 5, 6))
    (tri,) = call(
        triangle_kernel,
        [(full, F32)],
        *left,
        *(m[0] for m in mate),
        *right,
        *(m[1] for m in mate),
        scratch=[((cols * cols, hidden), F32)] * 2,
        name="triangle",
    )
    block_out, d_tri, d_gate, tri_norm, d_update = call(
        cells_kernel,
        [((cells, channels), BF16)] + [(full, BF16)] * 4,
        tri,
        *normed,
        *cots,
        gate_weight,
        tri_gain,
        tri_bias,
        out_weight,
        name="cells",
    )
    d_tri_mate = over(d_tri)
    left_all, right_all, normed_all, d_left, d_right, small_grads = call(
        early_kernel,
        [
            (full, F32),
            (full, F32),
            ((every, channels), BF16),
            (full, F32),
            (part, F32),
            ((channels, 2 * channels), F32),
        ],
        d_tri,
        d_gate,
        tri_norm,
        d_update,
        *normed,
        *left,
        *right,
        scratch=[(full, F32)],
        name="early",
    )
    small_mate = over(small_grads)
    pair_grad, proj_grad = call(
        late_kernel,
        [((cells, channels), F32), ((channels, 4 * hidden), F32)],
        pair,
        d_tri_mate,
        d_gate,
        left_all,
        right_all,
        normed_all,
        d_left,
        d_right,
        *left_gate,
        *left_value,
        *right_gate,
        *right_value,
        norm_gain,
        norm_bias,
        proj_weight,
        gate_weight,
        scratch=[(full, F32), (full, F32), ((every, 4 * hidden), BF16)],
        name="late",
    )
    small = small_grads + small_mate
    return (
        block_out.reshape(pair_rep.shape),
        pair_grad.reshape(pair_rep.shape),
        proj_grad + over(proj_grad),
        small[:, :channels],
        small[:, channels:],
    )


def sharded(
    pair_rep,
    cotangent,
    norm_gain,
    norm_bias,
    proj_weight,
    gate_weight,
    tri_gain,
    tri_bias,
    out_weight,
):
    f32 = jnp.float32
    bf16 = jnp.bfloat16
    hidden = tri_gain.shape[0]
    channels = norm_gain.shape[0]
    row_count = pair_rep.shape[0]
    col_count = pair_rep.shape[1]
    crop_len = row_count * lax.axis_size("row")
    normed_f, pair_hat, pair_inv = layer_norm(pair_rep.astype(f32), norm_gain, norm_bias)
    normed = normed_f.astype(bf16)
    projected = jnp.einsum("ijc,cd->ijd", normed, proj_weight, preferred_element_type=f32)
    sig_left = jax.nn.sigmoid(projected[..., 0:hidden])
    val_left = projected[..., hidden : 2 * hidden]
    sig_right = jax.nn.sigmoid(projected[..., 2 * hidden : 3 * hidden])
    val_right = projected[..., 3 * hidden : 4 * hidden]
    left_edge = (sig_left * val_left).astype(bf16)
    right_edge = (sig_right * val_right).astype(bf16)
    out_gate = jax.nn.sigmoid(
        jnp.einsum("ijc,cd->ijd", normed, gate_weight, preferred_element_type=f32)
    )
    right_all = lax.all_gather(right_edge, "row", axis=0, tiled=True)
    block = right_all
    triangle = lax.psum_scatter(
        jnp.einsum("ikc,jkc->jic", left_edge, block, preferred_element_type=f32),
        "col",
        scatter_dimension=0,
        tiled=True,
    ).transpose(1, 0, 2)
    tri_f, tri_hat, tri_inv = layer_norm(triangle, tri_gain, tri_bias)
    tri_norm = tri_f.astype(bf16)
    update = jnp.einsum("ijh,hc->ijc", tri_norm, out_weight, preferred_element_type=f32)
    block_out = (out_gate * update).astype(bf16)
    cot = cotangent.astype(f32)
    d_update = (cot * out_gate).astype(bf16)
    d_gate = (cot * update * out_gate * (1.0 - out_gate)).astype(bf16)
    d_norm = jnp.einsum("ijc,hc->ijh", d_update, out_weight, preferred_element_type=f32)
    d_triangle = norm_back(d_norm, tri_gain, tri_hat, tri_inv).astype(bf16)
    tri_rows = lax.all_gather(d_triangle, "col", axis=1, tiled=True)
    d_left = jnp.einsum("ijc,jkc->ikc", tri_rows, right_all, preferred_element_type=f32)
    tri_cols = lax.all_to_all(tri_rows, "row", split_axis=1, concat_axis=0, tiled=True)
    block = tri_cols
    d_right = jnp.einsum(
        "ijc,ikc->jkc",
        block,
        lax.all_gather(left_edge, "row", axis=0, tiled=True),
        preferred_element_type=f32,
    )
    d_proj = jnp.concatenate(
        [
            d_left * val_left * sig_left * (1.0 - sig_left),
            d_left * sig_left,
            d_right * val_right * sig_right * (1.0 - sig_right),
            d_right * sig_right,
        ],
        axis=-1,
    ).astype(bf16)
    d_normed = jnp.einsum(
        "ijd,cd->ijc", d_proj, proj_weight, preferred_element_type=f32
    ) + jnp.einsum("ijd,cd->ijc", d_gate, gate_weight, preferred_element_type=f32)
    pair_grad = norm_back(d_normed, norm_gain, pair_hat, pair_inv)
    cells = row_count * col_count
    flat_norm = normed.reshape(cells, channels)
    local_proj = (
        jnp.dot(flat_norm.T, d_proj.reshape(cells, 4 * hidden), preferred_element_type=f32)
        / crop_len
    )
    local_gate = (
        jnp.dot(flat_norm.T, d_gate.reshape(cells, channels), preferred_element_type=f32) / crop_len
    )
    local_out = (
        jnp.dot(
            tri_norm.reshape(cells, hidden).T,
            d_update.reshape(cells, channels),
            preferred_element_type=f32,
        )
        / crop_len
    )
    proj_grad, gate_grad, out_grad = lax.psum((local_proj, local_gate, local_out), ("row", "col"))
    return (block_out, pair_grad, proj_grad, gate_grad, out_grad)


def local(pair_rep, *others):
    rows, cols, channels = pair_rep.shape
    hidden = others[7].shape[0]
    groups = lax.axis_size("row")
    every = rows * groups * cols
    fits = 24 * every * channels * 4 <= VMEM_BUDGET and hidden == channels
    paired = lax.axis_size("col") == 2 and groups & (groups - 1) == 0 and groups >= 2
    whole_tiles = cols % 8 == 0 and cols % (2 * rows) == 0 and rows * cols % 16 == 0
    plan = replicated if fits and paired and whole_tiles else sharded
    return plan(pair_rep, *others)


def solution(mesh):
    return jax.shard_map(
        local,
        mesh=mesh,
        in_specs=(
            P(("crop", "row"), "col", None),
            P(("crop", "row"), "col", None),
            P(),
            P(),
            P(),
            P(),
            P(),
            P(),
            P(),
        ),
        out_specs=(
            P(("crop", "row"), "col", None),
            P(("crop", "row"), "col", None),
            P("crop", None),
            P("crop", None),
            P("crop", None),
        ),
        check_vma=False,
    )
```

```python
import functools

import jax
import jax.numpy as jnp
from jax import lax
from jax.experimental import pallas as pl
from jax.experimental.pallas import tpu as pltpu
from jax.sharding import PartitionSpec as P

F32 = jnp.float32
BF16 = jnp.bfloat16
VMEM_BUDGET = 24 * 2**20
SWAP = ((0, 1), (1, 0))
NATIVE = ((1,), (0,))
BY_ROWS = ((0,), (0,))
TRANSPOSED = ((1,), (1,))


def layer_norm(values, gain, bias):
    centred = values - jnp.mean(values, axis=-1, keepdims=True)
    inverse = lax.rsqrt(jnp.mean(centred * centred, axis=-1, keepdims=True) + 1e-05)
    scaled = centred * inverse
    return (scaled * gain + bias, scaled, inverse)


def norm_back(grads, gain, scaled, inverse):
    weighted = grads * gain
    first = jnp.mean(weighted, axis=-1, keepdims=True)
    second = jnp.mean(weighted * scaled, axis=-1, keepdims=True)
    return inverse * (weighted - first - scaled * second)


def sigmoid(values):
    return 0.5 * jnp.tanh(0.5 * values) + 0.5


def dot(a, b, contract=NATIVE):
    return lax.dot_general(a, b, (contract, ((), ())), preferred_element_type=F32)


def at(index, size):
    return pl.ds(pl.multiple_of(index * size, size), size)


def tile(start):
    return pl.ds(pl.multiple_of(start, 8), 8)


def places(groups):
    me = lax.axis_index("row")
    return [lax.bitwise_xor(me // 2, t) for t in range(groups // 2)]


def row_block(which, b):
    me = lax.axis_index("row")
    parity = lax.rem(me, 2)
    return 2 * b + (parity if which == 0 else 1 - parity)


def edges(blocks, params, proj_weight):
    hidden = proj_weight.shape[1] // 4
    values = jnp.concatenate([block[...] for block in blocks], axis=0).astype(F32)
    normed = layer_norm(values, params[0:1, :], params[1:2, :])[0].astype(BF16)
    projected = dot(normed, proj_weight[...])
    sides = []
    for start in (0, 2 * hidden):
        gate = sigmoid(projected[:, start : start + hidden])
        edge = gate * projected[:, start + hidden : start + 2 * hidden]
        sides.append((edge.astype(BF16).astype(F32), gate, edge * (1.0 - gate)))
    return normed, sides


def own_edges_kernel(sizes, params, weight, *refs):
    rows, cols, groups = sizes
    cells = rows * cols
    blocks, normed_out, outs = refs[:-7], refs[-7], refs[-6:]
    normed, sides = edges(blocks, params, weight)
    for t, b in enumerate(places(groups)):
        part = slice(t * cells, (t + 1) * cells)
        place = at(b, cells)
        normed_out[place, :] = normed[part]
        for out, value in zip(outs, sides[0] + sides[1], strict=True):
            out[place, :] = value[part]


def mate_edges_kernel(sizes, params, weight, *refs):
    rows, cols, groups = sizes
    cells = rows * cols
    blocks, left, right = refs[:-2], refs[-2], refs[-1]
    _, sides = edges(blocks, params, weight)
    for t, b in enumerate(places(groups)):
        part = slice(t * cells, (t + 1) * cells)
        left[at(b, cells), :] = sides[0][0][part]
        right[at(b, cells), :] = sides[1][0][part]


def triangle_kernel(sizes, *refs):
    rows, cols, groups = sizes
    cells = rows * cols
    lefts, rights, (tri,), picked = refs[:4], refs[4:8], refs[8:9], refs[9:]
    hidden = tri.shape[-1]
    half = lax.axis_index("col")
    zero = jnp.zeros((8, hidden), F32)
    count = cols // 8
    blocks = cols // rows
    for side in range(2):
        for which in range(2):
            for s in range(blocks // 2):
                b = half * (blocks // 2) + s
                p = row_block(which, b) - half * blocks
                picked[side][at(p, cells), :] = rights[2 * side + which][at(b, cells), :]

    for which in range(2):

        def tri_block(b, carry, which=which):
            def step(k, sums):
                new = list(sums)
                for side in range(2):
                    left = lefts[2 * side + which]
                    tiles = [
                        picked[side][pl.ds(t * 8 * cols + k, 8, stride=cols), :]
                        for t in range(count)
                    ]
                    for a in range(rows):
                        row = left[pl.ds((b * rows + a) * cols + k, 1), :]
                        for t in range(count):
                            new[a * count + t] += row * tiles[t]
                return tuple(new)

            sums = lax.fori_loop(0, cols, step, (zero,) * (rows * count), unroll=4)
            start = row_block(which, b) * cells
            for t, value in enumerate(sums):
                tri[tile(start + t * 8), :] = value
            return carry

        lax.fori_loop(0, groups // 2, tri_block, 0)


def cells_kernel(
    sizes,
    params,
    tri,
    normed_0,
    normed_1,
    gate_weight,
    out_weight,
    *refs,
):
    rows, cols, groups = sizes
    cells = rows * cols
    cots, (block_out, d_tri, d_gate, tri_norm_out, d_update_out) = refs[:-5], refs[-5:]
    gain, bias = params[2:3, :], params[3:4, :]
    for which, normed in ((0, normed_0), (1, normed_1)):
        for t, b in enumerate(places(groups)):
            cot = cots[t][which * cells : (which + 1) * cells, :]
            place = at(row_block(which, b), cells)
            tri_f, hat, inverse = layer_norm(tri[place, :], gain, bias)
            tri_norm = tri_f.astype(BF16)
            update = dot(tri_norm, out_weight[...])
            out_gate = sigmoid(dot(normed[at(b, cells), :], gate_weight[...]))
            if which == 0 and t == 0:
                block_out[...] = (out_gate * update).astype(BF16)
            gated = cot.astype(F32) * out_gate
            d_update = gated.astype(BF16)
            d_gate[place, :] = (gated * update * (1.0 - out_gate)).astype(BF16)
            d_norm = dot(d_update, out_weight[...], TRANSPOSED)
            d_tri[place, :] = norm_back(d_norm, gain, hat, inverse).astype(BF16)
            tri_norm_out[place, :] = tri_norm
            d_update_out[place, :] = d_update


def contract(rows, cols, count, unroll, start, source, row_at, operand, operand_at):
    tiles = cols // 8

    def step(term, sums):
        new = list(sums)
        loaded = [operand[tile(operand_at(term) + t * 8), :] for t in range(tiles)]
        for a in range(rows):
            row = source[pl.ds(row_at(a, term), 1), :]
            for t in range(tiles):
                new[a * tiles + t] += row * loaded[t]
        return tuple(new)

    return lax.fori_loop(0, count, step, start, unroll=unroll)


def early_kernel(
    sizes,
    d_tri_ref,
    d_gate,
    tri_norm,
    d_update,
    normed_0,
    normed_1,
    left_0,
    left_1,
    right_0,
    right_1,
    left,
    right,
    normed,
    d_left,
    d_right,
    small_grads,
    source,
):
    rows, cols, groups = sizes
    cells = rows * cols
    hidden = left.shape[-1]
    channels = normed.shape[-1]
    half = lax.axis_index("col")
    zeros = (jnp.zeros((8, hidden), F32),) * (rows * cols // 8)
    source[...] = d_tri_ref[...].astype(F32)
    for which, part_n, part_l, part_r in (
        (0, normed_0, left_0, right_0),
        (1, normed_1, left_1, right_1),
    ):
        for b in range(groups // 2):
            place, part = at(row_block(which, b), cells), slice(b * cells, (b + 1) * cells)
            normed[place, :] = part_n[part, :]
            left[place, :] = part_l[part, :]
            right[place, :] = part_r[part, :]

    def left_block(p, carry):
        sums = contract(
            rows,
            cols,
            cols,
            8,
            zeros,
            source,
            lambda a, j: (p * rows + a) * cols + j,
            right,
            lambda j: (half * cols + j) * cols,
        )
        for t, value in enumerate(sums):
            d_left[tile(p * cells + t * 8), :] = value
        return carry

    lax.fori_loop(0, groups, left_block, 0)

    def right_block(p, carry):
        sums = contract(
            rows,
            cols,
            rows * groups,
            8,
            zeros,
            source,
            lambda a, i: i * cols + p * rows + a,
            left,
            lambda i: i * cols,
        )
        for t, value in enumerate(sums):
            d_right[tile(p * cells + t * 8), :] = value
        return carry

    lax.fori_loop(0, cols // rows, right_block, 0)
    scale = 1.0 / (rows * groups)
    small_grads[:, :channels] = dot(normed[...], d_gate[...], BY_ROWS) * scale
    small_grads[:, channels:] = dot(tri_norm[...], d_update[...], BY_ROWS) * scale


def late_kernel(
    sizes,
    params,
    pair,
    d_tri_ref,
    d_gate,
    left,
    right,
    normed,
    d_left,
    d_right,
    left_gate_0,
    left_gate_1,
    left_value_0,
    left_value_1,
    right_gate_0,
    right_gate_1,
    right_value_0,
    right_value_1,
    proj_weight,
    gate_weight,
    pair_grad,
    proj_grad,
    source,
    d_right_s,
    d_proj,
):
    rows, cols, groups = sizes
    cells = rows * cols
    hidden = left.shape[-1]
    half = lax.axis_index("col")
    me = lax.axis_index("row")
    zeros = (jnp.zeros((8, hidden), F32),) * (rows * cols // 8)
    source[...] = d_tri_ref[...].astype(F32)
    d_right_s[at(half, cols * cols), :] = d_right[...]

    def right_block(p, carry):
        sums = contract(
            rows,
            cols,
            rows * groups,
            8,
            zeros,
            source,
            lambda a, i: i * cols + p * rows + a,
            left,
            lambda i: i * cols,
        )
        start = (1 - half) * cols * cols + p * cells
        for t, value in enumerate(sums):
            d_right_s[tile(start + t * 8), :] = value
        return carry

    lax.fori_loop(0, cols // rows, right_block, 0)

    for which, left_gate, left_value, right_gate, right_value in (
        (0, left_gate_0, left_value_0, right_gate_0, right_value_0),
        (1, left_gate_1, left_value_1, right_gate_1, right_value_1),
    ):

        def left_block(
            b,
            carry,
            which=which,
            left_gate=left_gate,
            left_value=left_value,
            right_gate=right_gate,
            right_value=right_value,
        ):
            p = row_block(which, b)
            start = p * cells
            sums = contract(
                rows,
                cols,
                cols,
                8,
                tuple(d_left[tile(start + t * 8), :] for t in range(cells // 8)),
                source,
                lambda a, j: (p * rows + a) * cols + j,
                right,
                lambda j: ((1 - half) * cols + j) * cols,
            )
            part, place = at(b, cells), at(p, cells)
            grads = jnp.concatenate(sums, axis=0)
            d_proj[place, :hidden] = (grads * left_value[part, :]).astype(BF16)
            d_proj[place, hidden : 2 * hidden] = (grads * left_gate[part, :]).astype(BF16)
            grads = d_right_s[place, :]
            d_proj[place, 2 * hidden : 3 * hidden] = (grads * right_value[part, :]).astype(BF16)
            d_proj[place, 3 * hidden :] = (grads * right_gate[part, :]).astype(BF16)
            return carry

        lax.fori_loop(0, groups // 2, left_block, 0)

    scale = 1.0 / (rows * groups)
    proj_grad[...] = dot(normed[...], d_proj[...], BY_ROWS) * scale
    own = at(me, cells)
    d_normed = dot(d_proj[own, :], proj_weight[...], TRANSPOSED) + dot(
        d_gate[own, :], gate_weight[...], TRANSPOSED
    )
    gain = params[0:1, :]
    _, hat, inverse = layer_norm(pair[...].astype(F32), gain, params[1:2, :])
    pair_grad[...] = norm_back(d_normed, gain, hat, inverse)


def replicated(
    pair_rep,
    cotangent,
    norm_gain,
    norm_bias,
    proj_weight,
    gate_weight,
    tri_gain,
    tri_bias,
    out_weight,
):
    rows, cols, channels = pair_rep.shape
    hidden = tri_gain.shape[0]
    groups = lax.axis_size("row")
    cells = rows * cols
    every = cells * groups
    some = every // 2
    sizes = (rows, cols, groups)

    def call(kernel, outs, *args, scratch=(), micros=1, name):
        cost = pl.CostEstimate(flops=micros * 10**9, bytes_accessed=0, transcendentals=0)
        return pl.pallas_call(
            functools.partial(kernel, sizes),
            out_shape=[jax.ShapeDtypeStruct(*out) for out in outs],
            scratch_shapes=[pltpu.VMEM(*one) for one in scratch],
            compiler_params=pltpu.CompilerParams(vmem_limit_bytes=VMEM_BUDGET),
            cost_estimate=cost,
            name=name,
        )(*args)

    def across(value, mask):
        return lax.ppermute(value, "row", [(i, i ^ mask) for i in range(groups)])

    def over(value):
        return lax.ppermute(value, "col", SWAP)

    def along(value):
        return [across(value, 2 * s) for s in range(1, groups // 2)]

    def join(*values):
        return jnp.concatenate(values, axis=0)

    def after(value, *others):
        return lax.optimization_barrier((value, *others))[0]

    full, part = (every, hidden), (some, hidden)

    def own_edges(*blocks):
        outs = [((some, channels), BF16)] + [(part, F32)] * 6
        return call(own_edges_kernel, outs, params, proj_weight, *blocks, name="own_edges")

    def mate_edges(*blocks):
        outs = [(part, F32)] * 2
        return call(mate_edges_kernel, outs, params, proj_weight, *blocks, name="mate_edges")

    pair = pair_rep.reshape(cells, channels)
    cot = cotangent.reshape(cells, channels)
    params = jnp.stack([norm_gain, norm_bias, tri_gain, tri_bias])
    pair_far = across(pair, 1)
    near = along(pair)
    mate_pair = over(pair)
    cot_far = across(after(cot, params), 1)
    far = along(pair_far)
    near_all = join(*near)
    own_0 = own_edges(pair, near_all)
    mate_0 = mate_edges(mate_pair, over(near_all))
    cots = join(cot, cot_far)
    cots = [cots] + along(after(cots, own_0[0]))
    far_all = after(join(pair_far, *far), own_0[0], mate_0[0])
    own_1 = own_edges(far_all)
    mate_1 = mate_edges(over(far_all))
    own, mate = (own_0, own_1), (mate_0, mate_1)
    normed = [o[0] for o in own]
    left, left_gate, left_value = ([o[n] for o in own] for n in (1, 2, 3))
    right, right_gate, right_value = ([o[n] for o in own] for n in (4, 5, 6))
    (tri,) = call(
        triangle_kernel,
        [(full, F32)],
        *left,
        *(m[0] for m in mate),
        *right,
        *(m[1] for m in mate),
        scratch=[((cols * cols, hidden), F32)] * 2,
        micros=2,
        name="triangle",
    )
    block_out, d_tri, d_gate, tri_norm, d_update = call(
        cells_kernel,
        [((cells, channels), BF16)] + [(full, BF16)] * 4,
        params,
        tri,
        *normed,
        gate_weight,
        out_weight,
        *cots,
        micros=2,
        name="cells",
    )
    d_tri_mate = over(d_tri)
    left_all, right_all, normed_all, d_left, d_right, small_grads = call(
        early_kernel,
        [
            (full, F32),
            (full, F32),
            ((every, channels), BF16),
            (full, F32),
            (part, F32),
            ((channels, 2 * channels), F32),
        ],
        d_tri,
        d_gate,
        tri_norm,
        d_update,
        *normed,
        *left,
        *right,
        scratch=[(full, F32)],
        micros=3,
        name="early",
    )
    small_mate = over(small_grads)
    pair_grad, proj_grad = call(
        late_kernel,
        [((cells, channels), F32), ((channels, 4 * hidden), F32)],
        params,
        pair,
        d_tri_mate,
        d_gate,
        left_all,
        right_all,
        normed_all,
        d_left,
        d_right,
        *left_gate,
        *left_value,
        *right_gate,
        *right_value,
        proj_weight,
        gate_weight,
        scratch=[(full, F32), (full, F32), ((every, 4 * hidden), BF16)],
        micros=4,
        name="late",
    )
    small = small_grads + small_mate
    return (
        block_out.reshape(pair_rep.shape),
        pair_grad.reshape(pair_rep.shape),
        proj_grad + over(proj_grad),
        small[:, :channels],
        small[:, channels:],
    )


def sharded(
    pair_rep,
    cotangent,
    norm_gain,
    norm_bias,
    proj_weight,
    gate_weight,
    tri_gain,
    tri_bias,
    out_weight,
):
    f32 = jnp.float32
    bf16 = jnp.bfloat16
    hidden = tri_gain.shape[0]
    channels = norm_gain.shape[0]
    row_count = pair_rep.shape[0]
    col_count = pair_rep.shape[1]
    crop_len = row_count * lax.axis_size("row")
    normed_f, pair_hat, pair_inv = layer_norm(pair_rep.astype(f32), norm_gain, norm_bias)
    normed = normed_f.astype(bf16)
    projected = jnp.einsum("ijc,cd->ijd", normed, proj_weight, preferred_element_type=f32)
    sig_left = jax.nn.sigmoid(projected[..., 0:hidden])
    val_left = projected[..., hidden : 2 * hidden]
    sig_right = jax.nn.sigmoid(projected[..., 2 * hidden : 3 * hidden])
    val_right = projected[..., 3 * hidden : 4 * hidden]
    left_edge = (sig_left * val_left).astype(bf16)
    right_edge = (sig_right * val_right).astype(bf16)
    out_gate = jax.nn.sigmoid(
        jnp.einsum("ijc,cd->ijd", normed, gate_weight, preferred_element_type=f32)
    )
    right_all = lax.all_gather(right_edge, "row", axis=0, tiled=True)
    block = right_all
    triangle = lax.psum_scatter(
        jnp.einsum("ikc,jkc->jic", left_edge, block, preferred_element_type=f32),
        "col",
        scatter_dimension=0,
        tiled=True,
    ).transpose(1, 0, 2)
    tri_f, tri_hat, tri_inv = layer_norm(triangle, tri_gain, tri_bias)
    tri_norm = tri_f.astype(bf16)
    update = jnp.einsum("ijh,hc->ijc", tri_norm, out_weight, preferred_element_type=f32)
    block_out = (out_gate * update).astype(bf16)
    cot = cotangent.astype(f32)
    d_update = (cot * out_gate).astype(bf16)
    d_gate = (cot * update * out_gate * (1.0 - out_gate)).astype(bf16)
    d_norm = jnp.einsum("ijc,hc->ijh", d_update, out_weight, preferred_element_type=f32)
    d_triangle = norm_back(d_norm, tri_gain, tri_hat, tri_inv).astype(bf16)
    tri_rows = lax.all_gather(d_triangle, "col", axis=1, tiled=True)
    d_left = jnp.einsum("ijc,jkc->ikc", tri_rows, right_all, preferred_element_type=f32)
    tri_cols = lax.all_to_all(tri_rows, "row", split_axis=1, concat_axis=0, tiled=True)
    block = tri_cols
    d_right = jnp.einsum(
        "ijc,ikc->jkc",
        block,
        lax.all_gather(left_edge, "row", axis=0, tiled=True),
        preferred_element_type=f32,
    )
    d_proj = jnp.concatenate(
        [
            d_left * val_left * sig_left * (1.0 - sig_left),
            d_left * sig_left,
            d_right * val_right * sig_right * (1.0 - sig_right),
            d_right * sig_right,
        ],
        axis=-1,
    ).astype(bf16)
    d_normed = jnp.einsum(
        "ijd,cd->ijc", d_proj, proj_weight, preferred_element_type=f32
    ) + jnp.einsum("ijd,cd->ijc", d_gate, gate_weight, preferred_element_type=f32)
    pair_grad = norm_back(d_normed, norm_gain, pair_hat, pair_inv)
    cells = row_count * col_count
    flat_norm = normed.reshape(cells, channels)
    local_proj = (
        jnp.dot(flat_norm.T, d_proj.reshape(cells, 4 * hidden), preferred_element_type=f32)
        / crop_len
    )
    local_gate = (
        jnp.dot(flat_norm.T, d_gate.reshape(cells, channels), preferred_element_type=f32) / crop_len
    )
    local_out = (
        jnp.dot(
            tri_norm.reshape(cells, hidden).T,
            d_update.reshape(cells, channels),
            preferred_element_type=f32,
        )
        / crop_len
    )
    proj_grad, gate_grad, out_grad = lax.psum((local_proj, local_gate, local_out), ("row", "col"))
    return (block_out, pair_grad, proj_grad, gate_grad, out_grad)


def local(pair_rep, *others):
    rows, cols, channels = pair_rep.shape
    hidden = others[7].shape[0]
    groups = lax.axis_size("row")
    every = rows * groups * cols
    fits = 24 * every * channels * 4 <= VMEM_BUDGET and hidden == channels
    paired = lax.axis_size("col") == 2 and groups & (groups - 1) == 0 and groups >= 2
    whole_tiles = cols % 8 == 0 and cols % (2 * rows) == 0 and rows * cols % 16 == 0
    plan = replicated if fits and paired and whole_tiles else sharded
    return plan(pair_rep, *others)


def solution(mesh):
    return jax.shard_map(
        local,
        mesh=mesh,
        in_specs=(
            P(("crop", "row"), "col", None),
            P(("crop", "row"), "col", None),
            P(),
            P(),
            P(),
            P(),
            P(),
            P(),
            P(),
        ),
        out_specs=(
            P(("crop", "row"), "col", None),
            P(("crop", "row"), "col", None),
            P("crop", None),
            P("crop", None),
            P("crop", None),
        ),
        check_vma=False,
    )
```

```python
import functools

import jax
import jax.numpy as jnp
from jax import lax
from jax.experimental import pallas as pl
from jax.experimental.pallas import tpu as pltpu
from jax.sharding import PartitionSpec as P

F32 = jnp.float32
BF16 = jnp.bfloat16
VMEM_BUDGET = 24 * 2**20
SWAP = ((0, 1), (1, 0))
NATIVE = ((1,), (0,))
BY_ROWS = ((0,), (0,))
TRANSPOSED = ((1,), (1,))


def layer_norm(values, gain, bias):
    centred = values - jnp.mean(values, axis=-1, keepdims=True)
    inverse = lax.rsqrt(jnp.mean(centred * centred, axis=-1, keepdims=True) + 1e-05)
    scaled = centred * inverse
    return (scaled * gain + bias, scaled, inverse)


def norm_back(grads, gain, scaled, inverse):
    weighted = grads * gain
    first = jnp.mean(weighted, axis=-1, keepdims=True)
    second = jnp.mean(weighted * scaled, axis=-1, keepdims=True)
    return inverse * (weighted - first - scaled * second)


def sigmoid(values):
    return 0.5 * jnp.tanh(0.5 * values) + 0.5


def dot(a, b, contract=NATIVE):
    return lax.dot_general(a, b, (contract, ((), ())), preferred_element_type=F32)


def at(index, size):
    return pl.ds(pl.multiple_of(index * size, size), size)


def tile(start):
    return pl.ds(pl.multiple_of(start, 8), 8)


def places(groups):
    me = lax.axis_index("row")
    return [lax.bitwise_xor(me // 2, t) for t in range(groups // 2)]


def row_block(which, b):
    me = lax.axis_index("row")
    parity = lax.rem(me, 2)
    return 2 * b + (parity if which == 0 else 1 - parity)


def edges(blocks, params, proj_weight):
    hidden = proj_weight.shape[1] // 4
    values = jnp.concatenate([block[...] for block in blocks], axis=0).astype(F32)
    normed = layer_norm(values, params[0:1, :], params[1:2, :])[0].astype(BF16)
    projected = dot(normed, proj_weight[...])
    sides = []
    for start in (0, 2 * hidden):
        gate = sigmoid(projected[:, start : start + hidden])
        edge = gate * projected[:, start + hidden : start + 2 * hidden]
        sides.append((edge.astype(BF16).astype(F32), gate, edge * (1.0 - gate)))
    return normed, sides


def own_edges_kernel(sizes, params, weight, *refs):
    rows, cols, groups = sizes
    cells = rows * cols
    blocks, normed_out, outs = refs[:-7], refs[-7], refs[-6:]
    normed, sides = edges(blocks, params, weight)
    for t, b in enumerate(places(groups)):
        part = slice(t * cells, (t + 1) * cells)
        place = at(b, cells)
        normed_out[place, :] = normed[part]
        for out, value in zip(outs, sides[0] + sides[1], strict=True):
            out[place, :] = value[part]


def mate_edges_kernel(sizes, params, weight, *refs):
    rows, cols, groups = sizes
    cells = rows * cols
    blocks, left, right = refs[:-2], refs[-2], refs[-1]
    _, sides = edges(blocks, params, weight)
    for t, b in enumerate(places(groups)):
        part = slice(t * cells, (t + 1) * cells)
        left[at(b, cells), :] = sides[0][0][part]
        right[at(b, cells), :] = sides[1][0][part]


def triangle_kernel(sizes, *refs):
    rows, cols, groups = sizes
    cells = rows * cols
    lefts, rights, (tri,), picked = refs[:4], refs[4:8], refs[8:9], refs[9:]
    hidden = tri.shape[-1]
    half = lax.axis_index("col")
    zero = jnp.zeros((8, hidden), F32)
    count = cols // 8
    blocks = cols // rows
    for side in range(2):
        for which in range(2):
            for s in range(blocks // 2):
                b = half * (blocks // 2) + s
                p = row_block(which, b) - half * blocks
                picked[side][at(p, cells), :] = rights[2 * side + which][at(b, cells), :]

    for which in range(2):

        def tri_block(b, carry, which=which):
            def step(k, sums):
                new = list(sums)
                for side in range(2):
                    left = lefts[2 * side + which]
                    tiles = [
                        picked[side][pl.ds(t * 8 * cols + k, 8, stride=cols), :]
                        for t in range(count)
                    ]
                    for a in range(rows):
                        row = left[pl.ds((b * rows + a) * cols + k, 1), :]
                        for t in range(count):
                            new[a * count + t] += row * tiles[t]
                return tuple(new)

            sums = lax.fori_loop(0, cols, step, (zero,) * (rows * count), unroll=4)
            start = row_block(which, b) * cells
            for t, value in enumerate(sums):
                tri[tile(start + t * 8), :] = value
            return carry

        lax.fori_loop(0, groups // 2, tri_block, 0)


def cells_kernel(
    sizes,
    params,
    tri,
    normed_0,
    normed_1,
    gate_weight,
    out_weight,
    *refs,
):
    rows, cols, groups = sizes
    cells = rows * cols
    cots, (block_out, d_tri, d_gate, tri_norm_out, d_update_out) = refs[:-5], refs[-5:]
    gain, bias = params[2:3, :], params[3:4, :]
    for which, normed in ((0, normed_0), (1, normed_1)):
        for t, b in enumerate(places(groups)):
            cot = cots[which][t * cells : (t + 1) * cells, :]
            place = at(row_block(which, b), cells)
            tri_f, hat, inverse = layer_norm(tri[place, :], gain, bias)
            tri_norm = tri_f.astype(BF16)
            update = dot(tri_norm, out_weight[...])
            out_gate = sigmoid(dot(normed[at(b, cells), :], gate_weight[...]))
            if which == 0 and t == 0:
                block_out[...] = (out_gate * update).astype(BF16)
            gated = cot.astype(F32) * out_gate
            d_update = gated.astype(BF16)
            d_gate[place, :] = (gated * update * (1.0 - out_gate)).astype(BF16)
            d_norm = dot(d_update, out_weight[...], TRANSPOSED)
            d_tri[place, :] = norm_back(d_norm, gain, hat, inverse).astype(BF16)
            tri_norm_out[place, :] = tri_norm
            d_update_out[place, :] = d_update


def contract(rows, cols, count, unroll, start, source, row_at, operand, operand_at):
    tiles = cols // 8

    def step(term, sums):
        new = list(sums)
        loaded = [operand[tile(operand_at(term) + t * 8), :] for t in range(tiles)]
        for a in range(rows):
            row = source[pl.ds(row_at(a, term), 1), :]
            for t in range(tiles):
                new[a * tiles + t] += row * loaded[t]
        return tuple(new)

    return lax.fori_loop(0, count, step, start, unroll=unroll)


def early_kernel(
    sizes,
    d_tri_ref,
    d_gate,
    tri_norm,
    d_update,
    normed_0,
    normed_1,
    left_0,
    left_1,
    right_0,
    right_1,
    left,
    right,
    normed,
    d_left,
    d_right,
    small_grads,
    source,
):
    rows, cols, groups = sizes
    cells = rows * cols
    hidden = left.shape[-1]
    channels = normed.shape[-1]
    half = lax.axis_index("col")
    zeros = (jnp.zeros((8, hidden), F32),) * (rows * cols // 8)
    source[...] = d_tri_ref[...].astype(F32)
    for which, part_n, part_l, part_r in (
        (0, normed_0, left_0, right_0),
        (1, normed_1, left_1, right_1),
    ):
        for b in range(groups // 2):
            place, part = at(row_block(which, b), cells), slice(b * cells, (b + 1) * cells)
            normed[place, :] = part_n[part, :]
            left[place, :] = part_l[part, :]
            right[place, :] = part_r[part, :]

    def left_block(p, carry):
        sums = contract(
            rows,
            cols,
            cols,
            8,
            zeros,
            source,
            lambda a, j: (p * rows + a) * cols + j,
            right,
            lambda j: (half * cols + j) * cols,
        )
        for t, value in enumerate(sums):
            d_left[tile(p * cells + t * 8), :] = value
        return carry

    lax.fori_loop(0, groups, left_block, 0)

    def right_block(p, carry):
        sums = contract(
            rows,
            cols,
            rows * groups,
            8,
            zeros,
            source,
            lambda a, i: i * cols + p * rows + a,
            left,
            lambda i: i * cols,
        )
        for t, value in enumerate(sums):
            d_right[tile(p * cells + t * 8), :] = value
        return carry

    lax.fori_loop(0, cols // rows, right_block, 0)
    scale = 1.0 / (rows * groups)
    small_grads[:, :channels] = dot(normed[...], d_gate[...], BY_ROWS) * scale
    small_grads[:, channels:] = dot(tri_norm[...], d_update[...], BY_ROWS) * scale


def late_kernel(
    sizes,
    params,
    pair,
    d_tri_ref,
    d_gate,
    left,
    right,
    normed,
    d_left,
    d_right,
    left_gate_0,
    left_gate_1,
    left_value_0,
    left_value_1,
    right_gate_0,
    right_gate_1,
    right_value_0,
    right_value_1,
    proj_weight,
    gate_weight,
    pair_grad,
    proj_grad,
    source,
    d_right_s,
    d_proj,
):
    rows, cols, groups = sizes
    cells = rows * cols
    hidden = left.shape[-1]
    half = lax.axis_index("col")
    me = lax.axis_index("row")
    zeros = (jnp.zeros((8, hidden), F32),) * (rows * cols // 8)
    source[...] = d_tri_ref[...].astype(F32)
    d_right_s[at(half, cols * cols), :] = d_right[...]

    def right_block(p, carry):
        sums = contract(
            rows,
            cols,
            rows * groups,
            8,
            zeros,
            source,
            lambda a, i: i * cols + p * rows + a,
            left,
            lambda i: i * cols,
        )
        start = (1 - half) * cols * cols + p * cells
        for t, value in enumerate(sums):
            d_right_s[tile(start + t * 8), :] = value
        return carry

    lax.fori_loop(0, cols // rows, right_block, 0)

    for which, left_gate, left_value, right_gate, right_value in (
        (0, left_gate_0, left_value_0, right_gate_0, right_value_0),
        (1, left_gate_1, left_value_1, right_gate_1, right_value_1),
    ):

        def left_block(
            b,
            carry,
            which=which,
            left_gate=left_gate,
            left_value=left_value,
            right_gate=right_gate,
            right_value=right_value,
        ):
            p = row_block(which, b)
            start = p * cells
            sums = contract(
                rows,
                cols,
                cols,
                8,
                tuple(d_left[tile(start + t * 8), :] for t in range(cells // 8)),
                source,
                lambda a, j: (p * rows + a) * cols + j,
                right,
                lambda j: ((1 - half) * cols + j) * cols,
            )
            part, place = at(b, cells), at(p, cells)
            grads = jnp.concatenate(sums, axis=0)
            d_proj[place, :hidden] = (grads * left_value[part, :]).astype(BF16)
            d_proj[place, hidden : 2 * hidden] = (grads * left_gate[part, :]).astype(BF16)
            grads = d_right_s[place, :]
            d_proj[place, 2 * hidden : 3 * hidden] = (grads * right_value[part, :]).astype(BF16)
            d_proj[place, 3 * hidden :] = (grads * right_gate[part, :]).astype(BF16)
            return carry

        lax.fori_loop(0, groups // 2, left_block, 0)

    scale = 1.0 / (rows * groups)
    proj_grad[...] = dot(normed[...], d_proj[...], BY_ROWS) * scale
    own = at(me, cells)
    d_normed = dot(d_proj[own, :], proj_weight[...], TRANSPOSED) + dot(
        d_gate[own, :], gate_weight[...], TRANSPOSED
    )
    gain = params[0:1, :]
    _, hat, inverse = layer_norm(pair[...].astype(F32), gain, params[1:2, :])
    pair_grad[...] = norm_back(d_normed, gain, hat, inverse)


def replicated(
    pair_rep,
    cotangent,
    norm_gain,
    norm_bias,
    proj_weight,
    gate_weight,
    tri_gain,
    tri_bias,
    out_weight,
):
    rows, cols, channels = pair_rep.shape
    hidden = tri_gain.shape[0]
    groups = lax.axis_size("row")
    cells = rows * cols
    every = cells * groups
    some = every // 2
    sizes = (rows, cols, groups)

    def call(kernel, outs, *args, scratch=(), micros=1, name):
        cost = pl.CostEstimate(flops=micros * 10**8, bytes_accessed=0, transcendentals=0)
        return pl.pallas_call(
            functools.partial(kernel, sizes),
            out_shape=[jax.ShapeDtypeStruct(*out) for out in outs],
            scratch_shapes=[pltpu.VMEM(*one) for one in scratch],
            compiler_params=pltpu.CompilerParams(vmem_limit_bytes=VMEM_BUDGET),
            cost_estimate=cost,
            name=name,
        )(*args)

    def across(value, mask):
        return lax.ppermute(value, "row", [(i, i ^ mask) for i in range(groups)])

    def over(value):
        return lax.ppermute(value, "col", SWAP)

    def along(value):
        got = []
        for s in reversed(range(1, groups // 2)):
            arrived = across(value, 2 * s)
            got.append(after(arrived, got[-1]) if got else arrived)
        return got[::-1]

    def join(*values):
        return jnp.concatenate(values, axis=0)

    def after(value, *others):
        return lax.optimization_barrier((value, *others))[0]

    full, part = (every, hidden), (some, hidden)

    def own_edges(*blocks):
        outs = [((some, channels), BF16)] + [(part, F32)] * 6
        return call(own_edges_kernel, outs, params, proj_weight, *blocks, micros=7, name="own_edges")

    def mate_edges(*blocks):
        outs = [(part, F32)] * 2
        return call(mate_edges_kernel, outs, params, proj_weight, *blocks, micros=7, name="mate_edges")

    pair = pair_rep.reshape(cells, channels)
    cot = cotangent.reshape(cells, channels)
    params = jnp.stack([norm_gain, norm_bias, tri_gain, tri_bias])
    near = along(pair)
    pair_far = across(pair, 1)
    near_all = after(join(*near), params, pair_far)
    far = across(near_all, 1)
    own_0 = own_edges(pair, near_all)
    mate_0 = mate_edges(over(join(pair, near_all)))
    cot_near = join(cot, *along(cot))
    cot_far = across(cot_near, 1)
    far_all = after(join(pair_far, far), own_0[0], mate_0[0])
    own_1 = own_edges(far_all)
    mate_1 = mate_edges(over(far_all))
    own, mate = (own_0, own_1), (mate_0, mate_1)
    normed = [o[0] for o in own]
    left, left_gate, left_value = ([o[n] for o in own] for n in (1, 2, 3))
    right, right_gate, right_value = ([o[n] for o in own] for n in (4, 5, 6))
    (tri,) = call(
        triangle_kernel,
        [(full, F32)],
        *left,
        *(m[0] for m in mate),
        *right,
        *(m[1] for m in mate),
        scratch=[((cols * cols, hidden), F32)] * 2,
        micros=2,
        name="triangle",
    )
    block_out, d_tri, d_gate, tri_norm, d_update = call(
        cells_kernel,
        [((cells, channels), BF16)] + [(full, BF16)] * 4,
        params,
        tri,
        *normed,
        gate_weight,
        out_weight,
        cot_near,
        cot_far,
        micros=2,
        name="cells",
    )
    d_tri_mate = over(d_tri)
    left_all, right_all, normed_all, d_left, d_right, small_grads = call(
        early_kernel,
        [
            (full, F32),
            (full, F32),
            ((every, channels), BF16),
            (full, F32),
            (part, F32),
            ((channels, 2 * channels), F32),
        ],
        d_tri,
        d_gate,
        tri_norm,
        d_update,
        *normed,
        *left,
        *right,
        scratch=[(full, F32)],
        micros=3,
        name="early",
    )
    small_mate = over(small_grads)
    pair_grad, proj_grad = call(
        late_kernel,
        [((cells, channels), F32), ((channels, 4 * hidden), F32)],
        params,
        pair,
        d_tri_mate,
        d_gate,
        left_all,
        right_all,
        normed_all,
        d_left,
        d_right,
        *left_gate,
        *left_value,
        *right_gate,
        *right_value,
        proj_weight,
        gate_weight,
        scratch=[(full, F32), (full, F32), ((every, 4 * hidden), BF16)],
        micros=4,
        name="late",
    )
    small = small_grads + small_mate
    return (
        block_out.reshape(pair_rep.shape),
        pair_grad.reshape(pair_rep.shape),
        proj_grad + over(proj_grad),
        small[:, :channels],
        small[:, channels:],
    )


def sharded(
    pair_rep,
    cotangent,
    norm_gain,
    norm_bias,
    proj_weight,
    gate_weight,
    tri_gain,
    tri_bias,
    out_weight,
):
    f32 = jnp.float32
    bf16 = jnp.bfloat16
    hidden = tri_gain.shape[0]
    channels = norm_gain.shape[0]
    row_count = pair_rep.shape[0]
    col_count = pair_rep.shape[1]
    crop_len = row_count * lax.axis_size("row")
    normed_f, pair_hat, pair_inv = layer_norm(pair_rep.astype(f32), norm_gain, norm_bias)
    normed = normed_f.astype(bf16)
    projected = jnp.einsum("ijc,cd->ijd", normed, proj_weight, preferred_element_type=f32)
    sig_left = jax.nn.sigmoid(projected[..., 0:hidden])
    val_left = projected[..., hidden : 2 * hidden]
    sig_right = jax.nn.sigmoid(projected[..., 2 * hidden : 3 * hidden])
    val_right = projected[..., 3 * hidden : 4 * hidden]
    left_edge = (sig_left * val_left).astype(bf16)
    right_edge = (sig_right * val_right).astype(bf16)
    out_gate = jax.nn.sigmoid(
        jnp.einsum("ijc,cd->ijd", normed, gate_weight, preferred_element_type=f32)
    )
    right_all = lax.all_gather(right_edge, "row", axis=0, tiled=True)
    block = right_all
    triangle = lax.psum_scatter(
        jnp.einsum("ikc,jkc->jic", left_edge, block, preferred_element_type=f32),
        "col",
        scatter_dimension=0,
        tiled=True,
    ).transpose(1, 0, 2)
    tri_f, tri_hat, tri_inv = layer_norm(triangle, tri_gain, tri_bias)
    tri_norm = tri_f.astype(bf16)
    update = jnp.einsum("ijh,hc->ijc", tri_norm, out_weight, preferred_element_type=f32)
    block_out = (out_gate * update).astype(bf16)
    cot = cotangent.astype(f32)
    d_update = (cot * out_gate).astype(bf16)
    d_gate = (cot * update * out_gate * (1.0 - out_gate)).astype(bf16)
    d_norm = jnp.einsum("ijc,hc->ijh", d_update, out_weight, preferred_element_type=f32)
    d_triangle = norm_back(d_norm, tri_gain, tri_hat, tri_inv).astype(bf16)
    tri_rows = lax.all_gather(d_triangle, "col", axis=1, tiled=True)
    d_left = jnp.einsum("ijc,jkc->ikc", tri_rows, right_all, preferred_element_type=f32)
    tri_cols = lax.all_to_all(tri_rows, "row", split_axis=1, concat_axis=0, tiled=True)
    block = tri_cols
    d_right = jnp.einsum(
        "ijc,ikc->jkc",
        block,
        lax.all_gather(left_edge, "row", axis=0, tiled=True),
        preferred_element_type=f32,
    )
    d_proj = jnp.concatenate(
        [
            d_left * val_left * sig_left * (1.0 - sig_left),
            d_left * sig_left,
            d_right * val_right * sig_right * (1.0 - sig_right),
            d_right * sig_right,
        ],
        axis=-1,
    ).astype(bf16)
    d_normed = jnp.einsum(
        "ijd,cd->ijc", d_proj, proj_weight, preferred_element_type=f32
    ) + jnp.einsum("ijd,cd->ijc", d_gate, gate_weight, preferred_element_type=f32)
    pair_grad = norm_back(d_normed, norm_gain, pair_hat, pair_inv)
    cells = row_count * col_count
    flat_norm = normed.reshape(cells, channels)
    local_proj = (
        jnp.dot(flat_norm.T, d_proj.reshape(cells, 4 * hidden), preferred_element_type=f32)
        / crop_len
    )
    local_gate = (
        jnp.dot(flat_norm.T, d_gate.reshape(cells, channels), preferred_element_type=f32) / crop_len
    )
    local_out = (
        jnp.dot(
            tri_norm.reshape(cells, hidden).T,
            d_update.reshape(cells, channels),
            preferred_element_type=f32,
        )
        / crop_len
    )
    proj_grad, gate_grad, out_grad = lax.psum((local_proj, local_gate, local_out), ("row", "col"))
    return (block_out, pair_grad, proj_grad, gate_grad, out_grad)


def local(pair_rep, *others):
    rows, cols, channels = pair_rep.shape
    hidden = others[7].shape[0]
    groups = lax.axis_size("row")
    every = rows * groups * cols
    fits = 24 * every * channels * 4 <= VMEM_BUDGET and hidden == channels
    paired = lax.axis_size("col") == 2 and groups & (groups - 1) == 0 and groups >= 2
    whole_tiles = cols % 8 == 0 and cols % (2 * rows) == 0 and rows * cols % 16 == 0
    plan = replicated if fits and paired and whole_tiles else sharded
    return plan(pair_rep, *others)


def solution(mesh):
    return jax.shard_map(
        local,
        mesh=mesh,
        in_specs=(
            P(("crop", "row"), "col", None),
            P(("crop", "row"), "col", None),
            P(),
            P(),
            P(),
            P(),
            P(),
            P(),
            P(),
        ),
        out_specs=(
            P(("crop", "row"), "col", None),
            P(("crop", "row"), "col", None),
            P("crop", None),
            P("crop", None),
            P("crop", None),
        ),
        check_vma=False,
    )
```

```python
import functools

import jax
import jax.numpy as jnp
from jax import lax
from jax.experimental import pallas as pl
from jax.experimental.pallas import tpu as pltpu
from jax.sharding import PartitionSpec as P

F32 = jnp.float32
BF16 = jnp.bfloat16
VMEM_BUDGET = 24 * 2**20
SWAP = ((0, 1), (1, 0))
NATIVE = ((1,), (0,))
BY_ROWS = ((0,), (0,))
TRANSPOSED = ((1,), (1,))


def layer_norm(values, gain, bias):
    centred = values - jnp.mean(values, axis=-1, keepdims=True)
    inverse = lax.rsqrt(jnp.mean(centred * centred, axis=-1, keepdims=True) + 1e-05)
    scaled = centred * inverse
    return (scaled * gain + bias, scaled, inverse)


def norm_back(grads, gain, scaled, inverse):
    weighted = grads * gain
    first = jnp.mean(weighted, axis=-1, keepdims=True)
    second = jnp.mean(weighted * scaled, axis=-1, keepdims=True)
    return inverse * (weighted - first - scaled * second)


def sigmoid(values):
    return 0.5 * jnp.tanh(0.5 * values) + 0.5


def dot(a, b, contract=NATIVE):
    return lax.dot_general(a, b, (contract, ((), ())), preferred_element_type=F32)


def at(index, size):
    return pl.ds(pl.multiple_of(index * size, size), size)


def tile(start):
    return pl.ds(pl.multiple_of(start, 8), 8)


def places(groups):
    me = lax.axis_index("row")
    return [lax.bitwise_xor(me // 2, t) for t in range(groups // 2)]


def row_block(which, b):
    me = lax.axis_index("row")
    parity = lax.rem(me, 2)
    return 2 * b + (parity if which == 0 else 1 - parity)


def edges(blocks, params, proj_weight):
    hidden = proj_weight.shape[1] // 4
    values = jnp.concatenate([block[...] for block in blocks], axis=0).astype(F32)
    normed = layer_norm(values, params[0:1, :], params[1:2, :])[0].astype(BF16)
    projected = dot(normed, proj_weight[...])
    sides = []
    for start in (0, 2 * hidden):
        gate = sigmoid(projected[:, start : start + hidden])
        edge = gate * projected[:, start + hidden : start + 2 * hidden]
        sides.append((edge.astype(BF16).astype(F32), gate, edge * (1.0 - gate)))
    return normed, sides


def own_edges_kernel(sizes, params, weight, *refs):
    rows, cols, groups = sizes
    cells = rows * cols
    blocks, normed_out, outs = refs[:-7], refs[-7], refs[-6:]
    normed, sides = edges(blocks, params, weight)
    for t, b in enumerate(places(groups)):
        part = slice(t * cells, (t + 1) * cells)
        place = at(b, cells)
        normed_out[place, :] = normed[part]
        for out, value in zip(outs, sides[0] + sides[1], strict=True):
            out[place, :] = value[part]


def mate_edges_kernel(sizes, params, weight, *refs):
    rows, cols, groups = sizes
    cells = rows * cols
    blocks, left, right = refs[:-2], refs[-2], refs[-1]
    _, sides = edges(blocks, params, weight)
    for t, b in enumerate(places(groups)):
        part = slice(t * cells, (t + 1) * cells)
        left[at(b, cells), :] = sides[0][0][part]
        right[at(b, cells), :] = sides[1][0][part]


def triangle_kernel(sizes, *refs):
    rows, cols, groups = sizes
    cells = rows * cols
    lefts, rights, (tri,), picked = refs[:4], refs[4:8], refs[8:9], refs[9:]
    hidden = tri.shape[-1]
    half = lax.axis_index("col")
    zero = jnp.zeros((8, hidden), F32)
    count = cols // 8
    blocks = cols // rows
    for side in range(2):
        for which in range(2):
            for s in range(blocks // 2):
                b = half * (blocks // 2) + s
                p = row_block(which, b) - half * blocks
                picked[side][at(p, cells), :] = rights[2 * side + which][at(b, cells), :]

    for which in range(2):

        def tri_block(b, carry, which=which):
            def step(k, sums):
                new = list(sums)
                for side in range(2):
                    left = lefts[2 * side + which]
                    tiles = [
                        picked[side][pl.ds(t * 8 * cols + k, 8, stride=cols), :]
                        for t in range(count)
                    ]
                    for a in range(rows):
                        row = left[pl.ds((b * rows + a) * cols + k, 1), :]
                        for t in range(count):
                            new[a * count + t] += row * tiles[t]
                return tuple(new)

            sums = lax.fori_loop(0, cols, step, (zero,) * (rows * count), unroll=4)
            start = row_block(which, b) * cells
            for t, value in enumerate(sums):
                tri[tile(start + t * 8), :] = value
            return carry

        lax.fori_loop(0, groups // 2, tri_block, 0)


def cells_kernel(
    sizes,
    params,
    tri,
    normed_0,
    normed_1,
    gate_weight,
    out_weight,
    *refs,
):
    rows, cols, groups = sizes
    cells = rows * cols
    cots, (block_out, d_tri, d_gate, tri_norm_out, d_update_out) = refs[:-5], refs[-5:]
    gain, bias = params[2:3, :], params[3:4, :]
    for which, normed in ((0, normed_0), (1, normed_1)):
        for t, b in enumerate(places(groups)):
            cot = cots[t][which * cells : (which + 1) * cells, :]
            place = at(row_block(which, b), cells)
            tri_f, hat, inverse = layer_norm(tri[place, :], gain, bias)
            tri_norm = tri_f.astype(BF16)
            update = dot(tri_norm, out_weight[...])
            out_gate = sigmoid(dot(normed[at(b, cells), :], gate_weight[...]))
            if which == 0 and t == 0:
                block_out[...] = (out_gate * update).astype(BF16)
            gated = cot.astype(F32) * out_gate
            d_update = gated.astype(BF16)
            d_gate[place, :] = (gated * update * (1.0 - out_gate)).astype(BF16)
            d_norm = dot(d_update, out_weight[...], TRANSPOSED)
            d_tri[place, :] = norm_back(d_norm, gain, hat, inverse).astype(BF16)
            tri_norm_out[place, :] = tri_norm
            d_update_out[place, :] = d_update


def contract(rows, cols, count, unroll, start, source, row_at, operand, operand_at):
    tiles = cols // 8

    def step(term, sums):
        new = list(sums)
        loaded = [operand[tile(operand_at(term) + t * 8), :] for t in range(tiles)]
        for a in range(rows):
            row = source[pl.ds(row_at(a, term), 1), :]
            for t in range(tiles):
                new[a * tiles + t] += row * loaded[t]
        return tuple(new)

    return lax.fori_loop(0, count, step, start, unroll=unroll)


def early_kernel(
    sizes,
    d_tri_ref,
    d_gate,
    tri_norm,
    d_update,
    normed_0,
    normed_1,
    left_0,
    left_1,
    right_0,
    right_1,
    left,
    right,
    normed,
    d_left,
    d_right,
    small_grads,
    source,
):
    rows, cols, groups = sizes
    cells = rows * cols
    hidden = left.shape[-1]
    channels = normed.shape[-1]
    half = lax.axis_index("col")
    zeros = (jnp.zeros((8, hidden), F32),) * (rows * cols // 8)
    source[...] = d_tri_ref[...].astype(F32)
    for which, part_n, part_l, part_r in (
        (0, normed_0, left_0, right_0),
        (1, normed_1, left_1, right_1),
    ):
        for b in range(groups // 2):
            place, part = at(row_block(which, b), cells), slice(b * cells, (b + 1) * cells)
            normed[place, :] = part_n[part, :]
            left[place, :] = part_l[part, :]
            right[place, :] = part_r[part, :]

    def left_block(p, carry):
        sums = contract(
            rows,
            cols,
            cols,
            8,
            zeros,
            source,
            lambda a, j: (p * rows + a) * cols + j,
            right,
            lambda j: (half * cols + j) * cols,
        )
        for t, value in enumerate(sums):
            d_left[tile(p * cells + t * 8), :] = value
        return carry

    lax.fori_loop(0, groups, left_block, 0)

    def right_block(p, carry):
        sums = contract(
            rows,
            cols,
            rows * groups,
            8,
            zeros,
            source,
            lambda a, i: i * cols + p * rows + a,
            left,
            lambda i: i * cols,
        )
        for t, value in enumerate(sums):
            d_right[tile(p * cells + t * 8), :] = value
        return carry

    lax.fori_loop(0, cols // rows, right_block, 0)
    scale = 1.0 / (rows * groups)
    small_grads[:, :channels] = dot(normed[...], d_gate[...], BY_ROWS) * scale
    small_grads[:, channels:] = dot(tri_norm[...], d_update[...], BY_ROWS) * scale


def late_kernel(
    sizes,
    params,
    pair,
    d_tri_ref,
    d_gate,
    left,
    right,
    normed,
    d_left,
    d_right,
    left_gate_0,
    left_gate_1,
    left_value_0,
    left_value_1,
    right_gate_0,
    right_gate_1,
    right_value_0,
    right_value_1,
    proj_weight,
    gate_weight,
    pair_grad,
    proj_grad,
    source,
    d_right_s,
    d_proj,
):
    rows, cols, groups = sizes
    cells = rows * cols
    hidden = left.shape[-1]
    half = lax.axis_index("col")
    me = lax.axis_index("row")
    zeros = (jnp.zeros((8, hidden), F32),) * (rows * cols // 8)
    source[...] = d_tri_ref[...].astype(F32)
    d_right_s[at(half, cols * cols), :] = d_right[...]

    def right_block(p, carry):
        sums = contract(
            rows,
            cols,
            rows * groups,
            8,
            zeros,
            source,
            lambda a, i: i * cols + p * rows + a,
            left,
            lambda i: i * cols,
        )
        start = (1 - half) * cols * cols + p * cells
        for t, value in enumerate(sums):
            d_right_s[tile(start + t * 8), :] = value
        return carry

    lax.fori_loop(0, cols // rows, right_block, 0)

    for which, left_gate, left_value, right_gate, right_value in (
        (0, left_gate_0, left_value_0, right_gate_0, right_value_0),
        (1, left_gate_1, left_value_1, right_gate_1, right_value_1),
    ):

        def left_block(
            b,
            carry,
            which=which,
            left_gate=left_gate,
            left_value=left_value,
            right_gate=right_gate,
            right_value=right_value,
        ):
            p = row_block(which, b)
            start = p * cells
            sums = contract(
                rows,
                cols,
                cols,
                8,
                tuple(d_left[tile(start + t * 8), :] for t in range(cells // 8)),
                source,
                lambda a, j: (p * rows + a) * cols + j,
                right,
                lambda j: ((1 - half) * cols + j) * cols,
            )
            part, place = at(b, cells), at(p, cells)
            grads = jnp.concatenate(sums, axis=0)
            d_proj[place, :hidden] = (grads * left_value[part, :]).astype(BF16)
            d_proj[place, hidden : 2 * hidden] = (grads * left_gate[part, :]).astype(BF16)
            grads = d_right_s[place, :]
            d_proj[place, 2 * hidden : 3 * hidden] = (grads * right_value[part, :]).astype(BF16)
            d_proj[place, 3 * hidden :] = (grads * right_gate[part, :]).astype(BF16)
            return carry

        lax.fori_loop(0, groups // 2, left_block, 0)

    scale = 1.0 / (rows * groups)
    proj_grad[...] = dot(normed[...], d_proj[...], BY_ROWS) * scale
    own = at(me, cells)
    d_normed = dot(d_proj[own, :], proj_weight[...], TRANSPOSED) + dot(
        d_gate[own, :], gate_weight[...], TRANSPOSED
    )
    gain = params[0:1, :]
    _, hat, inverse = layer_norm(pair[...].astype(F32), gain, params[1:2, :])
    pair_grad[...] = norm_back(d_normed, gain, hat, inverse)


def replicated(
    pair_rep,
    cotangent,
    norm_gain,
    norm_bias,
    proj_weight,
    gate_weight,
    tri_gain,
    tri_bias,
    out_weight,
):
    rows, cols, channels = pair_rep.shape
    hidden = tri_gain.shape[0]
    groups = lax.axis_size("row")
    cells = rows * cols
    every = cells * groups
    some = every // 2
    sizes = (rows, cols, groups)

    def call(kernel, outs, *args, scratch=(), micros=1, name):
        cost = pl.CostEstimate(flops=micros * 10**10, bytes_accessed=0, transcendentals=0)
        return pl.pallas_call(
            functools.partial(kernel, sizes),
            out_shape=[jax.ShapeDtypeStruct(*out) for out in outs],
            scratch_shapes=[pltpu.VMEM(*one) for one in scratch],
            compiler_params=pltpu.CompilerParams(vmem_limit_bytes=VMEM_BUDGET),
            cost_estimate=cost,
            name=name,
        )(*args)

    def across(value, mask):
        return lax.ppermute(value, "row", [(i, i ^ mask) for i in range(groups)])

    def over(value):
        return lax.ppermute(value, "col", SWAP)

    def along(value, tied=False):
        got = []
        for s in reversed(range(1, groups // 2)):
            arrived = across(value, 2 * s)
            got.append(after(arrived, got[-1]) if got and tied else arrived)
        return got[::-1]

    def join(*values):
        return jnp.concatenate(values, axis=0)

    def after(value, *others):
        return lax.optimization_barrier((value, *others))[0]

    full, part = (every, hidden), (some, hidden)

    def own_edges(*blocks):
        outs = [((some, channels), BF16)] + [(part, F32)] * 6
        return call(own_edges_kernel, outs, params, proj_weight, *blocks, name="own_edges")

    def mate_edges(*blocks):
        outs = [(part, F32)] * 2
        return call(mate_edges_kernel, outs, params, proj_weight, *blocks, name="mate_edges")

    pair = pair_rep.reshape(cells, channels)
    cot = cotangent.reshape(cells, channels)
    params = jnp.stack([norm_gain, norm_bias, tri_gain, tri_bias])
    near = along(pair, tied=True)
    pair_far = across(pair, 1)
    cot_far = across(cot, 1)
    near_all = after(join(*near), params, pair_far, cot_far)
    far = across(near_all, 1)
    mate_near = over(join(pair, near_all))
    cots = after(join(cot, cot_far), near_all)
    own_0 = own_edges(pair, near_all)
    mate_0 = mate_edges(mate_near)
    far_all = after(join(pair_far, far), own_0[0], mate_0[0])
    cots = [cots] + along(cots)
    own_1 = own_edges(far_all)
    mate_1 = mate_edges(over(far_all))
    own, mate = (own_0, own_1), (mate_0, mate_1)
    normed = [o[0] for o in own]
    left, left_gate, left_value = ([o[n] for o in own] for n in (1, 2, 3))
    right, right_gate, right_value = ([o[n] for o in own] for n in (4, 5, 6))
    (tri,) = call(
        triangle_kernel,
        [(full, F32)],
        *left,
        *(m[0] for m in mate),
        *right,
        *(m[1] for m in mate),
        scratch=[((cols * cols, hidden), F32)] * 2,
        micros=2,
        name="triangle",
    )
    block_out, d_tri, d_gate, tri_norm, d_update = call(
        cells_kernel,
        [((cells, channels), BF16)] + [(full, BF16)] * 4,
        params,
        tri,
        *normed,
        gate_weight,
        out_weight,
        *cots,
        micros=2,
        name="cells",
    )
    d_tri_mate = over(d_tri)
    left_all, right_all, normed_all, d_left, d_right, small_grads = call(
        early_kernel,
        [
            (full, F32),
            (full, F32),
            ((every, channels), BF16),
            (full, F32),
            (part, F32),
            ((channels, 2 * channels), F32),
        ],
        d_tri,
        d_gate,
        tri_norm,
        d_update,
        *normed,
        *left,
        *right,
        scratch=[(full, F32)],
        micros=3,
        name="early",
    )
    small_mate = over(small_grads)
    pair_grad, proj_grad = call(
        late_kernel,
        [((cells, channels), F32), ((channels, 4 * hidden), F32)],
        params,
        pair,
        d_tri_mate,
        d_gate,
        left_all,
        right_all,
        normed_all,
        d_left,
        d_right,
        *left_gate,
        *left_value,
        *right_gate,
        *right_value,
        proj_weight,
        gate_weight,
        scratch=[(full, F32), (full, F32), ((every, 4 * hidden), BF16)],
        micros=4,
        name="late",
    )
    small = small_grads + small_mate
    return (
        block_out.reshape(pair_rep.shape),
        pair_grad.reshape(pair_rep.shape),
        proj_grad + over(proj_grad),
        small[:, :channels],
        small[:, channels:],
    )


def sharded(
    pair_rep,
    cotangent,
    norm_gain,
    norm_bias,
    proj_weight,
    gate_weight,
    tri_gain,
    tri_bias,
    out_weight,
):
    f32 = jnp.float32
    bf16 = jnp.bfloat16
    hidden = tri_gain.shape[0]
    channels = norm_gain.shape[0]
    row_count = pair_rep.shape[0]
    col_count = pair_rep.shape[1]
    crop_len = row_count * lax.axis_size("row")
    normed_f, pair_hat, pair_inv = layer_norm(pair_rep.astype(f32), norm_gain, norm_bias)
    normed = normed_f.astype(bf16)
    projected = jnp.einsum("ijc,cd->ijd", normed, proj_weight, preferred_element_type=f32)
    sig_left = jax.nn.sigmoid(projected[..., 0:hidden])
    val_left = projected[..., hidden : 2 * hidden]
    sig_right = jax.nn.sigmoid(projected[..., 2 * hidden : 3 * hidden])
    val_right = projected[..., 3 * hidden : 4 * hidden]
    left_edge = (sig_left * val_left).astype(bf16)
    right_edge = (sig_right * val_right).astype(bf16)
    out_gate = jax.nn.sigmoid(
        jnp.einsum("ijc,cd->ijd", normed, gate_weight, preferred_element_type=f32)
    )
    right_all = lax.all_gather(right_edge, "row", axis=0, tiled=True)
    block = right_all
    triangle = lax.psum_scatter(
        jnp.einsum("ikc,jkc->jic", left_edge, block, preferred_element_type=f32),
        "col",
        scatter_dimension=0,
        tiled=True,
    ).transpose(1, 0, 2)
    tri_f, tri_hat, tri_inv = layer_norm(triangle, tri_gain, tri_bias)
    tri_norm = tri_f.astype(bf16)
    update = jnp.einsum("ijh,hc->ijc", tri_norm, out_weight, preferred_element_type=f32)
    block_out = (out_gate * update).astype(bf16)
    cot = cotangent.astype(f32)
    d_update = (cot * out_gate).astype(bf16)
    d_gate = (cot * update * out_gate * (1.0 - out_gate)).astype(bf16)
    d_norm = jnp.einsum("ijc,hc->ijh", d_update, out_weight, preferred_element_type=f32)
    d_triangle = norm_back(d_norm, tri_gain, tri_hat, tri_inv).astype(bf16)
    tri_rows = lax.all_gather(d_triangle, "col", axis=1, tiled=True)
    d_left = jnp.einsum("ijc,jkc->ikc", tri_rows, right_all, preferred_element_type=f32)
    tri_cols = lax.all_to_all(tri_rows, "row", split_axis=1, concat_axis=0, tiled=True)
    block = tri_cols
    d_right = jnp.einsum(
        "ijc,ikc->jkc",
        block,
        lax.all_gather(left_edge, "row", axis=0, tiled=True),
        preferred_element_type=f32,
    )
    d_proj = jnp.concatenate(
        [
            d_left * val_left * sig_left * (1.0 - sig_left),
            d_left * sig_left,
            d_right * val_right * sig_right * (1.0 - sig_right),
            d_right * sig_right,
        ],
        axis=-1,
    ).astype(bf16)
    d_normed = jnp.einsum(
        "ijd,cd->ijc", d_proj, proj_weight, preferred_element_type=f32
    ) + jnp.einsum("ijd,cd->ijc", d_gate, gate_weight, preferred_element_type=f32)
    pair_grad = norm_back(d_normed, norm_gain, pair_hat, pair_inv)
    cells = row_count * col_count
    flat_norm = normed.reshape(cells, channels)
    local_proj = (
        jnp.dot(flat_norm.T, d_proj.reshape(cells, 4 * hidden), preferred_element_type=f32)
        / crop_len
    )
    local_gate = (
        jnp.dot(flat_norm.T, d_gate.reshape(cells, channels), preferred_element_type=f32) / crop_len
    )
    local_out = (
        jnp.dot(
            tri_norm.reshape(cells, hidden).T,
            d_update.reshape(cells, channels),
            preferred_element_type=f32,
        )
        / crop_len
    )
    proj_grad, gate_grad, out_grad = lax.psum((local_proj, local_gate, local_out), ("row", "col"))
    return (block_out, pair_grad, proj_grad, gate_grad, out_grad)


def local(pair_rep, *others):
    rows, cols, channels = pair_rep.shape
    hidden = others[7].shape[0]
    groups = lax.axis_size("row")
    every = rows * groups * cols
    fits = 24 * every * channels * 4 <= VMEM_BUDGET and hidden == channels
    paired = lax.axis_size("col") == 2 and groups & (groups - 1) == 0 and groups >= 2
    whole_tiles = cols % 8 == 0 and cols % (2 * rows) == 0 and rows * cols % 16 == 0
    plan = replicated if fits and paired and whole_tiles else sharded
    return plan(pair_rep, *others)


def solution(mesh):
    return jax.shard_map(
        local,
        mesh=mesh,
        in_specs=(
            P(("crop", "row"), "col", None),
            P(("crop", "row"), "col", None),
            P(),
            P(),
            P(),
            P(),
            P(),
            P(),
            P(),
        ),
        out_specs=(
            P(("crop", "row"), "col", None),
            P(("crop", "row"), "col", None),
            P("crop", None),
            P("crop", None),
            P("crop", None),
        ),
        check_vma=False,
    )
```

```python
import functools

import jax
import jax.numpy as jnp
from jax import lax
from jax.experimental import pallas as pl
from jax.experimental.pallas import tpu as pltpu
from jax.sharding import PartitionSpec as P

F32 = jnp.float32
BF16 = jnp.bfloat16
VMEM_BUDGET = 24 * 2**20
SWAP = ((0, 1), (1, 0))
NATIVE = ((1,), (0,))
BY_ROWS = ((0,), (0,))
TRANSPOSED = ((1,), (1,))


def layer_norm(values, gain, bias):
    centred = values - jnp.mean(values, axis=-1, keepdims=True)
    inverse = lax.rsqrt(jnp.mean(centred * centred, axis=-1, keepdims=True) + 1e-05)
    scaled = centred * inverse
    return (scaled * gain + bias, scaled, inverse)


def norm_back(grads, gain, scaled, inverse):
    weighted = grads * gain
    first = jnp.mean(weighted, axis=-1, keepdims=True)
    second = jnp.mean(weighted * scaled, axis=-1, keepdims=True)
    return inverse * (weighted - first - scaled * second)


def sigmoid(values):
    return 0.5 * jnp.tanh(0.5 * values) + 0.5


def dot(a, b, contract=NATIVE):
    return lax.dot_general(a, b, (contract, ((), ())), preferred_element_type=F32)


def at(index, size):
    return pl.ds(pl.multiple_of(index * size, size), size)


def tile(start):
    return pl.ds(pl.multiple_of(start, 8), 8)


def places(groups):
    me = lax.axis_index("row")
    return [lax.bitwise_xor(me // 2, t) for t in range(groups // 2)]


def row_block(which, b):
    me = lax.axis_index("row")
    parity = lax.rem(me, 2)
    return 2 * b + (parity if which == 0 else 1 - parity)


def edges(blocks, params, proj_weight):
    hidden = proj_weight.shape[1] // 4
    values = jnp.concatenate([block[...] for block in blocks], axis=0).astype(F32)
    normed = layer_norm(values, params[0:1, :], params[1:2, :])[0].astype(BF16)
    projected = dot(normed, proj_weight[...])
    sides = []
    for start in (0, 2 * hidden):
        gate = sigmoid(projected[:, start : start + hidden])
        edge = gate * projected[:, start + hidden : start + 2 * hidden]
        sides.append((edge.astype(BF16).astype(F32), gate, edge * (1.0 - gate)))
    return normed, sides


def own_edges_kernel(sizes, params, weight, *refs):
    rows, cols, groups = sizes
    cells = rows * cols
    blocks, normed_out, outs = refs[:-7], refs[-7], refs[-6:]
    normed, sides = edges(blocks, params, weight)
    for t, b in enumerate(places(groups)):
        part = slice(t * cells, (t + 1) * cells)
        place = at(b, cells)
        normed_out[place, :] = normed[part]
        for out, value in zip(outs, sides[0] + sides[1], strict=True):
            out[place, :] = value[part]


def mate_edges_kernel(sizes, params, weight, *refs):
    rows, cols, groups = sizes
    cells = rows * cols
    blocks, left, right = refs[:-2], refs[-2], refs[-1]
    _, sides = edges(blocks, params, weight)
    for t, b in enumerate(places(groups)):
        part = slice(t * cells, (t + 1) * cells)
        left[at(b, cells), :] = sides[0][0][part]
        right[at(b, cells), :] = sides[1][0][part]


def triangle_kernel(sizes, *refs):
    rows, cols, groups = sizes
    cells = rows * cols
    lefts, rights, (tri,), picked = refs[:4], refs[4:8], refs[8:9], refs[9:]
    hidden = tri.shape[-1]
    half = lax.axis_index("col")
    zero = jnp.zeros((8, hidden), F32)
    count = cols // 8
    blocks = cols // rows
    for side in range(2):
        for which in range(2):
            for s in range(blocks // 2):
                b = half * (blocks // 2) + s
                p = row_block(which, b) - half * blocks
                picked[side][at(p, cells), :] = rights[2 * side + which][at(b, cells), :]

    for which in range(2):

        def tri_block(b, carry, which=which):
            def step(k, sums):
                new = list(sums)
                for side in range(2):
                    left = lefts[2 * side + which]
                    tiles = [
                        picked[side][pl.ds(t * 8 * cols + k, 8, stride=cols), :]
                        for t in range(count)
                    ]
                    for a in range(rows):
                        row = left[pl.ds((b * rows + a) * cols + k, 1), :]
                        for t in range(count):
                            new[a * count + t] += row * tiles[t]
                return tuple(new)

            sums = lax.fori_loop(0, cols, step, (zero,) * (rows * count), unroll=4)
            start = row_block(which, b) * cells
            for t, value in enumerate(sums):
                tri[tile(start + t * 8), :] = value
            return carry

        lax.fori_loop(0, groups // 2, tri_block, 0)


def cells_kernel(
    sizes,
    params,
    tri,
    normed_0,
    normed_1,
    gate_weight,
    out_weight,
    *refs,
):
    rows, cols, groups = sizes
    cells = rows * cols
    cots, (block_out, d_tri, d_gate, tri_norm_out, d_update_out) = refs[:-5], refs[-5:]
    gain, bias = params[2:3, :], params[3:4, :]
    for which, normed in ((0, normed_0), (1, normed_1)):
        for t, b in enumerate(places(groups)):
            cot = cots[which][t * cells : (t + 1) * cells, :]
            place = at(row_block(which, b), cells)
            tri_f, hat, inverse = layer_norm(tri[place, :], gain, bias)
            tri_norm = tri_f.astype(BF16)
            update = dot(tri_norm, out_weight[...])
            out_gate = sigmoid(dot(normed[at(b, cells), :], gate_weight[...]))
            if which == 0 and t == 0:
                block_out[...] = (out_gate * update).astype(BF16)
            gated = cot.astype(F32) * out_gate
            d_update = gated.astype(BF16)
            d_gate[place, :] = (gated * update * (1.0 - out_gate)).astype(BF16)
            d_norm = dot(d_update, out_weight[...], TRANSPOSED)
            d_tri[place, :] = norm_back(d_norm, gain, hat, inverse).astype(BF16)
            tri_norm_out[place, :] = tri_norm
            d_update_out[place, :] = d_update


def contract(rows, cols, count, unroll, start, source, row_at, operand, operand_at):
    tiles = cols // 8

    def step(term, sums):
        new = list(sums)
        loaded = [operand[tile(operand_at(term) + t * 8), :] for t in range(tiles)]
        for a in range(rows):
            row = source[pl.ds(row_at(a, term), 1), :]
            for t in range(tiles):
                new[a * tiles + t] += row * loaded[t]
        return tuple(new)

    return lax.fori_loop(0, count, step, start, unroll=unroll)


def early_kernel(
    sizes,
    d_tri_ref,
    d_gate,
    tri_norm,
    d_update,
    normed_0,
    normed_1,
    left_0,
    left_1,
    right_0,
    right_1,
    left,
    right,
    normed,
    d_left,
    d_right,
    small_grads,
    source,
):
    rows, cols, groups = sizes
    cells = rows * cols
    hidden = left.shape[-1]
    channels = normed.shape[-1]
    half = lax.axis_index("col")
    zeros = (jnp.zeros((8, hidden), F32),) * (rows * cols // 8)
    source[...] = d_tri_ref[...].astype(F32)
    for which, part_n, part_l, part_r in (
        (0, normed_0, left_0, right_0),
        (1, normed_1, left_1, right_1),
    ):
        for b in range(groups // 2):
            place, part = at(row_block(which, b), cells), slice(b * cells, (b + 1) * cells)
            normed[place, :] = part_n[part, :]
            left[place, :] = part_l[part, :]
            right[place, :] = part_r[part, :]

    def left_block(p, carry):
        sums = contract(
            rows,
            cols,
            cols,
            8,
            zeros,
            source,
            lambda a, j: (p * rows + a) * cols + j,
            right,
            lambda j: (half * cols + j) * cols,
        )
        for t, value in enumerate(sums):
            d_left[tile(p * cells + t * 8), :] = value
        return carry

    lax.fori_loop(0, groups, left_block, 0)

    def right_block(p, carry):
        sums = contract(
            rows,
            cols,
            rows * groups,
            8,
            zeros,
            source,
            lambda a, i: i * cols + p * rows + a,
            left,
            lambda i: i * cols,
        )
        for t, value in enumerate(sums):
            d_right[tile(p * cells + t * 8), :] = value
        return carry

    lax.fori_loop(0, cols // rows, right_block, 0)
    scale = 1.0 / (rows * groups)
    small_grads[:, :channels] = dot(normed[...], d_gate[...], BY_ROWS) * scale
    small_grads[:, channels:] = dot(tri_norm[...], d_update[...], BY_ROWS) * scale


def late_kernel(
    sizes,
    d_tri_ref,
    left,
    right,
    normed,
    d_left,
    d_right,
    left_gate_0,
    left_gate_1,
    left_value_0,
    left_value_1,
    right_gate_0,
    right_gate_1,
    right_value_0,
    right_value_1,
    proj_grad,
    d_proj,
    source,
    d_right_s,
):
    rows, cols, groups = sizes
    cells = rows * cols
    hidden = left.shape[-1]
    half = lax.axis_index("col")
    zeros = (jnp.zeros((8, hidden), F32),) * (rows * cols // 8)
    source[...] = d_tri_ref[...].astype(F32)
    d_right_s[at(half, cols * cols), :] = d_right[...]

    def right_block(p, carry):
        sums = contract(
            rows,
            cols,
            rows * groups,
            8,
            zeros,
            source,
            lambda a, i: i * cols + p * rows + a,
            left,
            lambda i: i * cols,
        )
        start = (1 - half) * cols * cols + p * cells
        for t, value in enumerate(sums):
            d_right_s[tile(start + t * 8), :] = value
        return carry

    lax.fori_loop(0, cols // rows, right_block, 0)

    for which, left_gate, left_value, right_gate, right_value in (
        (0, left_gate_0, left_value_0, right_gate_0, right_value_0),
        (1, left_gate_1, left_value_1, right_gate_1, right_value_1),
    ):

        def left_block(
            b,
            carry,
            which=which,
            left_gate=left_gate,
            left_value=left_value,
            right_gate=right_gate,
            right_value=right_value,
        ):
            p = row_block(which, b)
            start = p * cells
            sums = contract(
                rows,
                cols,
                cols,
                8,
                tuple(d_left[tile(start + t * 8), :] for t in range(cells // 8)),
                source,
                lambda a, j: (p * rows + a) * cols + j,
                right,
                lambda j: ((1 - half) * cols + j) * cols,
            )
            part, place = at(b, cells), at(p, cells)
            grads = jnp.concatenate(sums, axis=0)
            d_proj[place, :hidden] = (grads * left_value[part, :]).astype(BF16)
            d_proj[place, hidden : 2 * hidden] = (grads * left_gate[part, :]).astype(BF16)
            grads = d_right_s[place, :]
            d_proj[place, 2 * hidden : 3 * hidden] = (grads * right_value[part, :]).astype(BF16)
            d_proj[place, 3 * hidden :] = (grads * right_gate[part, :]).astype(BF16)
            return carry

        lax.fori_loop(0, groups // 2, left_block, 0)

    scale = 1.0 / (rows * groups)
    proj_grad[...] = dot(normed[...], d_proj[...], BY_ROWS) * scale


def outputs_kernel(
    sizes,
    params,
    pair,
    d_proj,
    d_gate,
    proj_weight,
    gate_weight,
    block_in,
    small_own,
    small_mate,
    block_out,
    pair_grad,
    gate_grad,
    out_grad,
):
    rows, cols, _ = sizes
    cells = rows * cols
    own = at(lax.axis_index("row"), cells)
    d_normed = dot(d_proj[own, :], proj_weight[...], TRANSPOSED) + dot(
        d_gate[own, :], gate_weight[...], TRANSPOSED
    )
    gain = params[0:1, :]
    _, hat, inverse = layer_norm(pair[...].astype(F32), gain, params[1:2, :])
    pair_grad[...] = norm_back(d_normed, gain, hat, inverse)
    block_out[...] = block_in[...]
    channels = gate_grad.shape[1]
    small = small_own[...] + small_mate[...]
    gate_grad[...] = small[:, :channels]
    out_grad[...] = small[:, channels:]


def replicated(
    pair_rep,
    cotangent,
    norm_gain,
    norm_bias,
    proj_weight,
    gate_weight,
    tri_gain,
    tri_bias,
    out_weight,
):
    rows, cols, channels = pair_rep.shape
    hidden = tri_gain.shape[0]
    groups = lax.axis_size("row")
    cells = rows * cols
    every = cells * groups
    some = every // 2
    sizes = (rows, cols, groups)

    def call(kernel, outs, *args, scratch=(), micros=1, name):
        cost = pl.CostEstimate(flops=micros * 10**9, bytes_accessed=0, transcendentals=0)
        return pl.pallas_call(
            functools.partial(kernel, sizes),
            out_shape=[jax.ShapeDtypeStruct(*out) for out in outs],
            scratch_shapes=[pltpu.VMEM(*one) for one in scratch],
            compiler_params=pltpu.CompilerParams(vmem_limit_bytes=VMEM_BUDGET),
            cost_estimate=cost,
            name=name,
        )(*args)

    def across(value, mask):
        return lax.ppermute(value, "row", [(i, i ^ mask) for i in range(groups)])

    def over(value):
        return lax.ppermute(value, "col", SWAP)

    def along(value, tied=False):
        got = []
        for s in reversed(range(1, groups // 2)):
            arrived = across(value, 2 * s)
            got.append(after(arrived, got[-1]) if got and tied else arrived)
        return got[::-1]

    def join(*values):
        return jnp.concatenate(values, axis=0)

    def after(value, *others):
        return lax.optimization_barrier((value, *others))[0]

    full, part = (every, hidden), (some, hidden)

    def own_edges(*blocks):
        outs = [((some, channels), BF16)] + [(part, F32)] * 6
        return call(own_edges_kernel, outs, params, proj_weight, *blocks, name="own_edges")

    def mate_edges(*blocks):
        outs = [(part, F32)] * 2
        return call(mate_edges_kernel, outs, params, proj_weight, *blocks, name="mate_edges")

    pair = pair_rep.reshape(cells, channels)
    cot = cotangent.reshape(cells, channels)
    params = jnp.stack([norm_gain, norm_bias, tri_gain, tri_bias])
    near = along(pair, tied=True)
    pair_far = across(after(pair, params), 1)
    near_all = after(join(*near), params)
    far = across(near_all, 1)
    mate_near = over(join(pair, near_all))
    cot_near = join(cot, *along(cot))
    cot_far = across(cot_near, 1)
    own_0 = own_edges(pair, near_all)
    mate_0 = mate_edges(mate_near)
    far_all = join(pair_far, far)
    own_1 = own_edges(far_all)
    mate_1 = mate_edges(over(far_all))
    own, mate = (own_0, own_1), (mate_0, mate_1)
    normed = [o[0] for o in own]
    left, left_gate, left_value = ([o[n] for o in own] for n in (1, 2, 3))
    right, right_gate, right_value = ([o[n] for o in own] for n in (4, 5, 6))
    (tri,) = call(
        triangle_kernel,
        [(full, F32)],
        *left,
        *(m[0] for m in mate),
        *right,
        *(m[1] for m in mate),
        scratch=[((cols * cols, hidden), F32)] * 2,
        micros=2,
        name="triangle",
    )
    block_out, d_tri, d_gate, tri_norm, d_update = call(
        cells_kernel,
        [((cells, channels), BF16)] + [(full, BF16)] * 4,
        params,
        tri,
        *normed,
        gate_weight,
        out_weight,
        cot_near,
        cot_far,
        micros=2,
        name="cells",
    )
    d_tri_mate = over(d_tri)
    left_all, right_all, normed_all, d_left, d_right, small_grads = call(
        early_kernel,
        [
            (full, F32),
            (full, F32),
            ((every, channels), BF16),
            (full, F32),
            (part, F32),
            ((channels, 2 * channels), F32),
        ],
        d_tri,
        d_gate,
        tri_norm,
        d_update,
        *normed,
        *left,
        *right,
        scratch=[(full, F32)],
        micros=30,
        name="early",
    )
    small_mate = over(small_grads)
    proj_grad, d_proj = call(
        late_kernel,
        [((channels, 4 * hidden), F32), ((every, 4 * hidden), BF16)],
        d_tri_mate,
        left_all,
        right_all,
        normed_all,
        d_left,
        d_right,
        *left_gate,
        *left_value,
        *right_gate,
        *right_value,
        scratch=[(full, F32), (full, F32)],
        micros=40,
        name="late",
    )
    proj_mate = over(proj_grad)
    square = ((channels, channels), F32)
    block_out, pair_grad, gate_grad, out_grad = call(
        outputs_kernel,
        [((cells, channels), BF16), ((cells, channels), F32), square, square],
        params,
        pair,
        d_proj,
        d_gate,
        proj_weight,
        gate_weight,
        block_out,
        small_grads,
        small_mate,
        name="outputs",
    )
    return (
        block_out.reshape(pair_rep.shape),
        pair_grad.reshape(pair_rep.shape),
        proj_grad + proj_mate,
        gate_grad,
        out_grad,
    )


def sharded(
    pair_rep,
    cotangent,
    norm_gain,
    norm_bias,
    proj_weight,
    gate_weight,
    tri_gain,
    tri_bias,
    out_weight,
):
    f32 = jnp.float32
    bf16 = jnp.bfloat16
    hidden = tri_gain.shape[0]
    channels = norm_gain.shape[0]
    row_count = pair_rep.shape[0]
    col_count = pair_rep.shape[1]
    crop_len = row_count * lax.axis_size("row")
    normed_f, pair_hat, pair_inv = layer_norm(pair_rep.astype(f32), norm_gain, norm_bias)
    normed = normed_f.astype(bf16)
    projected = jnp.einsum("ijc,cd->ijd", normed, proj_weight, preferred_element_type=f32)
    sig_left = jax.nn.sigmoid(projected[..., 0:hidden])
    val_left = projected[..., hidden : 2 * hidden]
    sig_right = jax.nn.sigmoid(projected[..., 2 * hidden : 3 * hidden])
    val_right = projected[..., 3 * hidden : 4 * hidden]
    left_edge = (sig_left * val_left).astype(bf16)
    right_edge = (sig_right * val_right).astype(bf16)
    out_gate = jax.nn.sigmoid(
        jnp.einsum("ijc,cd->ijd", normed, gate_weight, preferred_element_type=f32)
    )
    right_all = lax.all_gather(right_edge, "row", axis=0, tiled=True)
    block = right_all
    triangle = lax.psum_scatter(
        jnp.einsum("ikc,jkc->jic", left_edge, block, preferred_element_type=f32),
        "col",
        scatter_dimension=0,
        tiled=True,
    ).transpose(1, 0, 2)
    tri_f, tri_hat, tri_inv = layer_norm(triangle, tri_gain, tri_bias)
    tri_norm = tri_f.astype(bf16)
    update = jnp.einsum("ijh,hc->ijc", tri_norm, out_weight, preferred_element_type=f32)
    block_out = (out_gate * update).astype(bf16)
    cot = cotangent.astype(f32)
    d_update = (cot * out_gate).astype(bf16)
    d_gate = (cot * update * out_gate * (1.0 - out_gate)).astype(bf16)
    d_norm = jnp.einsum("ijc,hc->ijh", d_update, out_weight, preferred_element_type=f32)
    d_triangle = norm_back(d_norm, tri_gain, tri_hat, tri_inv).astype(bf16)
    tri_rows = lax.all_gather(d_triangle, "col", axis=1, tiled=True)
    d_left = jnp.einsum("ijc,jkc->ikc", tri_rows, right_all, preferred_element_type=f32)
    tri_cols = lax.all_to_all(tri_rows, "row", split_axis=1, concat_axis=0, tiled=True)
    block = tri_cols
    d_right = jnp.einsum(
        "ijc,ikc->jkc",
        block,
        lax.all_gather(left_edge, "row", axis=0, tiled=True),
        preferred_element_type=f32,
    )
    d_proj = jnp.concatenate(
        [
            d_left * val_left * sig_left * (1.0 - sig_left),
            d_left * sig_left,
            d_right * val_right * sig_right * (1.0 - sig_right),
            d_right * sig_right,
        ],
        axis=-1,
    ).astype(bf16)
    d_normed = jnp.einsum(
        "ijd,cd->ijc", d_proj, proj_weight, preferred_element_type=f32
    ) + jnp.einsum("ijd,cd->ijc", d_gate, gate_weight, preferred_element_type=f32)
    pair_grad = norm_back(d_normed, norm_gain, pair_hat, pair_inv)
    cells = row_count * col_count
    flat_norm = normed.reshape(cells, channels)
    local_proj = (
        jnp.dot(flat_norm.T, d_proj.reshape(cells, 4 * hidden), preferred_element_type=f32)
        / crop_len
    )
    local_gate = (
        jnp.dot(flat_norm.T, d_gate.reshape(cells, channels), preferred_element_type=f32) / crop_len
    )
    local_out = (
        jnp.dot(
            tri_norm.reshape(cells, hidden).T,
            d_update.reshape(cells, channels),
            preferred_element_type=f32,
        )
        / crop_len
    )
    proj_grad, gate_grad, out_grad = lax.psum((local_proj, local_gate, local_out), ("row", "col"))
    return (block_out, pair_grad, proj_grad, gate_grad, out_grad)


def local(pair_rep, *others):
    rows, cols, channels = pair_rep.shape
    hidden = others[7].shape[0]
    groups = lax.axis_size("row")
    every = rows * groups * cols
    fits = 24 * every * channels * 4 <= VMEM_BUDGET and hidden == channels
    paired = lax.axis_size("col") == 2 and groups & (groups - 1) == 0 and groups >= 2
    whole_tiles = cols % 8 == 0 and cols % (2 * rows) == 0 and rows * cols % 16 == 0
    plan = replicated if fits and paired and whole_tiles else sharded
    return plan(pair_rep, *others)


def solution(mesh):
    return jax.shard_map(
        local,
        mesh=mesh,
        in_specs=(
            P(("crop", "row"), "col", None),
            P(("crop", "row"), "col", None),
            P(),
            P(),
            P(),
            P(),
            P(),
            P(),
            P(),
        ),
        out_specs=(
            P(("crop", "row"), "col", None),
            P(("crop", "row"), "col", None),
            P("crop", None),
            P("crop", None),
            P("crop", None),
        ),
        check_vma=False,
    )
```

```python
import functools

import jax
import jax.numpy as jnp
from jax import lax
from jax.experimental import pallas as pl
from jax.experimental.pallas import tpu as pltpu
from jax.sharding import PartitionSpec as P

F32 = jnp.float32
BF16 = jnp.bfloat16
VMEM_BUDGET = 24 * 2**20
SWAP = ((0, 1), (1, 0))
NATIVE = ((1,), (0,))
BY_ROWS = ((0,), (0,))
TRANSPOSED = ((1,), (1,))


def layer_norm(values, gain, bias):
    centred = values - jnp.mean(values, axis=-1, keepdims=True)
    inverse = lax.rsqrt(jnp.mean(centred * centred, axis=-1, keepdims=True) + 1e-05)
    scaled = centred * inverse
    return (scaled * gain + bias, scaled, inverse)


def norm_back(grads, gain, scaled, inverse):
    weighted = grads * gain
    first = jnp.mean(weighted, axis=-1, keepdims=True)
    second = jnp.mean(weighted * scaled, axis=-1, keepdims=True)
    return inverse * (weighted - first - scaled * second)


def sigmoid(values):
    return 0.5 * jnp.tanh(0.5 * values) + 0.5


def dot(a, b, contract=NATIVE):
    return lax.dot_general(a, b, (contract, ((), ())), preferred_element_type=F32)


def at(index, size):
    return pl.ds(pl.multiple_of(index * size, size), size)


def tile(start):
    return pl.ds(pl.multiple_of(start, 8), 8)


def places(groups):
    me = lax.axis_index("row")
    return [lax.bitwise_xor(me // 2, t) for t in range(groups // 2)]


def row_block(which, b):
    me = lax.axis_index("row")
    parity = lax.rem(me, 2)
    return 2 * b + (parity if which == 0 else 1 - parity)


def edges(blocks, params, proj_weight):
    hidden = proj_weight.shape[1] // 4
    values = jnp.concatenate([block[...] for block in blocks], axis=0).astype(F32)
    normed = layer_norm(values, params[0:1, :], params[1:2, :])[0].astype(BF16)
    projected = dot(normed, proj_weight[...])
    sides = []
    for start in (0, 2 * hidden):
        gate = sigmoid(projected[:, start : start + hidden])
        edge = gate * projected[:, start + hidden : start + 2 * hidden]
        sides.append((edge.astype(BF16).astype(F32), gate, edge * (1.0 - gate)))
    return normed, sides


def fetch_kernel(sizes, *refs):
    half = (len(refs) + 3) // 2
    vectors, ins, params, outs = refs[:4], refs[4:half], refs[half], refs[half + 1 :]
    for n, vector in enumerate(vectors):
        params[n : n + 1, :] = vector[...]
    for given, out in zip(ins, outs, strict=True):
        out[...] = given[...]


def own_edges_kernel(sizes, params, weight, *refs):
    rows, cols, groups = sizes
    cells = rows * cols
    blocks, normed_out, outs = refs[:-7], refs[-7], refs[-6:]
    normed, sides = edges(blocks, params, weight)
    for t, b in enumerate(places(groups)):
        part = slice(t * cells, (t + 1) * cells)
        place = at(b, cells)
        normed_out[place, :] = normed[part]
        for out, value in zip(outs, sides[0] + sides[1], strict=True):
            out[place, :] = value[part]


def mate_edges_kernel(sizes, params, weight, *refs):
    rows, cols, groups = sizes
    cells = rows * cols
    blocks, left, right = refs[:-2], refs[-2], refs[-1]
    _, sides = edges(blocks, params, weight)
    for t, b in enumerate(places(groups)):
        part = slice(t * cells, (t + 1) * cells)
        left[at(b, cells), :] = sides[0][0][part]
        right[at(b, cells), :] = sides[1][0][part]


def triangle_kernel(sizes, *refs):
    rows, cols, groups = sizes
    cells = rows * cols
    lefts, rights, (tri,), picked = refs[:4], refs[4:8], refs[8:9], refs[9:]
    hidden = tri.shape[-1]
    half = lax.axis_index("col")
    zero = jnp.zeros((8, hidden), F32)
    count = cols // 8
    blocks = cols // rows
    for side in range(2):
        for which in range(2):
            for s in range(blocks // 2):
                b = half * (blocks // 2) + s
                p = row_block(which, b) - half * blocks
                picked[side][at(p, cells), :] = rights[2 * side + which][at(b, cells), :]

    for which in range(2):

        def tri_block(b, carry, which=which):
            def step(k, sums):
                new = list(sums)
                for side in range(2):
                    left = lefts[2 * side + which]
                    tiles = [
                        picked[side][pl.ds(t * 8 * cols + k, 8, stride=cols), :]
                        for t in range(count)
                    ]
                    for a in range(rows):
                        row = left[pl.ds((b * rows + a) * cols + k, 1), :]
                        for t in range(count):
                            new[a * count + t] += row * tiles[t]
                return tuple(new)

            sums = lax.fori_loop(0, cols, step, (zero,) * (rows * count), unroll=4)
            start = row_block(which, b) * cells
            for t, value in enumerate(sums):
                tri[tile(start + t * 8), :] = value
            return carry

        lax.fori_loop(0, groups // 2, tri_block, 0)


def cells_kernel(
    sizes,
    params,
    tri,
    normed_0,
    normed_1,
    gate_weight,
    out_weight,
    *refs,
):
    rows, cols, groups = sizes
    cells = rows * cols
    cots, (block_out, d_tri, d_gate, tri_norm_out, d_update_out) = refs[:-5], refs[-5:]
    gain, bias = params[2:3, :], params[3:4, :]
    for which, normed in ((0, normed_0), (1, normed_1)):
        for t, b in enumerate(places(groups)):
            cot = cots[which][t * cells : (t + 1) * cells, :]
            place = at(row_block(which, b), cells)
            tri_f, hat, inverse = layer_norm(tri[place, :], gain, bias)
            tri_norm = tri_f.astype(BF16)
            update = dot(tri_norm, out_weight[...])
            out_gate = sigmoid(dot(normed[at(b, cells), :], gate_weight[...]))
            if which == 0 and t == 0:
                block_out[...] = (out_gate * update).astype(BF16)
            gated = cot.astype(F32) * out_gate
            d_update = gated.astype(BF16)
            d_gate[place, :] = (gated * update * (1.0 - out_gate)).astype(BF16)
            d_norm = dot(d_update, out_weight[...], TRANSPOSED)
            d_tri[place, :] = norm_back(d_norm, gain, hat, inverse).astype(BF16)
            tri_norm_out[place, :] = tri_norm
            d_update_out[place, :] = d_update


def contract(rows, cols, count, unroll, start, source, row_at, operand, operand_at):
    tiles = cols // 8

    def step(term, sums):
        new = list(sums)
        loaded = [operand[tile(operand_at(term) + t * 8), :] for t in range(tiles)]
        for a in range(rows):
            row = source[pl.ds(row_at(a, term), 1), :]
            for t in range(tiles):
                new[a * tiles + t] += row * loaded[t]
        return tuple(new)

    return lax.fori_loop(0, count, step, start, unroll=unroll)


def early_kernel(
    sizes,
    d_tri_ref,
    d_gate,
    tri_norm,
    d_update,
    normed_0,
    normed_1,
    left_0,
    left_1,
    right_0,
    right_1,
    left,
    right,
    normed,
    d_left,
    d_right,
    small_grads,
    source,
):
    rows, cols, groups = sizes
    cells = rows * cols
    hidden = left.shape[-1]
    channels = normed.shape[-1]
    half = lax.axis_index("col")
    zeros = (jnp.zeros((8, hidden), F32),) * (rows * cols // 8)
    source[...] = d_tri_ref[...].astype(F32)
    for which, part_n, part_l, part_r in (
        (0, normed_0, left_0, right_0),
        (1, normed_1, left_1, right_1),
    ):
        for b in range(groups // 2):
            place, part = at(row_block(which, b), cells), slice(b * cells, (b + 1) * cells)
            normed[place, :] = part_n[part, :]
            left[place, :] = part_l[part, :]
            right[place, :] = part_r[part, :]

    def left_block(p, carry):
        sums = contract(
            rows,
            cols,
            cols,
            8,
            zeros,
            source,
            lambda a, j: (p * rows + a) * cols + j,
            right,
            lambda j: (half * cols + j) * cols,
        )
        for t, value in enumerate(sums):
            d_left[tile(p * cells + t * 8), :] = value
        return carry

    lax.fori_loop(0, groups, left_block, 0)

    def right_block(p, carry):
        sums = contract(
            rows,
            cols,
            rows * groups,
            8,
            zeros,
            source,
            lambda a, i: i * cols + p * rows + a,
            left,
            lambda i: i * cols,
        )
        for t, value in enumerate(sums):
            d_right[tile(p * cells + t * 8), :] = value
        return carry

    lax.fori_loop(0, cols // rows, right_block, 0)
    scale = 1.0 / (rows * groups)
    small_grads[:, :channels] = dot(normed[...], d_gate[...], BY_ROWS) * scale
    small_grads[:, channels:] = dot(tri_norm[...], d_update[...], BY_ROWS) * scale


def late_kernel(
    sizes,
    d_tri_ref,
    left,
    right,
    normed,
    d_left,
    d_right,
    left_gate_0,
    left_gate_1,
    left_value_0,
    left_value_1,
    right_gate_0,
    right_gate_1,
    right_value_0,
    right_value_1,
    proj_grad,
    d_proj,
    source,
    d_right_s,
):
    rows, cols, groups = sizes
    cells = rows * cols
    hidden = left.shape[-1]
    half = lax.axis_index("col")
    zeros = (jnp.zeros((8, hidden), F32),) * (rows * cols // 8)
    source[...] = d_tri_ref[...].astype(F32)
    d_right_s[at(half, cols * cols), :] = d_right[...]

    def right_block(p, carry):
        sums = contract(
            rows,
            cols,
            rows * groups,
            8,
            zeros,
            source,
            lambda a, i: i * cols + p * rows + a,
            left,
            lambda i: i * cols,
        )
        start = (1 - half) * cols * cols + p * cells
        for t, value in enumerate(sums):
            d_right_s[tile(start + t * 8), :] = value
        return carry

    lax.fori_loop(0, cols // rows, right_block, 0)

    for which, left_gate, left_value, right_gate, right_value in (
        (0, left_gate_0, left_value_0, right_gate_0, right_value_0),
        (1, left_gate_1, left_value_1, right_gate_1, right_value_1),
    ):

        def left_block(
            b,
            carry,
            which=which,
            left_gate=left_gate,
            left_value=left_value,
            right_gate=right_gate,
            right_value=right_value,
        ):
            p = row_block(which, b)
            start = p * cells
            sums = contract(
                rows,
                cols,
                cols,
                8,
                tuple(d_left[tile(start + t * 8), :] for t in range(cells // 8)),
                source,
                lambda a, j: (p * rows + a) * cols + j,
                right,
                lambda j: ((1 - half) * cols + j) * cols,
            )
            part, place = at(b, cells), at(p, cells)
            grads = jnp.concatenate(sums, axis=0)
            d_proj[place, :hidden] = (grads * left_value[part, :]).astype(BF16)
            d_proj[place, hidden : 2 * hidden] = (grads * left_gate[part, :]).astype(BF16)
            grads = d_right_s[place, :]
            d_proj[place, 2 * hidden : 3 * hidden] = (grads * right_value[part, :]).astype(BF16)
            d_proj[place, 3 * hidden :] = (grads * right_gate[part, :]).astype(BF16)
            return carry

        lax.fori_loop(0, groups // 2, left_block, 0)

    scale = 1.0 / (rows * groups)
    proj_grad[...] = dot(normed[...], d_proj[...], BY_ROWS) * scale


def outputs_kernel(
    sizes,
    params,
    pair,
    d_proj,
    d_gate,
    proj_weight,
    gate_weight,
    block_in,
    small_own,
    small_mate,
    block_out,
    pair_grad,
    gate_grad,
    out_grad,
):
    rows, cols, _ = sizes
    cells = rows * cols
    own = at(lax.axis_index("row"), cells)
    d_normed = dot(d_proj[own, :], proj_weight[...], TRANSPOSED) + dot(
        d_gate[own, :], gate_weight[...], TRANSPOSED
    )
    gain = params[0:1, :]
    _, hat, inverse = layer_norm(pair[...].astype(F32), gain, params[1:2, :])
    pair_grad[...] = norm_back(d_normed, gain, hat, inverse)
    block_out[...] = block_in[...]
    channels = gate_grad.shape[1]
    small = small_own[...] + small_mate[...]
    gate_grad[...] = small[:, :channels]
    out_grad[...] = small[:, channels:]


def replicated(
    pair_rep,
    cotangent,
    norm_gain,
    norm_bias,
    proj_weight,
    gate_weight,
    tri_gain,
    tri_bias,
    out_weight,
):
    rows, cols, channels = pair_rep.shape
    hidden = tri_gain.shape[0]
    groups = lax.axis_size("row")
    cells = rows * cols
    every = cells * groups
    some = every // 2
    sizes = (rows, cols, groups)

    def call(kernel, outs, *args, scratch=(), micros=1, name):
        cost = pl.CostEstimate(flops=micros * 10**9, bytes_accessed=0, transcendentals=0)
        return pl.pallas_call(
            functools.partial(kernel, sizes),
            out_shape=[jax.ShapeDtypeStruct(*out) for out in outs],
            scratch_shapes=[pltpu.VMEM(*one) for one in scratch],
            compiler_params=pltpu.CompilerParams(vmem_limit_bytes=VMEM_BUDGET),
            cost_estimate=cost,
            name=name,
        )(*args)

    def across(value, mask):
        return lax.ppermute(value, "row", [(i, i ^ mask) for i in range(groups)])

    def over(value):
        return lax.ppermute(value, "col", SWAP)

    def along(value, tied=False):
        got = []
        for s in reversed(range(1, groups // 2)):
            arrived = across(value, 2 * s)
            got.append(after(arrived, got[-1]) if got and tied else arrived)
        return got[::-1]

    def join(*values):
        return jnp.concatenate(values, axis=0)

    def after(value, *others):
        return lax.optimization_barrier((value, *others))[0]

    full, part = (every, hidden), (some, hidden)

    def own_edges(*blocks):
        outs = [((some, channels), BF16)] + [(part, F32)] * 6
        return call(own_edges_kernel, outs, params, proj_weight, *blocks, name="own_edges")

    def mate_edges(*blocks):
        outs = [(part, F32)] * 2
        return call(mate_edges_kernel, outs, params, proj_weight, *blocks, name="mate_edges")

    pair_in = pair_rep.reshape(cells, channels)
    near = along(pair_in, tied=True)
    vectors = [v[None] for v in (norm_gain, norm_bias, tri_gain, tri_bias)]
    arrays = (pair_in, cotangent.reshape(cells, channels), proj_weight, gate_weight, out_weight)
    params, pair, cot, proj_weight, gate_weight, out_weight = call(
        fetch_kernel,
        [((4, channels), F32)] + [(a.shape, a.dtype) for a in arrays],
        *vectors,
        *arrays,
        name="fetch",
    )
    pair_far = across(pair, 1)
    near_all = after(join(*near), params)
    far = across(near_all, 1)
    mate_near = over(join(pair, near_all))
    cot_near = join(cot, *along(cot))
    cot_far = across(cot_near, 1)
    own_0 = own_edges(pair, near_all)
    mate_0 = mate_edges(mate_near)
    far_all = join(pair_far, far)
    own_1 = own_edges(far_all)
    mate_1 = mate_edges(over(far_all))
    own, mate = (own_0, own_1), (mate_0, mate_1)
    normed = [o[0] for o in own]
    left, left_gate, left_value = ([o[n] for o in own] for n in (1, 2, 3))
    right, right_gate, right_value = ([o[n] for o in own] for n in (4, 5, 6))
    (tri,) = call(
        triangle_kernel,
        [(full, F32)],
        *left,
        *(m[0] for m in mate),
        *right,
        *(m[1] for m in mate),
        scratch=[((cols * cols, hidden), F32)] * 2,
        micros=2,
        name="triangle",
    )
    block_out, d_tri, d_gate, tri_norm, d_update = call(
        cells_kernel,
        [((cells, channels), BF16)] + [(full, BF16)] * 4,
        params,
        tri,
        *normed,
        gate_weight,
        out_weight,
        cot_near,
        cot_far,
        micros=2,
        name="cells",
    )
    d_tri_mate = over(d_tri)
    left_all, right_all, normed_all, d_left, d_right, small_grads = call(
        early_kernel,
        [
            (full, F32),
            (full, F32),
            ((every, channels), BF16),
            (full, F32),
            (part, F32),
            ((channels, 2 * channels), F32),
        ],
        d_tri,
        d_gate,
        tri_norm,
        d_update,
        *normed,
        *left,
        *right,
        scratch=[(full, F32)],
        micros=30,
        name="early",
    )
    small_mate = over(small_grads)
    proj_grad, d_proj = call(
        late_kernel,
        [((channels, 4 * hidden), F32), ((every, 4 * hidden), BF16)],
        d_tri_mate,
        left_all,
        right_all,
        normed_all,
        d_left,
        d_right,
        *left_gate,
        *left_value,
        *right_gate,
        *right_value,
        scratch=[(full, F32), (full, F32)],
        micros=40,
        name="late",
    )
    proj_mate = over(proj_grad)
    square = ((channels, channels), F32)
    block_out, pair_grad, gate_grad, out_grad = call(
        outputs_kernel,
        [((cells, channels), BF16), ((cells, channels), F32), square, square],
        params,
        pair,
        d_proj,
        d_gate,
        proj_weight,
        gate_weight,
        block_out,
        small_grads,
        small_mate,
        micros=10,
        name="outputs",
    )
    return (
        block_out.reshape(pair_rep.shape),
        pair_grad.reshape(pair_rep.shape),
        proj_grad + proj_mate,
        gate_grad,
        out_grad,
    )


def sharded(
    pair_rep,
    cotangent,
    norm_gain,
    norm_bias,
    proj_weight,
    gate_weight,
    tri_gain,
    tri_bias,
    out_weight,
):
    f32 = jnp.float32
    bf16 = jnp.bfloat16
    hidden = tri_gain.shape[0]
    channels = norm_gain.shape[0]
    row_count = pair_rep.shape[0]
    col_count = pair_rep.shape[1]
    crop_len = row_count * lax.axis_size("row")
    normed_f, pair_hat, pair_inv = layer_norm(pair_rep.astype(f32), norm_gain, norm_bias)
    normed = normed_f.astype(bf16)
    projected = jnp.einsum("ijc,cd->ijd", normed, proj_weight, preferred_element_type=f32)
    sig_left = jax.nn.sigmoid(projected[..., 0:hidden])
    val_left = projected[..., hidden : 2 * hidden]
    sig_right = jax.nn.sigmoid(projected[..., 2 * hidden : 3 * hidden])
    val_right = projected[..., 3 * hidden : 4 * hidden]
    left_edge = (sig_left * val_left).astype(bf16)
    right_edge = (sig_right * val_right).astype(bf16)
    out_gate = jax.nn.sigmoid(
        jnp.einsum("ijc,cd->ijd", normed, gate_weight, preferred_element_type=f32)
    )
    right_all = lax.all_gather(right_edge, "row", axis=0, tiled=True)
    block = right_all
    triangle = lax.psum_scatter(
        jnp.einsum("ikc,jkc->jic", left_edge, block, preferred_element_type=f32),
        "col",
        scatter_dimension=0,
        tiled=True,
    ).transpose(1, 0, 2)
    tri_f, tri_hat, tri_inv = layer_norm(triangle, tri_gain, tri_bias)
    tri_norm = tri_f.astype(bf16)
    update = jnp.einsum("ijh,hc->ijc", tri_norm, out_weight, preferred_element_type=f32)
    block_out = (out_gate * update).astype(bf16)
    cot = cotangent.astype(f32)
    d_update = (cot * out_gate).astype(bf16)
    d_gate = (cot * update * out_gate * (1.0 - out_gate)).astype(bf16)
    d_norm = jnp.einsum("ijc,hc->ijh", d_update, out_weight, preferred_element_type=f32)
    d_triangle = norm_back(d_norm, tri_gain, tri_hat, tri_inv).astype(bf16)
    tri_rows = lax.all_gather(d_triangle, "col", axis=1, tiled=True)
    d_left = jnp.einsum("ijc,jkc->ikc", tri_rows, right_all, preferred_element_type=f32)
    tri_cols = lax.all_to_all(tri_rows, "row", split_axis=1, concat_axis=0, tiled=True)
    block = tri_cols
    d_right = jnp.einsum(
        "ijc,ikc->jkc",
        block,
        lax.all_gather(left_edge, "row", axis=0, tiled=True),
        preferred_element_type=f32,
    )
    d_proj = jnp.concatenate(
        [
            d_left * val_left * sig_left * (1.0 - sig_left),
            d_left * sig_left,
            d_right * val_right * sig_right * (1.0 - sig_right),
            d_right * sig_right,
        ],
        axis=-1,
    ).astype(bf16)
    d_normed = jnp.einsum(
        "ijd,cd->ijc", d_proj, proj_weight, preferred_element_type=f32
    ) + jnp.einsum("ijd,cd->ijc", d_gate, gate_weight, preferred_element_type=f32)
    pair_grad = norm_back(d_normed, norm_gain, pair_hat, pair_inv)
    cells = row_count * col_count
    flat_norm = normed.reshape(cells, channels)
    local_proj = (
        jnp.dot(flat_norm.T, d_proj.reshape(cells, 4 * hidden), preferred_element_type=f32)
        / crop_len
    )
    local_gate = (
        jnp.dot(flat_norm.T, d_gate.reshape(cells, channels), preferred_element_type=f32) / crop_len
    )
    local_out = (
        jnp.dot(
            tri_norm.reshape(cells, hidden).T,
            d_update.reshape(cells, channels),
            preferred_element_type=f32,
        )
        / crop_len
    )
    proj_grad, gate_grad, out_grad = lax.psum((local_proj, local_gate, local_out), ("row", "col"))
    return (block_out, pair_grad, proj_grad, gate_grad, out_grad)


def local(pair_rep, *others):
    rows, cols, channels = pair_rep.shape
    hidden = others[7].shape[0]
    groups = lax.axis_size("row")
    every = rows * groups * cols
    fits = 24 * every * channels * 4 <= VMEM_BUDGET and hidden == channels
    paired = lax.axis_size("col") == 2 and groups & (groups - 1) == 0 and groups >= 2
    whole_tiles = cols % 8 == 0 and cols % (2 * rows) == 0 and rows * cols % 16 == 0
    plan = replicated if fits and paired and whole_tiles else sharded
    return plan(pair_rep, *others)


def solution(mesh):
    return jax.shard_map(
        local,
        mesh=mesh,
        in_specs=(
            P(("crop", "row"), "col", None),
            P(("crop", "row"), "col", None),
            P(),
            P(),
            P(),
            P(),
            P(),
            P(),
            P(),
        ),
        out_specs=(
            P(("crop", "row"), "col", None),
            P(("crop", "row"), "col", None),
            P("crop", None),
            P("crop", None),
            P("crop", None),
        ),
        check_vma=False,
    )
```

```python
import functools

import jax
import jax.numpy as jnp
from jax import lax
from jax.experimental import pallas as pl
from jax.experimental.pallas import tpu as pltpu
from jax.sharding import PartitionSpec as P

F32 = jnp.float32
BF16 = jnp.bfloat16
VMEM_BUDGET = 24 * 2**20
SWAP = ((0, 1), (1, 0))
NATIVE = ((1,), (0,))
BY_ROWS = ((0,), (0,))
TRANSPOSED = ((1,), (1,))


def layer_norm(values, gain, bias):
    centred = values - jnp.mean(values, axis=-1, keepdims=True)
    inverse = lax.rsqrt(jnp.mean(centred * centred, axis=-1, keepdims=True) + 1e-05)
    scaled = centred * inverse
    return (scaled * gain + bias, scaled, inverse)


def norm_back(grads, gain, scaled, inverse):
    weighted = grads * gain
    first = jnp.mean(weighted, axis=-1, keepdims=True)
    second = jnp.mean(weighted * scaled, axis=-1, keepdims=True)
    return inverse * (weighted - first - scaled * second)


def sigmoid(values):
    return 0.5 * jnp.tanh(0.5 * values) + 0.5


def dot(a, b, contract=NATIVE):
    return lax.dot_general(a, b, (contract, ((), ())), preferred_element_type=F32)


def at(index, size):
    return pl.ds(pl.multiple_of(index * size, size), size)


def tile(start):
    return pl.ds(pl.multiple_of(start, 8), 8)


def places(groups):
    me = lax.axis_index("row")
    return [lax.bitwise_xor(me // 2, t) for t in range(groups // 2)]


def row_block(which, b):
    me = lax.axis_index("row")
    parity = lax.rem(me, 2)
    return 2 * b + (parity if which == 0 else 1 - parity)


def edges(blocks, params, proj_weight):
    hidden = proj_weight.shape[1] // 4
    values = jnp.concatenate([block[...] for block in blocks], axis=0).astype(F32)
    normed = layer_norm(values, params[0:1, :], params[1:2, :])[0].astype(BF16)
    projected = dot(normed, proj_weight[...])
    sides = []
    for start in (0, 2 * hidden):
        gate = sigmoid(projected[:, start : start + hidden])
        edge = gate * projected[:, start + hidden : start + 2 * hidden]
        sides.append((edge.astype(BF16).astype(F32), gate, edge * (1.0 - gate)))
    return normed, sides


def fetch_kernel(sizes, *refs):
    cells = sizes[0] * sizes[1]
    pair, cot, gain_0, bias_0, gain_1, bias_1, *weights = refs[:9]
    both, params, *held = refs[9:14]
    sems = refs[14]
    moves = [(pair, both.at[:cells]), (cot, both.at[cells:])]
    moves += [(v, params.at[n : n + 1]) for n, v in enumerate((gain_0, bias_0, gain_1, bias_1))]
    moves += list(zip(weights, held, strict=True))
    copies = [pltpu.make_async_copy(a, b, sems.at[n]) for n, (a, b) in enumerate(moves)]
    for copy in copies:
        copy.start()
    for copy in copies:
        copy.wait()


def own_edges_kernel(sizes, params, weight, *refs):
    rows, cols, groups = sizes
    cells = rows * cols
    blocks, normed_out, outs = refs[:-7], refs[-7], refs[-6:]
    normed, sides = edges(blocks, params, weight)
    for t, b in enumerate(places(groups)):
        part = slice(t * cells, (t + 1) * cells)
        place = at(b, cells)
        normed_out[place, :] = normed[part]
        for out, value in zip(outs, sides[0] + sides[1], strict=True):
            out[place, :] = value[part]


def mate_edges_kernel(sizes, params, weight, *refs):
    rows, cols, groups = sizes
    cells = rows * cols
    blocks, left, right = refs[:-2], refs[-2], refs[-1]
    _, sides = edges(blocks, params, weight)
    for t, b in enumerate(places(groups)):
        part = slice(t * cells, (t + 1) * cells)
        left[at(b, cells), :] = sides[0][0][part]
        right[at(b, cells), :] = sides[1][0][part]


def triangle_kernel(sizes, *refs):
    rows, cols, groups = sizes
    cells = rows * cols
    lefts, rights, (tri,), picked = refs[:4], refs[4:8], refs[8:9], refs[9:]
    hidden = tri.shape[-1]
    half = lax.axis_index("col")
    zero = jnp.zeros((8, hidden), F32)
    count = cols // 8
    blocks = cols // rows
    for side in range(2):
        for which in range(2):
            for s in range(blocks // 2):
                b = half * (blocks // 2) + s
                p = row_block(which, b) - half * blocks
                picked[side][at(p, cells), :] = rights[2 * side + which][at(b, cells), :]

    for which in range(2):

        def tri_block(b, carry, which=which):
            def step(k, sums):
                new = list(sums)
                for side in range(2):
                    left = lefts[2 * side + which]
                    tiles = [
                        picked[side][pl.ds(t * 8 * cols + k, 8, stride=cols), :]
                        for t in range(count)
                    ]
                    for a in range(rows):
                        row = left[pl.ds((b * rows + a) * cols + k, 1), :]
                        for t in range(count):
                            new[a * count + t] += row * tiles[t]
                return tuple(new)

            sums = lax.fori_loop(0, cols, step, (zero,) * (rows * count), unroll=4)
            start = row_block(which, b) * cells
            for t, value in enumerate(sums):
                tri[tile(start + t * 8), :] = value
            return carry

        lax.fori_loop(0, groups // 2, tri_block, 0)


def cells_kernel(
    sizes,
    params,
    tri,
    normed_0,
    normed_1,
    gate_weight,
    out_weight,
    *refs,
):
    rows, cols, groups = sizes
    cells = rows * cols
    cots, (block_out, d_tri, d_gate, tri_norm_out, d_update_out) = refs[:-5], refs[-5:]
    gain, bias = params[2:3, :], params[3:4, :]
    for which, normed in ((0, normed_0), (1, normed_1)):
        for t, b in enumerate(places(groups)):
            block = cots[2 * which + min(t, 1)]
            cot = block[max(t - 1, 0) * cells : max(t, 1) * cells, :]
            place = at(row_block(which, b), cells)
            tri_f, hat, inverse = layer_norm(tri[place, :], gain, bias)
            tri_norm = tri_f.astype(BF16)
            update = dot(tri_norm, out_weight[...])
            out_gate = sigmoid(dot(normed[at(b, cells), :], gate_weight[...]))
            if which == 0 and t == 0:
                block_out[...] = (out_gate * update).astype(BF16)
            gated = cot.astype(F32) * out_gate
            d_update = gated.astype(BF16)
            d_gate[place, :] = (gated * update * (1.0 - out_gate)).astype(BF16)
            d_norm = dot(d_update, out_weight[...], TRANSPOSED)
            d_tri[place, :] = norm_back(d_norm, gain, hat, inverse).astype(BF16)
            tri_norm_out[place, :] = tri_norm
            d_update_out[place, :] = d_update


def contract(rows, cols, count, unroll, start, source, row_at, operand, operand_at):
    tiles = cols // 8

    def step(term, sums):
        new = list(sums)
        loaded = [operand[tile(operand_at(term) + t * 8), :] for t in range(tiles)]
        for a in range(rows):
            row = source[pl.ds(row_at(a, term), 1), :]
            for t in range(tiles):
                new[a * tiles + t] += row * loaded[t]
        return tuple(new)

    return lax.fori_loop(0, count, step, start, unroll=unroll)


def early_kernel(
    sizes,
    d_tri_ref,
    d_gate,
    tri_norm,
    d_update,
    normed_0,
    normed_1,
    left_0,
    left_1,
    right_0,
    right_1,
    left,
    right,
    normed,
    d_left,
    d_right,
    small_grads,
    source,
):
    rows, cols, groups = sizes
    cells = rows * cols
    hidden = left.shape[-1]
    channels = normed.shape[-1]
    half = lax.axis_index("col")
    zeros = (jnp.zeros((8, hidden), F32),) * (rows * cols // 8)
    source[...] = d_tri_ref[...].astype(F32)
    for which, part_n, part_l, part_r in (
        (0, normed_0, left_0, right_0),
        (1, normed_1, left_1, right_1),
    ):
        for b in range(groups // 2):
            place, part = at(row_block(which, b), cells), slice(b * cells, (b + 1) * cells)
            normed[place, :] = part_n[part, :]
            left[place, :] = part_l[part, :]
            right[place, :] = part_r[part, :]

    def left_block(p, carry):
        sums = contract(
            rows,
            cols,
            cols,
            8,
            zeros,
            source,
            lambda a, j: (p * rows + a) * cols + j,
            right,
            lambda j: (half * cols + j) * cols,
        )
        for t, value in enumerate(sums):
            d_left[tile(p * cells + t * 8), :] = value
        return carry

    lax.fori_loop(0, groups, left_block, 0)

    def right_block(p, carry):
        sums = contract(
            rows,
            cols,
            rows * groups,
            8,
            zeros,
            source,
            lambda a, i: i * cols + p * rows + a,
            left,
            lambda i: i * cols,
        )
        for t, value in enumerate(sums):
            d_right[tile(p * cells + t * 8), :] = value
        return carry

    lax.fori_loop(0, cols // rows, right_block, 0)
    scale = 1.0 / (rows * groups)
    small_grads[:, :channels] = dot(normed[...], d_gate[...], BY_ROWS) * scale
    small_grads[:, channels:] = dot(tri_norm[...], d_update[...], BY_ROWS) * scale


def late_kernel(
    sizes,
    d_tri_ref,
    left,
    right,
    normed,
    d_left,
    d_right,
    left_gate_0,
    left_gate_1,
    left_value_0,
    left_value_1,
    right_gate_0,
    right_gate_1,
    right_value_0,
    right_value_1,
    proj_grad,
    d_proj,
    source,
    d_right_s,
):
    rows, cols, groups = sizes
    cells = rows * cols
    hidden = left.shape[-1]
    half = lax.axis_index("col")
    zeros = (jnp.zeros((8, hidden), F32),) * (rows * cols // 8)
    source[...] = d_tri_ref[...].astype(F32)
    d_right_s[at(half, cols * cols), :] = d_right[...]

    def right_block(p, carry):
        sums = contract(
            rows,
            cols,
            rows * groups,
            8,
            zeros,
            source,
            lambda a, i: i * cols + p * rows + a,
            left,
            lambda i: i * cols,
        )
        start = (1 - half) * cols * cols + p * cells
        for t, value in enumerate(sums):
            d_right_s[tile(start + t * 8), :] = value
        return carry

    lax.fori_loop(0, cols // rows, right_block, 0)

    for which, left_gate, left_value, right_gate, right_value in (
        (0, left_gate_0, left_value_0, right_gate_0, right_value_0),
        (1, left_gate_1, left_value_1, right_gate_1, right_value_1),
    ):

        def left_block(
            b,
            carry,
            which=which,
            left_gate=left_gate,
            left_value=left_value,
            right_gate=right_gate,
            right_value=right_value,
        ):
            p = row_block(which, b)
            start = p * cells
            sums = contract(
                rows,
                cols,
                cols,
                8,
                tuple(d_left[tile(start + t * 8), :] for t in range(cells // 8)),
                source,
                lambda a, j: (p * rows + a) * cols + j,
                right,
                lambda j: ((1 - half) * cols + j) * cols,
            )
            part, place = at(b, cells), at(p, cells)
            grads = jnp.concatenate(sums, axis=0)
            d_proj[place, :hidden] = (grads * left_value[part, :]).astype(BF16)
            d_proj[place, hidden : 2 * hidden] = (grads * left_gate[part, :]).astype(BF16)
            grads = d_right_s[place, :]
            d_proj[place, 2 * hidden : 3 * hidden] = (grads * right_value[part, :]).astype(BF16)
            d_proj[place, 3 * hidden :] = (grads * right_gate[part, :]).astype(BF16)
            return carry

        lax.fori_loop(0, groups // 2, left_block, 0)

    scale = 1.0 / (rows * groups)
    proj_grad[...] = dot(normed[...], d_proj[...], BY_ROWS) * scale


def outputs_kernel(
    sizes,
    params,
    pair,
    d_proj,
    d_gate,
    proj_weight,
    gate_weight,
    block_in,
    small_own,
    small_mate,
    block_out,
    pair_grad,
    gate_grad,
    out_grad,
):
    rows, cols, _ = sizes
    cells = rows * cols
    own = at(lax.axis_index("row"), cells)
    d_normed = dot(d_proj[own, :], proj_weight[...], TRANSPOSED) + dot(
        d_gate[own, :], gate_weight[...], TRANSPOSED
    )
    gain = params[0:1, :]
    _, hat, inverse = layer_norm(pair[...].astype(F32), gain, params[1:2, :])
    pair_grad[...] = norm_back(d_normed, gain, hat, inverse)
    block_out[...] = block_in[...]
    channels = gate_grad.shape[1]
    small = small_own[...] + small_mate[...]
    gate_grad[...] = small[:, :channels]
    out_grad[...] = small[:, channels:]


def replicated(
    pair_rep,
    cotangent,
    norm_gain,
    norm_bias,
    proj_weight,
    gate_weight,
    tri_gain,
    tri_bias,
    out_weight,
):
    rows, cols, channels = pair_rep.shape
    hidden = tri_gain.shape[0]
    groups = lax.axis_size("row")
    cells = rows * cols
    every = cells * groups
    some = every // 2
    sizes = (rows, cols, groups)

    def call(kernel, outs, *args, scratch=(), micros=1, name, **more):
        cost = pl.CostEstimate(flops=micros * 10**9, bytes_accessed=0, transcendentals=0)
        return pl.pallas_call(
            functools.partial(kernel, sizes),
            out_shape=[jax.ShapeDtypeStruct(*out) for out in outs],
            scratch_shapes=[pltpu.VMEM(*one) if isinstance(one, tuple) else one for one in scratch],
            **more,
            compiler_params=pltpu.CompilerParams(vmem_limit_bytes=VMEM_BUDGET),
            cost_estimate=cost,
            name=name,
        )(*args)

    def across(value, mask):
        return lax.ppermute(value, "row", [(i, i ^ mask) for i in range(groups)])

    def over(value):
        return lax.ppermute(value, "col", SWAP)

    def along(value, tied=False):
        got = []
        for s in reversed(range(1, groups // 2)):
            arrived = across(value, 2 * s)
            got.append(after(arrived, got[-1]) if got and tied else arrived)
        return got[::-1]

    def join(*values):
        return jnp.concatenate(values, axis=0)

    def after(value, *others):
        return lax.optimization_barrier((value, *others))[0]

    full, part = (every, hidden), (some, hidden)

    def own_edges(*blocks):
        outs = [((some, channels), BF16)] + [(part, F32)] * 6
        return call(own_edges_kernel, outs, params, proj_weight, *blocks, name="own_edges")

    def mate_edges(*blocks):
        outs = [(part, F32)] * 2
        return call(mate_edges_kernel, outs, params, proj_weight, *blocks, name="mate_edges")

    given = [pair_rep.reshape(cells, channels), cotangent.reshape(cells, channels)]
    given += [v[None] for v in (norm_gain, norm_bias, tri_gain, tri_bias)]
    given += [proj_weight, gate_weight, out_weight]
    given = [pltpu.with_memory_space_constraint(v, pltpu.HBM) for v in given]
    both, params, proj_weight, gate_weight, out_weight = call(
        fetch_kernel,
        [((2 * cells, channels), BF16), ((4, channels), F32)] + [(a.shape, BF16) for a in given[6:]],
        *given,
        scratch=[pltpu.SemaphoreType.DMA((len(given),))],
        in_specs=[pl.BlockSpec(memory_space=pltpu.HBM)] * len(given),
        name="fetch",
    )
    got = along(both, tied=True)
    both_far = across(both, 1)
    pair, pair_far = both[:cells], both_far[:cells]
    cot_0, cot_1 = both[cells:], both_far[cells:]
    near_all = join(*(block[:cells] for block in got))
    far = across(near_all, 1)
    cot_near = join(*(block[cells:] for block in got))
    cot_far = across(cot_near, 1)
    mate_near = over(join(pair, near_all))
    own_0 = own_edges(pair, near_all)
    mate_0 = mate_edges(mate_near)
    far_all = join(pair_far, far)
    own_1 = own_edges(far_all)
    mate_1 = mate_edges(over(far_all))
    own, mate = (own_0, own_1), (mate_0, mate_1)
    normed = [o[0] for o in own]
    left, left_gate, left_value = ([o[n] for o in own] for n in (1, 2, 3))
    right, right_gate, right_value = ([o[n] for o in own] for n in (4, 5, 6))
    (tri,) = call(
        triangle_kernel,
        [(full, F32)],
        *left,
        *(m[0] for m in mate),
        *right,
        *(m[1] for m in mate),
        scratch=[((cols * cols, hidden), F32)] * 2,
        micros=2,
        name="triangle",
    )
    block_out, d_tri, d_gate, tri_norm, d_update = call(
        cells_kernel,
        [((cells, channels), BF16)] + [(full, BF16)] * 4,
        params,
        tri,
        *normed,
        gate_weight,
        out_weight,
        cot_0,
        cot_near,
        cot_1,
        cot_far,
        micros=2,
        name="cells",
    )
    d_tri_mate = over(d_tri)
    left_all, right_all, normed_all, d_left, d_right, small_grads = call(
        early_kernel,
        [
            (full, F32),
            (full, F32),
            ((every, channels), BF16),
            (full, F32),
            (part, F32),
            ((channels, 2 * channels), F32),
        ],
        d_tri,
        d_gate,
        tri_norm,
        d_update,
        *normed,
        *left,
        *right,
        scratch=[(full, F32)],
        micros=30,
        name="early",
    )
    small_mate = over(small_grads)
    proj_grad, d_proj = call(
        late_kernel,
        [((channels, 4 * hidden), F32), ((every, 4 * hidden), BF16)],
        d_tri_mate,
        left_all,
        right_all,
        normed_all,
        d_left,
        d_right,
        *left_gate,
        *left_value,
        *right_gate,
        *right_value,
        scratch=[(full, F32), (full, F32)],
        micros=40,
        name="late",
    )
    proj_mate = over(proj_grad)
    square = ((channels, channels), F32)
    block_out, pair_grad, gate_grad, out_grad = call(
        outputs_kernel,
        [((cells, channels), BF16), ((cells, channels), F32), square, square],
        params,
        pair,
        d_proj,
        d_gate,
        proj_weight,
        gate_weight,
        block_out,
        small_grads,
        small_mate,
        micros=10,
        name="outputs",
    )
    return (
        block_out.reshape(pair_rep.shape),
        pair_grad.reshape(pair_rep.shape),
        proj_grad + proj_mate,
        gate_grad,
        out_grad,
    )


def sharded(
    pair_rep,
    cotangent,
    norm_gain,
    norm_bias,
    proj_weight,
    gate_weight,
    tri_gain,
    tri_bias,
    out_weight,
):
    f32 = jnp.float32
    bf16 = jnp.bfloat16
    hidden = tri_gain.shape[0]
    channels = norm_gain.shape[0]
    row_count = pair_rep.shape[0]
    col_count = pair_rep.shape[1]
    crop_len = row_count * lax.axis_size("row")
    normed_f, pair_hat, pair_inv = layer_norm(pair_rep.astype(f32), norm_gain, norm_bias)
    normed = normed_f.astype(bf16)
    projected = jnp.einsum("ijc,cd->ijd", normed, proj_weight, preferred_element_type=f32)
    sig_left = jax.nn.sigmoid(projected[..., 0:hidden])
    val_left = projected[..., hidden : 2 * hidden]
    sig_right = jax.nn.sigmoid(projected[..., 2 * hidden : 3 * hidden])
    val_right = projected[..., 3 * hidden : 4 * hidden]
    left_edge = (sig_left * val_left).astype(bf16)
    right_edge = (sig_right * val_right).astype(bf16)
    out_gate = jax.nn.sigmoid(
        jnp.einsum("ijc,cd->ijd", normed, gate_weight, preferred_element_type=f32)
    )
    right_all = lax.all_gather(right_edge, "row", axis=0, tiled=True)
    block = right_all
    triangle = lax.psum_scatter(
        jnp.einsum("ikc,jkc->jic", left_edge, block, preferred_element_type=f32),
        "col",
        scatter_dimension=0,
        tiled=True,
    ).transpose(1, 0, 2)
    tri_f, tri_hat, tri_inv = layer_norm(triangle, tri_gain, tri_bias)
    tri_norm = tri_f.astype(bf16)
    update = jnp.einsum("ijh,hc->ijc", tri_norm, out_weight, preferred_element_type=f32)
    block_out = (out_gate * update).astype(bf16)
    cot = cotangent.astype(f32)
    d_update = (cot * out_gate).astype(bf16)
    d_gate = (cot * update * out_gate * (1.0 - out_gate)).astype(bf16)
    d_norm = jnp.einsum("ijc,hc->ijh", d_update, out_weight, preferred_element_type=f32)
    d_triangle = norm_back(d_norm, tri_gain, tri_hat, tri_inv).astype(bf16)
    tri_rows = lax.all_gather(d_triangle, "col", axis=1, tiled=True)
    d_left = jnp.einsum("ijc,jkc->ikc", tri_rows, right_all, preferred_element_type=f32)
    tri_cols = lax.all_to_all(tri_rows, "row", split_axis=1, concat_axis=0, tiled=True)
    block = tri_cols
    d_right = jnp.einsum(
        "ijc,ikc->jkc",
        block,
        lax.all_gather(left_edge, "row", axis=0, tiled=True),
        preferred_element_type=f32,
    )
    d_proj = jnp.concatenate(
        [
            d_left * val_left * sig_left * (1.0 - sig_left),
            d_left * sig_left,
            d_right * val_right * sig_right * (1.0 - sig_right),
            d_right * sig_right,
        ],
        axis=-1,
    ).astype(bf16)
    d_normed = jnp.einsum(
        "ijd,cd->ijc", d_proj, proj_weight, preferred_element_type=f32
    ) + jnp.einsum("ijd,cd->ijc", d_gate, gate_weight, preferred_element_type=f32)
    pair_grad = norm_back(d_normed, norm_gain, pair_hat, pair_inv)
    cells = row_count * col_count
    flat_norm = normed.reshape(cells, channels)
    local_proj = (
        jnp.dot(flat_norm.T, d_proj.reshape(cells, 4 * hidden), preferred_element_type=f32)
        / crop_len
    )
    local_gate = (
        jnp.dot(flat_norm.T, d_gate.reshape(cells, channels), preferred_element_type=f32) / crop_len
    )
    local_out = (
        jnp.dot(
            tri_norm.reshape(cells, hidden).T,
            d_update.reshape(cells, channels),
            preferred_element_type=f32,
        )
        / crop_len
    )
    proj_grad, gate_grad, out_grad = lax.psum((local_proj, local_gate, local_out), ("row", "col"))
    return (block_out, pair_grad, proj_grad, gate_grad, out_grad)


def local(pair_rep, *others):
    rows, cols, channels = pair_rep.shape
    hidden = others[7].shape[0]
    groups = lax.axis_size("row")
    every = rows * groups * cols
    fits = 24 * every * channels * 4 <= VMEM_BUDGET and hidden == channels
    paired = lax.axis_size("col") == 2 and groups & (groups - 1) == 0 and groups >= 2
    whole_tiles = cols % 8 == 0 and cols % (2 * rows) == 0 and rows * cols % 16 == 0
    plan = replicated if fits and paired and whole_tiles else sharded
    return plan(pair_rep, *others)


def solution(mesh):
    return jax.shard_map(
        local,
        mesh=mesh,
        in_specs=(
            P(("crop", "row"), "col", None),
            P(("crop", "row"), "col", None),
            P(),
            P(),
            P(),
            P(),
            P(),
            P(),
            P(),
        ),
        out_specs=(
            P(("crop", "row"), "col", None),
            P(("crop", "row"), "col", None),
            P("crop", None),
            P("crop", None),
            P("crop", None),
        ),
        check_vma=False,
    )
```

```python
import functools

import jax
import jax.numpy as jnp
from jax import lax
from jax.experimental import pallas as pl
from jax.experimental.pallas import tpu as pltpu
from jax.sharding import PartitionSpec as P

F32 = jnp.float32
BF16 = jnp.bfloat16
VMEM_BUDGET = 24 * 2**20
SWAP = ((0, 1), (1, 0))
NATIVE = ((1,), (0,))
BY_ROWS = ((0,), (0,))
TRANSPOSED = ((1,), (1,))


def layer_norm(values, gain, bias):
    centred = values - jnp.mean(values, axis=-1, keepdims=True)
    inverse = lax.rsqrt(jnp.mean(centred * centred, axis=-1, keepdims=True) + 1e-05)
    scaled = centred * inverse
    return (scaled * gain + bias, scaled, inverse)


def norm_back(grads, gain, scaled, inverse):
    weighted = grads * gain
    first = jnp.mean(weighted, axis=-1, keepdims=True)
    second = jnp.mean(weighted * scaled, axis=-1, keepdims=True)
    return inverse * (weighted - first - scaled * second)


def sigmoid(values):
    return 0.5 * jnp.tanh(0.5 * values) + 0.5


def dot(a, b, contract=NATIVE):
    return lax.dot_general(a, b, (contract, ((), ())), preferred_element_type=F32)


def at(index, size):
    return pl.ds(pl.multiple_of(index * size, size), size)


def tile(start):
    return pl.ds(pl.multiple_of(start, 8), 8)


def places(groups):
    me = lax.axis_index("row")
    return [lax.bitwise_xor(me // 2, t) for t in range(groups // 2)]


def row_block(which, b):
    me = lax.axis_index("row")
    parity = lax.rem(me, 2)
    return 2 * b + (parity if which == 0 else 1 - parity)


def edges(blocks, params, proj_weight):
    hidden = proj_weight.shape[1] // 4
    values = jnp.concatenate([block[...] for block in blocks], axis=0).astype(F32)
    normed = layer_norm(values, params[0:1, :], params[1:2, :])[0].astype(BF16)
    projected = dot(normed, proj_weight[...])
    sides = []
    for start in (0, 2 * hidden):
        gate = sigmoid(projected[:, start : start + hidden])
        edge = gate * projected[:, start + hidden : start + 2 * hidden]
        sides.append((edge.astype(BF16).astype(F32), gate, edge * (1.0 - gate)))
    return normed, sides


def fetch_kernel(sizes, *refs):
    cells = sizes[0] * sizes[1]
    pair, cot, gain_0, bias_0, gain_1, bias_1, *weights = refs[:9]
    both, params, *held = refs[9:14]
    sems = refs[14]
    moves = [(pair, both.at[:cells]), (cot, both.at[cells:])]
    moves += [(v, params.at[n : n + 1]) for n, v in enumerate((gain_0, bias_0, gain_1, bias_1))]
    moves += list(zip(weights, held, strict=True))
    copies = [pltpu.make_async_copy(a, b, sems.at[n]) for n, (a, b) in enumerate(moves)]
    for copy in copies:
        copy.start()
    for copy in copies:
        copy.wait()


def own_edges_kernel(sizes, params, weight, *refs):
    rows, cols, groups = sizes
    cells = rows * cols
    blocks, normed_out, outs = refs[:-7], refs[-7], refs[-6:]
    normed, sides = edges(blocks, params, weight)
    for t, b in enumerate(places(groups)):
        part = slice(t * cells, (t + 1) * cells)
        place = at(b, cells)
        normed_out[place, :] = normed[part]
        for out, value in zip(outs, sides[0] + sides[1], strict=True):
            out[place, :] = value[part]


def mate_edges_kernel(sizes, params, weight, *refs):
    rows, cols, groups = sizes
    cells = rows * cols
    blocks, left, right = refs[:-2], refs[-2], refs[-1]
    _, sides = edges(blocks, params, weight)
    for t, b in enumerate(places(groups)):
        part = slice(t * cells, (t + 1) * cells)
        left[at(b, cells), :] = sides[0][0][part]
        right[at(b, cells), :] = sides[1][0][part]


def triangle_kernel(sizes, *refs):
    rows, cols, groups = sizes
    cells = rows * cols
    lefts, rights, (tri,), picked = refs[:4], refs[4:8], refs[8:9], refs[9:]
    hidden = tri.shape[-1]
    half = lax.axis_index("col")
    zero = jnp.zeros((8, hidden), F32)
    count = cols // 8
    blocks = cols // rows
    for side in range(2):
        for which in range(2):
            for s in range(blocks // 2):
                b = half * (blocks // 2) + s
                p = row_block(which, b) - half * blocks
                picked[side][at(p, cells), :] = rights[2 * side + which][at(b, cells), :]

    for which in range(2):

        def tri_block(b, carry, which=which):
            def step(k, sums):
                new = list(sums)
                for side in range(2):
                    left = lefts[2 * side + which]
                    tiles = [
                        picked[side][pl.ds(t * 8 * cols + k, 8, stride=cols), :]
                        for t in range(count)
                    ]
                    for a in range(rows):
                        row = left[pl.ds((b * rows + a) * cols + k, 1), :]
                        for t in range(count):
                            new[a * count + t] += row * tiles[t]
                return tuple(new)

            sums = lax.fori_loop(0, cols, step, (zero,) * (rows * count), unroll=4)
            start = row_block(which, b) * cells
            for t, value in enumerate(sums):
                tri[tile(start + t * 8), :] = value
            return carry

        lax.fori_loop(0, groups // 2, tri_block, 0)


def cells_kernel(
    sizes,
    params,
    tri,
    normed_0,
    normed_1,
    gate_weight,
    out_weight,
    *refs,
):
    rows, cols, groups = sizes
    cells = rows * cols
    cots, (block_out, d_tri, d_gate, tri_norm_out, d_update_out) = refs[:-5], refs[-5:]
    gain, bias = params[2:3, :], params[3:4, :]
    for which, normed in ((0, normed_0), (1, normed_1)):
        for t, b in enumerate(places(groups)):
            block = cots[2 * which + min(t, 1)]
            cot = block[max(t - 1, 0) * cells : max(t, 1) * cells, :]
            place = at(row_block(which, b), cells)
            tri_f, hat, inverse = layer_norm(tri[place, :], gain, bias)
            tri_norm = tri_f.astype(BF16)
            update = dot(tri_norm, out_weight[...])
            out_gate = sigmoid(dot(normed[at(b, cells), :], gate_weight[...]))
            if which == 0 and t == 0:
                block_out[...] = (out_gate * update).astype(BF16)
            gated = cot.astype(F32) * out_gate
            d_update = gated.astype(BF16)
            d_gate[place, :] = (gated * update * (1.0 - out_gate)).astype(BF16)
            d_norm = dot(d_update, out_weight[...], TRANSPOSED)
            d_tri[place, :] = norm_back(d_norm, gain, hat, inverse).astype(BF16)
            tri_norm_out[place, :] = tri_norm
            d_update_out[place, :] = d_update


def contract(rows, cols, count, unroll, start, source, row_at, operand, operand_at):
    tiles = cols // 8

    def step(term, sums):
        new = list(sums)
        loaded = [operand[tile(operand_at(term) + t * 8), :] for t in range(tiles)]
        for a in range(rows):
            row = source[pl.ds(row_at(a, term), 1), :]
            for t in range(tiles):
                new[a * tiles + t] += row * loaded[t]
        return tuple(new)

    return lax.fori_loop(0, count, step, start, unroll=unroll)


def early_kernel(
    sizes,
    d_tri_ref,
    d_gate,
    tri_norm,
    d_update,
    normed_0,
    normed_1,
    left_0,
    left_1,
    right_0,
    right_1,
    left,
    right,
    normed,
    d_left,
    d_right,
    small_grads,
    source,
):
    rows, cols, groups = sizes
    cells = rows * cols
    hidden = left.shape[-1]
    channels = normed.shape[-1]
    half = lax.axis_index("col")
    zeros = (jnp.zeros((8, hidden), F32),) * (rows * cols // 8)
    source[...] = d_tri_ref[...].astype(F32)
    for which, part_n, part_l, part_r in (
        (0, normed_0, left_0, right_0),
        (1, normed_1, left_1, right_1),
    ):
        for b in range(groups // 2):
            place, part = at(row_block(which, b), cells), slice(b * cells, (b + 1) * cells)
            normed[place, :] = part_n[part, :]
            left[place, :] = part_l[part, :]
            right[place, :] = part_r[part, :]

    def left_block(p, carry):
        sums = contract(
            rows,
            cols,
            cols,
            8,
            zeros,
            source,
            lambda a, j: (p * rows + a) * cols + j,
            right,
            lambda j: (half * cols + j) * cols,
        )
        for t, value in enumerate(sums):
            d_left[tile(p * cells + t * 8), :] = value
        return carry

    lax.fori_loop(0, groups, left_block, 0)

    def right_block(p, carry):
        sums = contract(
            rows,
            cols,
            rows * groups,
            8,
            zeros,
            source,
            lambda a, i: i * cols + p * rows + a,
            left,
            lambda i: i * cols,
        )
        for t, value in enumerate(sums):
            d_right[tile(p * cells + t * 8), :] = value
        return carry

    lax.fori_loop(0, cols // rows, right_block, 0)
    scale = 1.0 / (rows * groups)
    small_grads[:, :channels] = dot(normed[...], d_gate[...], BY_ROWS) * scale
    small_grads[:, channels:] = dot(tri_norm[...], d_update[...], BY_ROWS) * scale


def late_kernel(
    sizes,
    d_tri_ref,
    left,
    right,
    normed,
    d_left,
    d_right,
    left_gate_0,
    left_gate_1,
    left_value_0,
    left_value_1,
    right_gate_0,
    right_gate_1,
    right_value_0,
    right_value_1,
    proj_grad,
    d_proj,
    source,
    d_right_s,
):
    rows, cols, groups = sizes
    cells = rows * cols
    hidden = left.shape[-1]
    half = lax.axis_index("col")
    zeros = (jnp.zeros((8, hidden), F32),) * (rows * cols // 8)
    source[...] = d_tri_ref[...].astype(F32)
    d_right_s[at(half, cols * cols), :] = d_right[...]

    def right_block(p, carry):
        sums = contract(
            rows,
            cols,
            rows * groups,
            8,
            zeros,
            source,
            lambda a, i: i * cols + p * rows + a,
            left,
            lambda i: i * cols,
        )
        start = (1 - half) * cols * cols + p * cells
        for t, value in enumerate(sums):
            d_right_s[tile(start + t * 8), :] = value
        return carry

    lax.fori_loop(0, cols // rows, right_block, 0)

    for which, left_gate, left_value, right_gate, right_value in (
        (0, left_gate_0, left_value_0, right_gate_0, right_value_0),
        (1, left_gate_1, left_value_1, right_gate_1, right_value_1),
    ):

        def left_block(
            b,
            carry,
            which=which,
            left_gate=left_gate,
            left_value=left_value,
            right_gate=right_gate,
            right_value=right_value,
        ):
            p = row_block(which, b)
            start = p * cells
            sums = contract(
                rows,
                cols,
                cols,
                8,
                tuple(d_left[tile(start + t * 8), :] for t in range(cells // 8)),
                source,
                lambda a, j: (p * rows + a) * cols + j,
                right,
                lambda j: ((1 - half) * cols + j) * cols,
            )
            part, place = at(b, cells), at(p, cells)
            grads = jnp.concatenate(sums, axis=0)
            d_proj[place, :hidden] = (grads * left_value[part, :]).astype(BF16)
            d_proj[place, hidden : 2 * hidden] = (grads * left_gate[part, :]).astype(BF16)
            grads = d_right_s[place, :]
            d_proj[place, 2 * hidden : 3 * hidden] = (grads * right_value[part, :]).astype(BF16)
            d_proj[place, 3 * hidden :] = (grads * right_gate[part, :]).astype(BF16)
            return carry

        lax.fori_loop(0, groups // 2, left_block, 0)

    scale = 1.0 / (rows * groups)
    proj_grad[...] = dot(normed[...], d_proj[...], BY_ROWS) * scale


def outputs_kernel(
    sizes,
    params,
    pair,
    d_proj,
    d_gate,
    proj_weight,
    gate_weight,
    block_in,
    small_own,
    small_mate,
    block_out,
    pair_grad,
    gate_grad,
    out_grad,
):
    rows, cols, _ = sizes
    cells = rows * cols
    own = at(lax.axis_index("row"), cells)
    d_normed = dot(d_proj[own, :], proj_weight[...], TRANSPOSED) + dot(
        d_gate[own, :], gate_weight[...], TRANSPOSED
    )
    gain = params[0:1, :]
    _, hat, inverse = layer_norm(pair[...].astype(F32), gain, params[1:2, :])
    pair_grad[...] = norm_back(d_normed, gain, hat, inverse)
    block_out[...] = block_in[...]
    channels = gate_grad.shape[1]
    small = small_own[...] + small_mate[...]
    gate_grad[...] = small[:, :channels]
    out_grad[...] = small[:, channels:]


def replicated(
    pair_rep,
    cotangent,
    norm_gain,
    norm_bias,
    proj_weight,
    gate_weight,
    tri_gain,
    tri_bias,
    out_weight,
):
    rows, cols, channels = pair_rep.shape
    hidden = tri_gain.shape[0]
    groups = lax.axis_size("row")
    cells = rows * cols
    every = cells * groups
    some = every // 2
    sizes = (rows, cols, groups)

    def call(kernel, outs, *args, scratch=(), micros=1, name, **more):
        cost = pl.CostEstimate(flops=micros * 10**9, bytes_accessed=0, transcendentals=0)
        return pl.pallas_call(
            functools.partial(kernel, sizes),
            out_shape=[jax.ShapeDtypeStruct(*out) for out in outs],
            scratch_shapes=[pltpu.VMEM(*one) if isinstance(one, tuple) else one for one in scratch],
            **more,
            compiler_params=pltpu.CompilerParams(vmem_limit_bytes=VMEM_BUDGET),
            cost_estimate=cost,
            name=name,
        )(*args)

    def across(value, mask):
        return lax.ppermute(value, "row", [(i, i ^ mask) for i in range(groups)])

    def over(value):
        return lax.ppermute(value, "col", SWAP)

    def along(value, last):
        got = [last]
        for s in reversed(range(1, groups // 2 - 1)):
            got.append(after(across(value, 2 * s), got[-1]))
        return got[:0:-1]

    def join(*values):
        return jnp.concatenate(values, axis=0)

    def after(value, *others):
        return lax.optimization_barrier((value, *others))[0]

    full, part = (every, hidden), (some, hidden)

    def own_edges(*blocks):
        outs = [((some, channels), BF16)] + [(part, F32)] * 6
        return call(own_edges_kernel, outs, params, proj_weight, *blocks, name="own_edges")

    def mate_edges(*blocks):
        outs = [(part, F32)] * 2
        return call(mate_edges_kernel, outs, params, proj_weight, *blocks, name="mate_edges")

    pair_in = pair_rep.reshape(cells, channels)
    span = groups - 2
    pair_last = across(pair_in, span)
    given = [pair_in, cotangent.reshape(cells, channels)]
    given += [v[None] for v in (norm_gain, norm_bias, tri_gain, tri_bias)]
    given += [proj_weight, gate_weight, out_weight]
    given = [pltpu.with_memory_space_constraint(v, pltpu.HBM) for v in given]
    both, params, proj_weight, gate_weight, out_weight = call(
        fetch_kernel,
        [((2 * cells, channels), BF16), ((4, channels), F32)] + [(a.shape, BF16) for a in given[6:]],
        *given,
        scratch=[pltpu.SemaphoreType.DMA((len(given),))],
        in_specs=[pl.BlockSpec(memory_space=pltpu.HBM)] * len(given),
        name="fetch",
    )
    got = along(both, pair_last)
    both_far = across(both, 1)
    pair, pair_far = both[:cells], both_far[:cells]
    cot_0, cot_1 = both[cells:], both_far[cells:]
    near_all = join(*(block[:cells] for block in got), pair_last)
    far = across(near_all, 1)
    cot_last = across(cot_0, span)
    cot_near = join(*(block[cells:] for block in got), cot_last)
    cot_far = across(cot_near, 1)
    mate_near = over(join(pair, near_all))
    own_0 = own_edges(pair, near_all)
    mate_0 = mate_edges(mate_near)
    far_all = join(pair_far, far)
    own_1 = own_edges(far_all)
    mate_1 = mate_edges(over(far_all))
    own, mate = (own_0, own_1), (mate_0, mate_1)
    normed = [o[0] for o in own]
    left, left_gate, left_value = ([o[n] for o in own] for n in (1, 2, 3))
    right, right_gate, right_value = ([o[n] for o in own] for n in (4, 5, 6))
    (tri,) = call(
        triangle_kernel,
        [(full, F32)],
        *left,
        *(m[0] for m in mate),
        *right,
        *(m[1] for m in mate),
        scratch=[((cols * cols, hidden), F32)] * 2,
        micros=2,
        name="triangle",
    )
    block_out, d_tri, d_gate, tri_norm, d_update = call(
        cells_kernel,
        [((cells, channels), BF16)] + [(full, BF16)] * 4,
        params,
        tri,
        *normed,
        gate_weight,
        out_weight,
        cot_0,
        cot_near,
        cot_1,
        cot_far,
        micros=2,
        name="cells",
    )
    d_tri_mate = over(d_tri)
    left_all, right_all, normed_all, d_left, d_right, small_grads = call(
        early_kernel,
        [
            (full, F32),
            (full, F32),
            ((every, channels), BF16),
            (full, F32),
            (part, F32),
            ((channels, 2 * channels), F32),
        ],
        d_tri,
        d_gate,
        tri_norm,
        d_update,
        *normed,
        *left,
        *right,
        scratch=[(full, F32)],
        micros=30,
        name="early",
    )
    small_mate = over(small_grads)
    proj_grad, d_proj = call(
        late_kernel,
        [((channels, 4 * hidden), F32), ((every, 4 * hidden), BF16)],
        d_tri_mate,
        left_all,
        right_all,
        normed_all,
        d_left,
        d_right,
        *left_gate,
        *left_value,
        *right_gate,
        *right_value,
        scratch=[(full, F32), (full, F32)],
        micros=40,
        name="late",
    )
    proj_mate = over(proj_grad)
    square = ((channels, channels), F32)
    block_out, pair_grad, gate_grad, out_grad = call(
        outputs_kernel,
        [((cells, channels), BF16), ((cells, channels), F32), square, square],
        params,
        pair,
        d_proj,
        d_gate,
        proj_weight,
        gate_weight,
        block_out,
        small_grads,
        small_mate,
        micros=10,
        name="outputs",
    )
    return (
        block_out.reshape(pair_rep.shape),
        pair_grad.reshape(pair_rep.shape),
        proj_grad + proj_mate,
        gate_grad,
        out_grad,
    )


def sharded(
    pair_rep,
    cotangent,
    norm_gain,
    norm_bias,
    proj_weight,
    gate_weight,
    tri_gain,
    tri_bias,
    out_weight,
):
    f32 = jnp.float32
    bf16 = jnp.bfloat16
    hidden = tri_gain.shape[0]
    channels = norm_gain.shape[0]
    row_count = pair_rep.shape[0]
    col_count = pair_rep.shape[1]
    crop_len = row_count * lax.axis_size("row")
    normed_f, pair_hat, pair_inv = layer_norm(pair_rep.astype(f32), norm_gain, norm_bias)
    normed = normed_f.astype(bf16)
    projected = jnp.einsum("ijc,cd->ijd", normed, proj_weight, preferred_element_type=f32)
    sig_left = jax.nn.sigmoid(projected[..., 0:hidden])
    val_left = projected[..., hidden : 2 * hidden]
    sig_right = jax.nn.sigmoid(projected[..., 2 * hidden : 3 * hidden])
    val_right = projected[..., 3 * hidden : 4 * hidden]
    left_edge = (sig_left * val_left).astype(bf16)
    right_edge = (sig_right * val_right).astype(bf16)
    out_gate = jax.nn.sigmoid(
        jnp.einsum("ijc,cd->ijd", normed, gate_weight, preferred_element_type=f32)
    )
    right_all = lax.all_gather(right_edge, "row", axis=0, tiled=True)
    block = right_all
    triangle = lax.psum_scatter(
        jnp.einsum("ikc,jkc->jic", left_edge, block, preferred_element_type=f32),
        "col",
        scatter_dimension=0,
        tiled=True,
    ).transpose(1, 0, 2)
    tri_f, tri_hat, tri_inv = layer_norm(triangle, tri_gain, tri_bias)
    tri_norm = tri_f.astype(bf16)
    update = jnp.einsum("ijh,hc->ijc", tri_norm, out_weight, preferred_element_type=f32)
    block_out = (out_gate * update).astype(bf16)
    cot = cotangent.astype(f32)
    d_update = (cot * out_gate).astype(bf16)
    d_gate = (cot * update * out_gate * (1.0 - out_gate)).astype(bf16)
    d_norm = jnp.einsum("ijc,hc->ijh", d_update, out_weight, preferred_element_type=f32)
    d_triangle = norm_back(d_norm, tri_gain, tri_hat, tri_inv).astype(bf16)
    tri_rows = lax.all_gather(d_triangle, "col", axis=1, tiled=True)
    d_left = jnp.einsum("ijc,jkc->ikc", tri_rows, right_all, preferred_element_type=f32)
    tri_cols = lax.all_to_all(tri_rows, "row", split_axis=1, concat_axis=0, tiled=True)
    block = tri_cols
    d_right = jnp.einsum(
        "ijc,ikc->jkc",
        block,
        lax.all_gather(left_edge, "row", axis=0, tiled=True),
        preferred_element_type=f32,
    )
    d_proj = jnp.concatenate(
        [
            d_left * val_left * sig_left * (1.0 - sig_left),
            d_left * sig_left,
            d_right * val_right * sig_right * (1.0 - sig_right),
            d_right * sig_right,
        ],
        axis=-1,
    ).astype(bf16)
    d_normed = jnp.einsum(
        "ijd,cd->ijc", d_proj, proj_weight, preferred_element_type=f32
    ) + jnp.einsum("ijd,cd->ijc", d_gate, gate_weight, preferred_element_type=f32)
    pair_grad = norm_back(d_normed, norm_gain, pair_hat, pair_inv)
    cells = row_count * col_count
    flat_norm = normed.reshape(cells, channels)
    local_proj = (
        jnp.dot(flat_norm.T, d_proj.reshape(cells, 4 * hidden), preferred_element_type=f32)
        / crop_len
    )
    local_gate = (
        jnp.dot(flat_norm.T, d_gate.reshape(cells, channels), preferred_element_type=f32) / crop_len
    )
    local_out = (
        jnp.dot(
            tri_norm.reshape(cells, hidden).T,
            d_update.reshape(cells, channels),
            preferred_element_type=f32,
        )
        / crop_len
    )
    proj_grad, gate_grad, out_grad = lax.psum((local_proj, local_gate, local_out), ("row", "col"))
    return (block_out, pair_grad, proj_grad, gate_grad, out_grad)


def local(pair_rep, *others):
    rows, cols, channels = pair_rep.shape
    hidden = others[7].shape[0]
    groups = lax.axis_size("row")
    every = rows * groups * cols
    fits = 24 * every * channels * 4 <= VMEM_BUDGET and hidden == channels
    paired = lax.axis_size("col") == 2 and groups & (groups - 1) == 0 and groups >= 4
    whole_tiles = cols % 8 == 0 and cols % (2 * rows) == 0 and rows * cols % 16 == 0
    plan = replicated if fits and paired and whole_tiles else sharded
    return plan(pair_rep, *others)


def solution(mesh):
    return jax.shard_map(
        local,
        mesh=mesh,
        in_specs=(
            P(("crop", "row"), "col", None),
            P(("crop", "row"), "col", None),
            P(),
            P(),
            P(),
            P(),
            P(),
            P(),
            P(),
        ),
        out_specs=(
            P(("crop", "row"), "col", None),
            P(("crop", "row"), "col", None),
            P("crop", None),
            P("crop", None),
            P("crop", None),
        ),
        check_vma=False,
    )
```

```python
import functools

import jax
import jax.numpy as jnp
from jax import lax
from jax.experimental import pallas as pl
from jax.experimental.pallas import tpu as pltpu
from jax.sharding import PartitionSpec as P

F32 = jnp.float32
BF16 = jnp.bfloat16
VMEM_BUDGET = 24 * 2**20
SWAP = ((0, 1), (1, 0))
NATIVE = ((1,), (0,))
BY_ROWS = ((0,), (0,))
TRANSPOSED = ((1,), (1,))


def layer_norm(values, gain, bias):
    centred = values - jnp.mean(values, axis=-1, keepdims=True)
    inverse = lax.rsqrt(jnp.mean(centred * centred, axis=-1, keepdims=True) + 1e-05)
    scaled = centred * inverse
    return (scaled * gain + bias, scaled, inverse)


def norm_back(grads, gain, scaled, inverse):
    weighted = grads * gain
    first = jnp.mean(weighted, axis=-1, keepdims=True)
    second = jnp.mean(weighted * scaled, axis=-1, keepdims=True)
    return inverse * (weighted - first - scaled * second)


def sigmoid(values):
    return 0.5 * jnp.tanh(0.5 * values) + 0.5


def dot(a, b, contract=NATIVE):
    return lax.dot_general(a, b, (contract, ((), ())), preferred_element_type=F32)


def at(index, size):
    return pl.ds(pl.multiple_of(index * size, size), size)


def tile(start):
    return pl.ds(pl.multiple_of(start, 8), 8)


def places(groups):
    me = lax.axis_index("row")
    return [lax.bitwise_xor(me // 2, t) for t in range(groups // 2)]


def row_block(which, b):
    me = lax.axis_index("row")
    parity = lax.rem(me, 2)
    return 2 * b + (parity if which == 0 else 1 - parity)


def edges(blocks, params, proj_weight):
    hidden = proj_weight.shape[1] // 4
    values = jnp.concatenate([block[...] for block in blocks], axis=0).astype(F32)
    normed = layer_norm(values, params[0:1, :], params[1:2, :])[0].astype(BF16)
    projected = dot(normed, proj_weight[...])
    sides = []
    for start in (0, 2 * hidden):
        gate = sigmoid(projected[:, start : start + hidden])
        edge = gate * projected[:, start + hidden : start + 2 * hidden]
        sides.append((edge.astype(BF16).astype(F32), gate, edge * (1.0 - gate)))
    return normed, sides


def fetch_kernel(sizes, *refs):
    cells = sizes[0] * sizes[1]
    pair, cot, gain_0, bias_0, gain_1, bias_1, *weights = refs[:9]
    both, params, *held = refs[9:14]
    sems = refs[14]
    moves = [(pair, both.at[:cells]), (cot, both.at[cells:])]
    moves += [(v, params.at[n : n + 1]) for n, v in enumerate((gain_0, bias_0, gain_1, bias_1))]
    moves += list(zip(weights, held, strict=True))
    copies = [pltpu.make_async_copy(a, b, sems.at[n]) for n, (a, b) in enumerate(moves)]
    for copy in copies:
        copy.start()
    for copy in copies:
        copy.wait()


def own_edges_kernel(sizes, params, weight, *refs):
    rows, cols, groups = sizes
    cells = rows * cols
    blocks, normed_out, outs = refs[:-7], refs[-7], refs[-6:]
    normed, sides = edges(blocks, params, weight)
    for t, b in enumerate(places(groups)):
        part = slice(t * cells, (t + 1) * cells)
        place = at(b, cells)
        normed_out[place, :] = normed[part]
        for out, value in zip(outs, sides[0] + sides[1], strict=True):
            out[place, :] = value[part]


def mate_edges_kernel(sizes, params, weight, *refs):
    rows, cols, groups = sizes
    cells = rows * cols
    blocks, left, right = refs[:-2], refs[-2], refs[-1]
    _, sides = edges(blocks, params, weight)
    for t, b in enumerate(places(groups)):
        part = slice(t * cells, (t + 1) * cells)
        left[at(b, cells), :] = sides[0][0][part]
        right[at(b, cells), :] = sides[1][0][part]


def triangle_kernel(sizes, *refs):
    rows, cols, groups = sizes
    cells = rows * cols
    lefts, rights, (tri,), picked = refs[:4], refs[4:8], refs[8:9], refs[9:]
    hidden = tri.shape[-1]
    half = lax.axis_index("col")
    zero = jnp.zeros((8, hidden), F32)
    count = cols // 8
    blocks = cols // rows
    for side in range(2):
        for which in range(2):
            for s in range(blocks // 2):
                b = half * (blocks // 2) + s
                p = row_block(which, b) - half * blocks
                picked[side][at(p, cells), :] = rights[2 * side + which][at(b, cells), :]

    for which in range(2):

        def tri_block(b, carry, which=which):
            def step(k, sums):
                new = list(sums)
                for side in range(2):
                    left = lefts[2 * side + which]
                    tiles = [
                        picked[side][pl.ds(t * 8 * cols + k, 8, stride=cols), :]
                        for t in range(count)
                    ]
                    for a in range(rows):
                        row = left[pl.ds((b * rows + a) * cols + k, 1), :]
                        for t in range(count):
                            new[a * count + t] += row * tiles[t]
                return tuple(new)

            sums = lax.fori_loop(0, cols, step, (zero,) * (rows * count), unroll=4)
            start = row_block(which, b) * cells
            for t, value in enumerate(sums):
                tri[tile(start + t * 8), :] = value
            return carry

        lax.fori_loop(0, groups // 2, tri_block, 0)


def cells_kernel(
    sizes,
    params,
    tri,
    normed_0,
    normed_1,
    gate_weight,
    out_weight,
    *refs,
):
    rows, cols, groups = sizes
    cells = rows * cols
    cots, (block_out, d_tri, d_gate, tri_norm_out, d_update_out) = refs[:-5], refs[-5:]
    gain, bias = params[2:3, :], params[3:4, :]
    for which, normed in ((0, normed_0), (1, normed_1)):
        for t, b in enumerate(places(groups)):
            if t == 0:
                cot = cots[2 * which][...]
            elif t < groups // 2 - 1:
                cot = cots[2 * which + 1][(t - 1) * cells : t * cells, :]
            else:
                cot = cots[4][which * cells : (which + 1) * cells, :]
            place = at(row_block(which, b), cells)
            tri_f, hat, inverse = layer_norm(tri[place, :], gain, bias)
            tri_norm = tri_f.astype(BF16)
            update = dot(tri_norm, out_weight[...])
            out_gate = sigmoid(dot(normed[at(b, cells), :], gate_weight[...]))
            if which == 0 and t == 0:
                block_out[...] = (out_gate * update).astype(BF16)
            gated = cot.astype(F32) * out_gate
            d_update = gated.astype(BF16)
            d_gate[place, :] = (gated * update * (1.0 - out_gate)).astype(BF16)
            d_norm = dot(d_update, out_weight[...], TRANSPOSED)
            d_tri[place, :] = norm_back(d_norm, gain, hat, inverse).astype(BF16)
            tri_norm_out[place, :] = tri_norm
            d_update_out[place, :] = d_update


def contract(rows, cols, count, unroll, start, source, row_at, operand, operand_at):
    tiles = cols // 8

    def step(term, sums):
        new = list(sums)
        loaded = [operand[tile(operand_at(term) + t * 8), :] for t in range(tiles)]
        for a in range(rows):
            row = source[pl.ds(row_at(a, term), 1), :]
            for t in range(tiles):
                new[a * tiles + t] += row * loaded[t]
        return tuple(new)

    return lax.fori_loop(0, count, step, start, unroll=unroll)


def early_kernel(
    sizes,
    d_tri_ref,
    d_gate,
    tri_norm,
    d_update,
    normed_0,
    normed_1,
    left_0,
    left_1,
    right_0,
    right_1,
    left,
    right,
    normed,
    d_left,
    d_right,
    small_grads,
    source,
):
    rows, cols, groups = sizes
    cells = rows * cols
    hidden = left.shape[-1]
    channels = normed.shape[-1]
    half = lax.axis_index("col")
    zeros = (jnp.zeros((8, hidden), F32),) * (rows * cols // 8)
    source[...] = d_tri_ref[...].astype(F32)
    for which, part_n, part_l, part_r in (
        (0, normed_0, left_0, right_0),
        (1, normed_1, left_1, right_1),
    ):
        for b in range(groups // 2):
            place, part = at(row_block(which, b), cells), slice(b * cells, (b + 1) * cells)
            normed[place, :] = part_n[part, :]
            left[place, :] = part_l[part, :]
            right[place, :] = part_r[part, :]

    def left_block(p, carry):
        sums = contract(
            rows,
            cols,
            cols,
            8,
            zeros,
            source,
            lambda a, j: (p * rows + a) * cols + j,
            right,
            lambda j: (half * cols + j) * cols,
        )
        for t, value in enumerate(sums):
            d_left[tile(p * cells + t * 8), :] = value
        return carry

    lax.fori_loop(0, groups, left_block, 0)

    def right_block(p, carry):
        sums = contract(
            rows,
            cols,
            rows * groups,
            8,
            zeros,
            source,
            lambda a, i: i * cols + p * rows + a,
            left,
            lambda i: i * cols,
        )
        for t, value in enumerate(sums):
            d_right[tile(p * cells + t * 8), :] = value
        return carry

    lax.fori_loop(0, cols // rows, right_block, 0)
    scale = 1.0 / (rows * groups)
    small_grads[:, :channels] = dot(normed[...], d_gate[...], BY_ROWS) * scale
    small_grads[:, channels:] = dot(tri_norm[...], d_update[...], BY_ROWS) * scale


def late_kernel(
    sizes,
    d_tri_ref,
    left,
    right,
    normed,
    d_left,
    d_right,
    left_gate_0,
    left_gate_1,
    left_value_0,
    left_value_1,
    right_gate_0,
    right_gate_1,
    right_value_0,
    right_value_1,
    proj_grad,
    d_proj,
    source,
    d_right_s,
):
    rows, cols, groups = sizes
    cells = rows * cols
    hidden = left.shape[-1]
    half = lax.axis_index("col")
    zeros = (jnp.zeros((8, hidden), F32),) * (rows * cols // 8)
    source[...] = d_tri_ref[...].astype(F32)
    d_right_s[at(half, cols * cols), :] = d_right[...]

    def right_block(p, carry):
        sums = contract(
            rows,
            cols,
            rows * groups,
            8,
            zeros,
            source,
            lambda a, i: i * cols + p * rows + a,
            left,
            lambda i: i * cols,
        )
        start = (1 - half) * cols * cols + p * cells
        for t, value in enumerate(sums):
            d_right_s[tile(start + t * 8), :] = value
        return carry

    lax.fori_loop(0, cols // rows, right_block, 0)

    for which, left_gate, left_value, right_gate, right_value in (
        (0, left_gate_0, left_value_0, right_gate_0, right_value_0),
        (1, left_gate_1, left_value_1, right_gate_1, right_value_1),
    ):

        def left_block(
            b,
            carry,
            which=which,
            left_gate=left_gate,
            left_value=left_value,
            right_gate=right_gate,
            right_value=right_value,
        ):
            p = row_block(which, b)
            start = p * cells
            sums = contract(
                rows,
                cols,
                cols,
                8,
                tuple(d_left[tile(start + t * 8), :] for t in range(cells // 8)),
                source,
                lambda a, j: (p * rows + a) * cols + j,
                right,
                lambda j: ((1 - half) * cols + j) * cols,
            )
            part, place = at(b, cells), at(p, cells)
            grads = jnp.concatenate(sums, axis=0)
            d_proj[place, :hidden] = (grads * left_value[part, :]).astype(BF16)
            d_proj[place, hidden : 2 * hidden] = (grads * left_gate[part, :]).astype(BF16)
            grads = d_right_s[place, :]
            d_proj[place, 2 * hidden : 3 * hidden] = (grads * right_value[part, :]).astype(BF16)
            d_proj[place, 3 * hidden :] = (grads * right_gate[part, :]).astype(BF16)
            return carry

        lax.fori_loop(0, groups // 2, left_block, 0)

    scale = 1.0 / (rows * groups)
    proj_grad[...] = dot(normed[...], d_proj[...], BY_ROWS) * scale


def outputs_kernel(
    sizes,
    params,
    pair,
    d_proj,
    d_gate,
    proj_weight,
    gate_weight,
    block_in,
    small_own,
    small_mate,
    block_out,
    pair_grad,
    gate_grad,
    out_grad,
):
    rows, cols, _ = sizes
    cells = rows * cols
    own = at(lax.axis_index("row"), cells)
    d_normed = dot(d_proj[own, :], proj_weight[...], TRANSPOSED) + dot(
        d_gate[own, :], gate_weight[...], TRANSPOSED
    )
    gain = params[0:1, :]
    _, hat, inverse = layer_norm(pair[...].astype(F32), gain, params[1:2, :])
    pair_grad[...] = norm_back(d_normed, gain, hat, inverse)
    block_out[...] = block_in[...]
    channels = gate_grad.shape[1]
    small = small_own[...] + small_mate[...]
    gate_grad[...] = small[:, :channels]
    out_grad[...] = small[:, channels:]


def replicated(
    pair_rep,
    cotangent,
    norm_gain,
    norm_bias,
    proj_weight,
    gate_weight,
    tri_gain,
    tri_bias,
    out_weight,
):
    rows, cols, channels = pair_rep.shape
    hidden = tri_gain.shape[0]
    groups = lax.axis_size("row")
    cells = rows * cols
    every = cells * groups
    some = every // 2
    sizes = (rows, cols, groups)

    def call(kernel, outs, *args, scratch=(), micros=1, name, **more):
        cost = pl.CostEstimate(flops=micros * 10**9, bytes_accessed=0, transcendentals=0)
        return pl.pallas_call(
            functools.partial(kernel, sizes),
            out_shape=[jax.ShapeDtypeStruct(*out) for out in outs],
            scratch_shapes=[pltpu.VMEM(*one) if isinstance(one, tuple) else one for one in scratch],
            **more,
            compiler_params=pltpu.CompilerParams(vmem_limit_bytes=VMEM_BUDGET),
            cost_estimate=cost,
            name=name,
        )(*args)

    def across(value, mask):
        return lax.ppermute(value, "row", [(i, i ^ mask) for i in range(groups)])

    def over(value):
        return lax.ppermute(value, "col", SWAP)

    def along(value, last):
        got = [last]
        for s in reversed(range(1, groups // 2 - 1)):
            got.append(after(across(value, 2 * s), got[-1]))
        return got[:0:-1]

    def join(*values):
        return jnp.concatenate(values, axis=0)

    def after(value, *others):
        return lax.optimization_barrier((value, *others))[0]

    full, part = (every, hidden), (some, hidden)

    def own_edges(*blocks):
        outs = [((some, channels), BF16)] + [(part, F32)] * 6
        return call(own_edges_kernel, outs, params, proj_weight, *blocks, name="own_edges")

    def mate_edges(*blocks):
        outs = [(part, F32)] * 2
        return call(mate_edges_kernel, outs, params, proj_weight, *blocks, name="mate_edges")

    pair_in = pair_rep.reshape(cells, channels)
    span = groups - 2
    pair_last = across(pair_in, span)
    given = [pair_in, cotangent.reshape(cells, channels)]
    given += [v[None] for v in (norm_gain, norm_bias, tri_gain, tri_bias)]
    given += [proj_weight, gate_weight, out_weight]
    given = [pltpu.with_memory_space_constraint(v, pltpu.HBM) for v in given]
    both, params, proj_weight, gate_weight, out_weight = call(
        fetch_kernel,
        [((2 * cells, channels), BF16), ((4, channels), F32)] + [(a.shape, BF16) for a in given[6:]],
        *given,
        scratch=[pltpu.SemaphoreType.DMA((len(given),))],
        in_specs=[pl.BlockSpec(memory_space=pltpu.HBM)] * len(given),
        name="fetch",
    )
    got = along(both, pair_last)
    both_far = across(both, 1)
    pair, pair_far = both[:cells], both_far[:cells]
    cot_0, cot_1 = both[cells:], both_far[cells:]
    near_all = join(*(block[:cells] for block in got), pair_last)
    far = across(near_all, 1)
    cot_near = join(*(block[cells:] for block in got))
    cot_far = across(cot_near, 1)
    cot_last = across(after(join(cot_0, cot_1), near_all), span)
    mate_near = over(join(pair, near_all))
    own_0 = own_edges(pair, near_all)
    mate_0 = mate_edges(mate_near)
    far_all = join(pair_far, far)
    own_1 = own_edges(far_all)
    mate_1 = mate_edges(over(far_all))
    own, mate = (own_0, own_1), (mate_0, mate_1)
    normed = [o[0] for o in own]
    left, left_gate, left_value = ([o[n] for o in own] for n in (1, 2, 3))
    right, right_gate, right_value = ([o[n] for o in own] for n in (4, 5, 6))
    (tri,) = call(
        triangle_kernel,
        [(full, F32)],
        *left,
        *(m[0] for m in mate),
        *right,
        *(m[1] for m in mate),
        scratch=[((cols * cols, hidden), F32)] * 2,
        micros=2,
        name="triangle",
    )
    block_out, d_tri, d_gate, tri_norm, d_update = call(
        cells_kernel,
        [((cells, channels), BF16)] + [(full, BF16)] * 4,
        params,
        tri,
        *normed,
        gate_weight,
        out_weight,
        cot_0,
        cot_near,
        cot_1,
        cot_far,
        cot_last,
        micros=2,
        name="cells",
    )
    d_tri_mate = over(d_tri)
    left_all, right_all, normed_all, d_left, d_right, small_grads = call(
        early_kernel,
        [
            (full, F32),
            (full, F32),
            ((every, channels), BF16),
            (full, F32),
            (part, F32),
            ((channels, 2 * channels), F32),
        ],
        d_tri,
        d_gate,
        tri_norm,
        d_update,
        *normed,
        *left,
        *right,
        scratch=[(full, F32)],
        micros=30,
        name="early",
    )
    small_mate = over(small_grads)
    proj_grad, d_proj = call(
        late_kernel,
        [((channels, 4 * hidden), F32), ((every, 4 * hidden), BF16)],
        d_tri_mate,
        left_all,
        right_all,
        normed_all,
        d_left,
        d_right,
        *left_gate,
        *left_value,
        *right_gate,
        *right_value,
        scratch=[(full, F32), (full, F32)],
        micros=40,
        name="late",
    )
    proj_mate = over(proj_grad)
    square = ((channels, channels), F32)
    block_out, pair_grad, gate_grad, out_grad = call(
        outputs_kernel,
        [((cells, channels), BF16), ((cells, channels), F32), square, square],
        params,
        pair,
        d_proj,
        d_gate,
        proj_weight,
        gate_weight,
        block_out,
        small_grads,
        small_mate,
        micros=10,
        name="outputs",
    )
    return (
        block_out.reshape(pair_rep.shape),
        pair_grad.reshape(pair_rep.shape),
        proj_grad + proj_mate,
        gate_grad,
        out_grad,
    )


def sharded(
    pair_rep,
    cotangent,
    norm_gain,
    norm_bias,
    proj_weight,
    gate_weight,
    tri_gain,
    tri_bias,
    out_weight,
):
    f32 = jnp.float32
    bf16 = jnp.bfloat16
    hidden = tri_gain.shape[0]
    channels = norm_gain.shape[0]
    row_count = pair_rep.shape[0]
    col_count = pair_rep.shape[1]
    crop_len = row_count * lax.axis_size("row")
    normed_f, pair_hat, pair_inv = layer_norm(pair_rep.astype(f32), norm_gain, norm_bias)
    normed = normed_f.astype(bf16)
    projected = jnp.einsum("ijc,cd->ijd", normed, proj_weight, preferred_element_type=f32)
    sig_left = jax.nn.sigmoid(projected[..., 0:hidden])
    val_left = projected[..., hidden : 2 * hidden]
    sig_right = jax.nn.sigmoid(projected[..., 2 * hidden : 3 * hidden])
    val_right = projected[..., 3 * hidden : 4 * hidden]
    left_edge = (sig_left * val_left).astype(bf16)
    right_edge = (sig_right * val_right).astype(bf16)
    out_gate = jax.nn.sigmoid(
        jnp.einsum("ijc,cd->ijd", normed, gate_weight, preferred_element_type=f32)
    )
    right_all = lax.all_gather(right_edge, "row", axis=0, tiled=True)
    block = right_all
    triangle = lax.psum_scatter(
        jnp.einsum("ikc,jkc->jic", left_edge, block, preferred_element_type=f32),
        "col",
        scatter_dimension=0,
        tiled=True,
    ).transpose(1, 0, 2)
    tri_f, tri_hat, tri_inv = layer_norm(triangle, tri_gain, tri_bias)
    tri_norm = tri_f.astype(bf16)
    update = jnp.einsum("ijh,hc->ijc", tri_norm, out_weight, preferred_element_type=f32)
    block_out = (out_gate * update).astype(bf16)
    cot = cotangent.astype(f32)
    d_update = (cot * out_gate).astype(bf16)
    d_gate = (cot * update * out_gate * (1.0 - out_gate)).astype(bf16)
    d_norm = jnp.einsum("ijc,hc->ijh", d_update, out_weight, preferred_element_type=f32)
    d_triangle = norm_back(d_norm, tri_gain, tri_hat, tri_inv).astype(bf16)
    tri_rows = lax.all_gather(d_triangle, "col", axis=1, tiled=True)
    d_left = jnp.einsum("ijc,jkc->ikc", tri_rows, right_all, preferred_element_type=f32)
    tri_cols = lax.all_to_all(tri_rows, "row", split_axis=1, concat_axis=0, tiled=True)
    block = tri_cols
    d_right = jnp.einsum(
        "ijc,ikc->jkc",
        block,
        lax.all_gather(left_edge, "row", axis=0, tiled=True),
        preferred_element_type=f32,
    )
    d_proj = jnp.concatenate(
        [
            d_left * val_left * sig_left * (1.0 - sig_left),
            d_left * sig_left,
            d_right * val_right * sig_right * (1.0 - sig_right),
            d_right * sig_right,
        ],
        axis=-1,
    ).astype(bf16)
    d_normed = jnp.einsum(
        "ijd,cd->ijc", d_proj, proj_weight, preferred_element_type=f32
    ) + jnp.einsum("ijd,cd->ijc", d_gate, gate_weight, preferred_element_type=f32)
    pair_grad = norm_back(d_normed, norm_gain, pair_hat, pair_inv)
    cells = row_count * col_count
    flat_norm = normed.reshape(cells, channels)
    local_proj = (
        jnp.dot(flat_norm.T, d_proj.reshape(cells, 4 * hidden), preferred_element_type=f32)
        / crop_len
    )
    local_gate = (
        jnp.dot(flat_norm.T, d_gate.reshape(cells, channels), preferred_element_type=f32) / crop_len
    )
    local_out = (
        jnp.dot(
            tri_norm.reshape(cells, hidden).T,
            d_update.reshape(cells, channels),
            preferred_element_type=f32,
        )
        / crop_len
    )
    proj_grad, gate_grad, out_grad = lax.psum((local_proj, local_gate, local_out), ("row", "col"))
    return (block_out, pair_grad, proj_grad, gate_grad, out_grad)


def local(pair_rep, *others):
    rows, cols, channels = pair_rep.shape
    hidden = others[7].shape[0]
    groups = lax.axis_size("row")
    every = rows * groups * cols
    fits = 24 * every * channels * 4 <= VMEM_BUDGET and hidden == channels
    paired = lax.axis_size("col") == 2 and groups & (groups - 1) == 0 and groups >= 4
    whole_tiles = cols % 8 == 0 and cols % (2 * rows) == 0 and rows * cols % 16 == 0
    plan = replicated if fits and paired and whole_tiles else sharded
    return plan(pair_rep, *others)


def solution(mesh):
    return jax.shard_map(
        local,
        mesh=mesh,
        in_specs=(
            P(("crop", "row"), "col", None),
            P(("crop", "row"), "col", None),
            P(),
            P(),
            P(),
            P(),
            P(),
            P(),
            P(),
        ),
        out_specs=(
            P(("crop", "row"), "col", None),
            P(("crop", "row"), "col", None),
            P("crop", None),
            P("crop", None),
            P("crop", None),
        ),
        check_vma=False,
    )
```

```python
import functools

import jax
import jax.numpy as jnp
from jax import lax
from jax.experimental import pallas as pl
from jax.experimental.pallas import tpu as pltpu
from jax.sharding import PartitionSpec as P

F32 = jnp.float32
BF16 = jnp.bfloat16
VMEM_BUDGET = 24 * 2**20
SWAP = ((0, 1), (1, 0))
NATIVE = ((1,), (0,))
BY_ROWS = ((0,), (0,))
TRANSPOSED = ((1,), (1,))


def layer_norm(values, gain, bias):
    centred = values - jnp.mean(values, axis=-1, keepdims=True)
    inverse = lax.rsqrt(jnp.mean(centred * centred, axis=-1, keepdims=True) + 1e-05)
    scaled = centred * inverse
    return (scaled * gain + bias, scaled, inverse)


def norm_back(grads, gain, scaled, inverse):
    weighted = grads * gain
    first = jnp.mean(weighted, axis=-1, keepdims=True)
    second = jnp.mean(weighted * scaled, axis=-1, keepdims=True)
    return inverse * (weighted - first - scaled * second)


def sigmoid(values):
    return 0.5 * jnp.tanh(0.5 * values) + 0.5


def dot(a, b, contract=NATIVE):
    return lax.dot_general(a, b, (contract, ((), ())), preferred_element_type=F32)


def at(index, size):
    return pl.ds(pl.multiple_of(index * size, size), size)


def tile(start):
    return pl.ds(pl.multiple_of(start, 8), 8)


def places(groups):
    me = lax.axis_index("row")
    return [lax.bitwise_xor(me // 2, t) for t in range(groups // 2)]


def row_block(which, b):
    me = lax.axis_index("row")
    parity = lax.rem(me, 2)
    return 2 * b + (parity if which == 0 else 1 - parity)


def edges(blocks, params, proj_weight):
    hidden = proj_weight.shape[1] // 4
    values = jnp.concatenate([block[...] for block in blocks], axis=0).astype(F32)
    normed = layer_norm(values, params[0:1, :], params[1:2, :])[0].astype(BF16)
    projected = dot(normed, proj_weight[...])
    sides = []
    for start in (0, 2 * hidden):
        gate = sigmoid(projected[:, start : start + hidden])
        edge = gate * projected[:, start + hidden : start + 2 * hidden]
        sides.append((edge.astype(BF16).astype(F32), gate, edge * (1.0 - gate)))
    return normed, sides


def fetch_kernel(sizes, *refs):
    cells = sizes[0] * sizes[1]
    pair, cot, gain_0, bias_0, gain_1, bias_1, *weights = refs[:9]
    both, params, *held = refs[9:14]
    sems = refs[14]
    moves = [(pair, both.at[:cells]), (cot, both.at[cells:])]
    moves += [(v, params.at[n : n + 1]) for n, v in enumerate((gain_0, bias_0, gain_1, bias_1))]
    moves += list(zip(weights, held, strict=True))
    copies = [pltpu.make_async_copy(a, b, sems.at[n]) for n, (a, b) in enumerate(moves)]
    for copy in copies:
        copy.start()
    for copy in copies:
        copy.wait()


def own_edges_kernel(sizes, params, weight, *refs):
    rows, cols, groups = sizes
    cells = rows * cols
    blocks, normed_out, outs = refs[:-7], refs[-7], refs[-6:]
    normed, sides = edges(blocks, params, weight)
    for t, b in enumerate(places(groups)):
        part = slice(t * cells, (t + 1) * cells)
        place = at(b, cells)
        normed_out[place, :] = normed[part]
        for out, value in zip(outs, sides[0] + sides[1], strict=True):
            out[place, :] = value[part]


def mate_edges_kernel(sizes, params, weight, *refs):
    rows, cols, groups = sizes
    cells = rows * cols
    blocks, left, right = refs[:-2], refs[-2], refs[-1]
    _, sides = edges(blocks, params, weight)
    for t, b in enumerate(places(groups)):
        part = slice(t * cells, (t + 1) * cells)
        left[at(b, cells), :] = sides[0][0][part]
        right[at(b, cells), :] = sides[1][0][part]


def triangle_kernel(sizes, *refs):
    rows, cols, groups = sizes
    cells = rows * cols
    lefts, rights, (tri,), picked = refs[:4], refs[4:8], refs[8:9], refs[9:]
    hidden = tri.shape[-1]
    half = lax.axis_index("col")
    zero = jnp.zeros((8, hidden), F32)
    count = cols // 8
    blocks = cols // rows
    for side in range(2):
        for which in range(2):
            for s in range(blocks // 2):
                b = half * (blocks // 2) + s
                p = row_block(which, b) - half * blocks
                picked[side][at(p, cells), :] = rights[2 * side + which][at(b, cells), :]

    for which in range(2):

        def tri_block(b, carry, which=which):
            def step(k, sums):
                new = list(sums)
                for side in range(2):
                    left = lefts[2 * side + which]
                    tiles = [
                        picked[side][pl.ds(t * 8 * cols + k, 8, stride=cols), :]
                        for t in range(count)
                    ]
                    for a in range(rows):
                        row = left[pl.ds((b * rows + a) * cols + k, 1), :]
                        for t in range(count):
                            new[a * count + t] += row * tiles[t]
                return tuple(new)

            sums = lax.fori_loop(0, cols, step, (zero,) * (rows * count), unroll=4)
            start = row_block(which, b) * cells
            for t, value in enumerate(sums):
                tri[tile(start + t * 8), :] = value
            return carry

        lax.fori_loop(0, groups // 2, tri_block, 0)


def cells_kernel(
    sizes,
    params,
    tri,
    normed_0,
    normed_1,
    gate_weight,
    out_weight,
    *refs,
):
    rows, cols, groups = sizes
    cells = rows * cols
    cots, (block_out, d_tri, d_gate, tri_norm_out, d_update_out) = refs[:-5], refs[-5:]
    gain, bias = params[2:3, :], params[3:4, :]
    for which, normed in ((0, normed_0), (1, normed_1)):
        for t, b in enumerate(places(groups)):
            cot = cots[t][which * cells : (which + 1) * cells, :]
            place = at(row_block(which, b), cells)
            tri_f, hat, inverse = layer_norm(tri[place, :], gain, bias)
            tri_norm = tri_f.astype(BF16)
            update = dot(tri_norm, out_weight[...])
            out_gate = sigmoid(dot(normed[at(b, cells), :], gate_weight[...]))
            if which == 0 and t == 0:
                block_out[...] = (out_gate * update).astype(BF16)
            gated = cot.astype(F32) * out_gate
            d_update = gated.astype(BF16)
            d_gate[place, :] = (gated * update * (1.0 - out_gate)).astype(BF16)
            d_norm = dot(d_update, out_weight[...], TRANSPOSED)
            d_tri[place, :] = norm_back(d_norm, gain, hat, inverse).astype(BF16)
            tri_norm_out[place, :] = tri_norm
            d_update_out[place, :] = d_update


def contract(rows, cols, count, unroll, start, source, row_at, operand, operand_at):
    tiles = cols // 8

    def step(term, sums):
        new = list(sums)
        loaded = [operand[tile(operand_at(term) + t * 8), :] for t in range(tiles)]
        for a in range(rows):
            row = source[pl.ds(row_at(a, term), 1), :]
            for t in range(tiles):
                new[a * tiles + t] += row * loaded[t]
        return tuple(new)

    return lax.fori_loop(0, count, step, start, unroll=unroll)


def early_kernel(
    sizes,
    d_tri_ref,
    d_gate,
    tri_norm,
    d_update,
    normed_0,
    normed_1,
    left_0,
    left_1,
    right_0,
    right_1,
    left,
    right,
    normed,
    d_left,
    d_right,
    small_grads,
    source,
):
    rows, cols, groups = sizes
    cells = rows * cols
    hidden = left.shape[-1]
    channels = normed.shape[-1]
    half = lax.axis_index("col")
    zeros = (jnp.zeros((8, hidden), F32),) * (rows * cols // 8)
    source[...] = d_tri_ref[...].astype(F32)
    for which, part_n, part_l, part_r in (
        (0, normed_0, left_0, right_0),
        (1, normed_1, left_1, right_1),
    ):
        for b in range(groups // 2):
            place, part = at(row_block(which, b), cells), slice(b * cells, (b + 1) * cells)
            normed[place, :] = part_n[part, :]
            left[place, :] = part_l[part, :]
            right[place, :] = part_r[part, :]

    def left_block(p, carry):
        sums = contract(
            rows,
            cols,
            cols,
            8,
            zeros,
            source,
            lambda a, j: (p * rows + a) * cols + j,
            right,
            lambda j: (half * cols + j) * cols,
        )
        for t, value in enumerate(sums):
            d_left[tile(p * cells + t * 8), :] = value
        return carry

    lax.fori_loop(0, groups, left_block, 0)

    def right_block(p, carry):
        sums = contract(
            rows,
            cols,
            rows * groups,
            8,
            zeros,
            source,
            lambda a, i: i * cols + p * rows + a,
            left,
            lambda i: i * cols,
        )
        for t, value in enumerate(sums):
            d_right[tile(p * cells + t * 8), :] = value
        return carry

    lax.fori_loop(0, cols // rows, right_block, 0)
    scale = 1.0 / (rows * groups)
    small_grads[:, :channels] = dot(normed[...], d_gate[...], BY_ROWS) * scale
    small_grads[:, channels:] = dot(tri_norm[...], d_update[...], BY_ROWS) * scale


def late_kernel(
    sizes,
    d_tri_ref,
    left,
    right,
    normed,
    d_left,
    d_right,
    left_gate_0,
    left_gate_1,
    left_value_0,
    left_value_1,
    right_gate_0,
    right_gate_1,
    right_value_0,
    right_value_1,
    proj_grad,
    d_proj,
    source,
    d_right_s,
):
    rows, cols, groups = sizes
    cells = rows * cols
    hidden = left.shape[-1]
    half = lax.axis_index("col")
    zeros = (jnp.zeros((8, hidden), F32),) * (rows * cols // 8)
    source[...] = d_tri_ref[...].astype(F32)
    d_right_s[at(half, cols * cols), :] = d_right[...]

    def right_block(p, carry):
        sums = contract(
            rows,
            cols,
            rows * groups,
            8,
            zeros,
            source,
            lambda a, i: i * cols + p * rows + a,
            left,
            lambda i: i * cols,
        )
        start = (1 - half) * cols * cols + p * cells
        for t, value in enumerate(sums):
            d_right_s[tile(start + t * 8), :] = value
        return carry

    lax.fori_loop(0, cols // rows, right_block, 0)

    for which, left_gate, left_value, right_gate, right_value in (
        (0, left_gate_0, left_value_0, right_gate_0, right_value_0),
        (1, left_gate_1, left_value_1, right_gate_1, right_value_1),
    ):

        def left_block(
            b,
            carry,
            which=which,
            left_gate=left_gate,
            left_value=left_value,
            right_gate=right_gate,
            right_value=right_value,
        ):
            p = row_block(which, b)
            start = p * cells
            sums = contract(
                rows,
                cols,
                cols,
                8,
                tuple(d_left[tile(start + t * 8), :] for t in range(cells // 8)),
                source,
                lambda a, j: (p * rows + a) * cols + j,
                right,
                lambda j: ((1 - half) * cols + j) * cols,
            )
            part, place = at(b, cells), at(p, cells)
            grads = jnp.concatenate(sums, axis=0)
            d_proj[place, :hidden] = (grads * left_value[part, :]).astype(BF16)
            d_proj[place, hidden : 2 * hidden] = (grads * left_gate[part, :]).astype(BF16)
            grads = d_right_s[place, :]
            d_proj[place, 2 * hidden : 3 * hidden] = (grads * right_value[part, :]).astype(BF16)
            d_proj[place, 3 * hidden :] = (grads * right_gate[part, :]).astype(BF16)
            return carry

        lax.fori_loop(0, groups // 2, left_block, 0)

    scale = 1.0 / (rows * groups)
    proj_grad[...] = dot(normed[...], d_proj[...], BY_ROWS) * scale


def outputs_kernel(
    sizes,
    params,
    pair,
    d_proj,
    d_gate,
    proj_weight,
    gate_weight,
    block_in,
    small_own,
    small_mate,
    block_out,
    pair_grad,
    gate_grad,
    out_grad,
):
    rows, cols, _ = sizes
    cells = rows * cols
    own = at(lax.axis_index("row"), cells)
    d_normed = dot(d_proj[own, :], proj_weight[...], TRANSPOSED) + dot(
        d_gate[own, :], gate_weight[...], TRANSPOSED
    )
    gain = params[0:1, :]
    _, hat, inverse = layer_norm(pair[...].astype(F32), gain, params[1:2, :])
    pair_grad[...] = norm_back(d_normed, gain, hat, inverse)
    block_out[...] = block_in[...]
    channels = gate_grad.shape[1]
    small = small_own[...] + small_mate[...]
    gate_grad[...] = small[:, :channels]
    out_grad[...] = small[:, channels:]


def replicated(
    pair_rep,
    cotangent,
    norm_gain,
    norm_bias,
    proj_weight,
    gate_weight,
    tri_gain,
    tri_bias,
    out_weight,
):
    rows, cols, channels = pair_rep.shape
    hidden = tri_gain.shape[0]
    groups = lax.axis_size("row")
    cells = rows * cols
    every = cells * groups
    some = every // 2
    sizes = (rows, cols, groups)

    def call(kernel, outs, *args, scratch=(), micros=1, name, **more):
        cost = pl.CostEstimate(flops=micros * 10**9, bytes_accessed=0, transcendentals=0)
        return pl.pallas_call(
            functools.partial(kernel, sizes),
            out_shape=[jax.ShapeDtypeStruct(*out) for out in outs],
            scratch_shapes=[pltpu.VMEM(*one) if isinstance(one, tuple) else one for one in scratch],
            **more,
            compiler_params=pltpu.CompilerParams(vmem_limit_bytes=VMEM_BUDGET),
            cost_estimate=cost,
            name=name,
        )(*args)

    def across(value, mask):
        return lax.ppermute(value, "row", [(i, i ^ mask) for i in range(groups)])

    def over(value):
        return lax.ppermute(value, "col", SWAP)

    def along(value, tied=False):
        got = []
        for s in reversed(range(1, groups // 2)):
            arrived = across(value, 2 * s)
            got.append(after(arrived, got[-1]) if got and tied else arrived)
        return got[::-1]

    def join(*values):
        return jnp.concatenate(values, axis=0)

    def after(value, *others):
        return lax.optimization_barrier((value, *others))[0]

    full, part = (every, hidden), (some, hidden)

    def own_edges(*blocks):
        outs = [((some, channels), BF16)] + [(part, F32)] * 6
        return call(own_edges_kernel, outs, params, proj_weight, *blocks, name="own_edges")

    def mate_edges(*blocks):
        outs = [(part, F32)] * 2
        return call(mate_edges_kernel, outs, params, proj_weight, *blocks, name="mate_edges")

    pair_in = pair_rep.reshape(cells, channels)
    near = along(pair_in, tied=True)
    given = [pair_in, cotangent.reshape(cells, channels)]
    given += [v[None] for v in (norm_gain, norm_bias, tri_gain, tri_bias)]
    given += [proj_weight, gate_weight, out_weight]
    given = [pltpu.with_memory_space_constraint(v, pltpu.HBM) for v in given]
    both, params, proj_weight, gate_weight, out_weight = call(
        fetch_kernel,
        [((2 * cells, channels), BF16), ((4, channels), F32)] + [(a.shape, BF16) for a in given[6:]],
        *given,
        scratch=[pltpu.SemaphoreType.DMA((len(given),))],
        in_specs=[pl.BlockSpec(memory_space=pltpu.HBM)] * len(given),
        name="fetch",
    )
    both_far = across(both, 1)
    pair, pair_far = both[:cells], both_far[:cells]
    near_all = join(*near)
    far = across(near_all, 1)
    cots = after(join(both[cells:], both_far[cells:]), near_all)
    cots = [cots] + along(cots)
    mate_near = over(join(pair, near_all))
    own_0 = own_edges(pair, near_all)
    mate_0 = mate_edges(mate_near)
    far_all = join(pair_far, far)
    own_1 = own_edges(far_all)
    mate_1 = mate_edges(over(far_all))
    own, mate = (own_0, own_1), (mate_0, mate_1)
    normed = [o[0] for o in own]
    left, left_gate, left_value = ([o[n] for o in own] for n in (1, 2, 3))
    right, right_gate, right_value = ([o[n] for o in own] for n in (4, 5, 6))
    (tri,) = call(
        triangle_kernel,
        [(full, F32)],
        *left,
        *(m[0] for m in mate),
        *right,
        *(m[1] for m in mate),
        scratch=[((cols * cols, hidden), F32)] * 2,
        micros=2,
        name="triangle",
    )
    block_out, d_tri, d_gate, tri_norm, d_update = call(
        cells_kernel,
        [((cells, channels), BF16)] + [(full, BF16)] * 4,
        params,
        tri,
        *normed,
        gate_weight,
        out_weight,
        *cots,
        micros=2,
        name="cells",
    )
    d_tri_mate = over(d_tri)
    left_all, right_all, normed_all, d_left, d_right, small_grads = call(
        early_kernel,
        [
            (full, F32),
            (full, F32),
            ((every, channels), BF16),
            (full, F32),
            (part, F32),
            ((channels, 2 * channels), F32),
        ],
        d_tri,
        d_gate,
        tri_norm,
        d_update,
        *normed,
        *left,
        *right,
        scratch=[(full, F32)],
        micros=30,
        name="early",
    )
    small_mate = over(small_grads)
    proj_grad, d_proj = call(
        late_kernel,
        [((channels, 4 * hidden), F32), ((every, 4 * hidden), BF16)],
        d_tri_mate,
        left_all,
        right_all,
        normed_all,
        d_left,
        d_right,
        *left_gate,
        *left_value,
        *right_gate,
        *right_value,
        scratch=[(full, F32), (full, F32)],
        micros=40,
        name="late",
    )
    proj_mate = over(proj_grad)
    square = ((channels, channels), F32)
    block_out, pair_grad, gate_grad, out_grad = call(
        outputs_kernel,
        [((cells, channels), BF16), ((cells, channels), F32), square, square],
        params,
        pair,
        d_proj,
        d_gate,
        proj_weight,
        gate_weight,
        block_out,
        small_grads,
        small_mate,
        micros=10,
        name="outputs",
    )
    return (
        block_out.reshape(pair_rep.shape),
        pair_grad.reshape(pair_rep.shape),
        proj_grad + proj_mate,
        gate_grad,
        out_grad,
    )


def sharded(
    pair_rep,
    cotangent,
    norm_gain,
    norm_bias,
    proj_weight,
    gate_weight,
    tri_gain,
    tri_bias,
    out_weight,
):
    f32 = jnp.float32
    bf16 = jnp.bfloat16
    hidden = tri_gain.shape[0]
    channels = norm_gain.shape[0]
    row_count = pair_rep.shape[0]
    col_count = pair_rep.shape[1]
    crop_len = row_count * lax.axis_size("row")
    normed_f, pair_hat, pair_inv = layer_norm(pair_rep.astype(f32), norm_gain, norm_bias)
    normed = normed_f.astype(bf16)
    projected = jnp.einsum("ijc,cd->ijd", normed, proj_weight, preferred_element_type=f32)
    sig_left = jax.nn.sigmoid(projected[..., 0:hidden])
    val_left = projected[..., hidden : 2 * hidden]
    sig_right = jax.nn.sigmoid(projected[..., 2 * hidden : 3 * hidden])
    val_right = projected[..., 3 * hidden : 4 * hidden]
    left_edge = (sig_left * val_left).astype(bf16)
    right_edge = (sig_right * val_right).astype(bf16)
    out_gate = jax.nn.sigmoid(
        jnp.einsum("ijc,cd->ijd", normed, gate_weight, preferred_element_type=f32)
    )
    right_all = lax.all_gather(right_edge, "row", axis=0, tiled=True)
    block = right_all
    triangle = lax.psum_scatter(
        jnp.einsum("ikc,jkc->jic", left_edge, block, preferred_element_type=f32),
        "col",
        scatter_dimension=0,
        tiled=True,
    ).transpose(1, 0, 2)
    tri_f, tri_hat, tri_inv = layer_norm(triangle, tri_gain, tri_bias)
    tri_norm = tri_f.astype(bf16)
    update = jnp.einsum("ijh,hc->ijc", tri_norm, out_weight, preferred_element_type=f32)
    block_out = (out_gate * update).astype(bf16)
    cot = cotangent.astype(f32)
    d_update = (cot * out_gate).astype(bf16)
    d_gate = (cot * update * out_gate * (1.0 - out_gate)).astype(bf16)
    d_norm = jnp.einsum("ijc,hc->ijh", d_update, out_weight, preferred_element_type=f32)
    d_triangle = norm_back(d_norm, tri_gain, tri_hat, tri_inv).astype(bf16)
    tri_rows = lax.all_gather(d_triangle, "col", axis=1, tiled=True)
    d_left = jnp.einsum("ijc,jkc->ikc", tri_rows, right_all, preferred_element_type=f32)
    tri_cols = lax.all_to_all(tri_rows, "row", split_axis=1, concat_axis=0, tiled=True)
    block = tri_cols
    d_right = jnp.einsum(
        "ijc,ikc->jkc",
        block,
        lax.all_gather(left_edge, "row", axis=0, tiled=True),
        preferred_element_type=f32,
    )
    d_proj = jnp.concatenate(
        [
            d_left * val_left * sig_left * (1.0 - sig_left),
            d_left * sig_left,
            d_right * val_right * sig_right * (1.0 - sig_right),
            d_right * sig_right,
        ],
        axis=-1,
    ).astype(bf16)
    d_normed = jnp.einsum(
        "ijd,cd->ijc", d_proj, proj_weight, preferred_element_type=f32
    ) + jnp.einsum("ijd,cd->ijc", d_gate, gate_weight, preferred_element_type=f32)
    pair_grad = norm_back(d_normed, norm_gain, pair_hat, pair_inv)
    cells = row_count * col_count
    flat_norm = normed.reshape(cells, channels)
    local_proj = (
        jnp.dot(flat_norm.T, d_proj.reshape(cells, 4 * hidden), preferred_element_type=f32)
        / crop_len
    )
    local_gate = (
        jnp.dot(flat_norm.T, d_gate.reshape(cells, channels), preferred_element_type=f32) / crop_len
    )
    local_out = (
        jnp.dot(
            tri_norm.reshape(cells, hidden).T,
            d_update.reshape(cells, channels),
            preferred_element_type=f32,
        )
        / crop_len
    )
    proj_grad, gate_grad, out_grad = lax.psum((local_proj, local_gate, local_out), ("row", "col"))
    return (block_out, pair_grad, proj_grad, gate_grad, out_grad)


def local(pair_rep, *others):
    rows, cols, channels = pair_rep.shape
    hidden = others[7].shape[0]
    groups = lax.axis_size("row")
    every = rows * groups * cols
    fits = 24 * every * channels * 4 <= VMEM_BUDGET and hidden == channels
    paired = lax.axis_size("col") == 2 and groups & (groups - 1) == 0 and groups >= 4
    whole_tiles = cols % 8 == 0 and cols % (2 * rows) == 0 and rows * cols % 16 == 0
    plan = replicated if fits and paired and whole_tiles else sharded
    return plan(pair_rep, *others)


def solution(mesh):
    return jax.shard_map(
        local,
        mesh=mesh,
        in_specs=(
            P(("crop", "row"), "col", None),
            P(("crop", "row"), "col", None),
            P(),
            P(),
            P(),
            P(),
            P(),
            P(),
            P(),
        ),
        out_specs=(
            P(("crop", "row"), "col", None),
            P(("crop", "row"), "col", None),
            P("crop", None),
            P("crop", None),
            P("crop", None),
        ),
        check_vma=False,
    )
```

```python
import functools

import jax
import jax.numpy as jnp
from jax import lax
from jax.experimental import pallas as pl
from jax.experimental.pallas import tpu as pltpu
from jax.sharding import PartitionSpec as P

F32 = jnp.float32
BF16 = jnp.bfloat16
VMEM_BUDGET = 24 * 2**20
SWAP = ((0, 1), (1, 0))
NATIVE = ((1,), (0,))
BY_ROWS = ((0,), (0,))
TRANSPOSED = ((1,), (1,))


def layer_norm(values, gain, bias):
    centred = values - jnp.mean(values, axis=-1, keepdims=True)
    inverse = lax.rsqrt(jnp.mean(centred * centred, axis=-1, keepdims=True) + 1e-05)
    scaled = centred * inverse
    return (scaled * gain + bias, scaled, inverse)


def norm_back(grads, gain, scaled, inverse):
    weighted = grads * gain
    first = jnp.mean(weighted, axis=-1, keepdims=True)
    second = jnp.mean(weighted * scaled, axis=-1, keepdims=True)
    return inverse * (weighted - first - scaled * second)


def sigmoid(values):
    return 0.5 * jnp.tanh(0.5 * values) + 0.5


def dot(a, b, contract=NATIVE):
    return lax.dot_general(a, b, (contract, ((), ())), preferred_element_type=F32)


def at(index, size):
    return pl.ds(pl.multiple_of(index * size, size), size)


def tile(start):
    return pl.ds(pl.multiple_of(start, 8), 8)


def parts(groups):
    distances = tuple(range(groups // 2))
    return ((0, distances), (1, distances))


def row_block(side, distance):
    me = lax.axis_index("row")
    return lax.bitwise_xor(me, 2 * distance + side)


def slots(groups):
    found = []
    for n, (side, distances) in enumerate(parts(groups)):
        found += [(n, s, row_block(side, d)) for s, d in enumerate(distances)]
    return found


def edges(blocks, params, proj_weight):
    hidden = proj_weight.shape[1] // 4
    values = jnp.concatenate([block[...] for block in blocks], axis=0).astype(F32)
    normed = layer_norm(values, params[0:1, :], params[1:2, :])[0].astype(BF16)
    projected = dot(normed, proj_weight[...])
    sides = []
    for start in (0, 2 * hidden):
        gate = sigmoid(projected[:, start : start + hidden])
        edge = gate * projected[:, start + hidden : start + 2 * hidden]
        sides.append((edge.astype(BF16).astype(F32), gate, edge * (1.0 - gate)))
    return normed, sides


def fetch_inputs_kernel(sizes, pair, cot, both, sems):
    cells = sizes[0] * sizes[1]
    copies = [
        pltpu.make_async_copy(pair, both.at[:cells], sems.at[0]),
        pltpu.make_async_copy(cot, both.at[cells:], sems.at[1]),
    ]
    for copy in copies:
        copy.start()
    for copy in copies:
        copy.wait()


def fetch_weights_kernel(sizes, *refs):
    given, (params, *held), sems = refs[:7], refs[7:11], refs[11]
    moves = [(v, params.at[n : n + 1]) for n, v in enumerate(given[:4])]
    moves += list(zip(given[4:], held, strict=True))
    copies = [pltpu.make_async_copy(a, b, sems.at[n]) for n, (a, b) in enumerate(moves)]
    for copy in copies:
        copy.start()
    for copy in copies:
        copy.wait()


def own_edges_kernel(sizes, params, weight, *refs):
    blocks, normed_out, outs = refs[:-7], refs[-7], refs[-6:]
    normed, sides = edges(blocks, params, weight)
    normed_out[...] = normed
    for out, value in zip(outs, sides[0] + sides[1], strict=True):
        out[...] = value


def mate_edges_kernel(sizes, params, weight, *refs):
    blocks, left, right = refs[:-2], refs[-2], refs[-1]
    _, sides = edges(blocks, params, weight)
    left[...] = sides[0][0]
    right[...] = sides[1][0]


def triangle_kernel(sizes, *refs):
    rows, cols, groups = sizes
    cells = rows * cols
    lefts, rights, more, tri, picked = refs[:2], refs[2:4], refs[4:-2], refs[-2], refs[-1]
    hidden = tri.shape[-1]
    half = lax.axis_index("col")
    count = cols // 8
    blocks = cols // rows
    for n, s, p in slots(groups):

        @pl.when(p // blocks == half)
        def _(n=n, s=s, p=p):
            picked[at(p - half * blocks, cells), :] = rights[n][s * cells : (s + 1) * cells, :]

    for n, s, p in slots(groups):

        def step(k, sums, n=n, s=s):
            new = list(sums)
            tiles = [picked[pl.ds(t * 8 * cols + k, 8, stride=cols), :] for t in range(count)]
            for a in range(rows):
                row = lefts[n][pl.ds((s * rows + a) * cols + k, 1), :]
                for t in range(count):
                    new[a * count + t] += row * tiles[t]
            return tuple(new)

        if more:
            first = tuple(more[0][tile(p * cells + t * 8), :] for t in range(rows * count))
        else:
            first = (jnp.zeros((8, hidden), F32),) * (rows * count)
        sums = lax.fori_loop(0, cols, step, first, unroll=8)
        for t, value in enumerate(sums):
            tri[tile(p * cells + t * 8), :] = value


def cells_kernel(
    sizes,
    params,
    tri,
    gate_weight,
    out_weight,
    *refs,
):
    rows, cols, groups = sizes
    cells = rows * cols
    normed, cots, (block_out, d_tri, d_gate, tri_norm_out, d_update_out) = (
        refs[:2],
        refs[2:6],
        refs[6:],
    )
    gain, bias = params[2:3, :], params[3:4, :]
    every = slots(groups)
    for first in range(0, groups, 4):
        chunk = every[first : first + 4]
        places = [at(p, cells) for _, _, p in chunk]
        here = jnp.concatenate([tri[place, :] for place in places], axis=0)
        tri_f, hat, inverse = layer_norm(here, gain, bias)
        tri_norm = tri_f.astype(BF16)
        update = dot(tri_norm, out_weight[...])
        n, s, _ = chunk[0]
        out_gate = sigmoid(dot(normed[n][s * cells : (s + 4) * cells, :], gate_weight[...]))
        if first == 0:
            block_out[...] = (out_gate[:cells] * update[:cells]).astype(BF16)
        cot = jnp.concatenate([cots[2 * n + min(s, 1)][max(s - 1, 0) * cells : max(s, 1) * cells, :] for n, s, _ in chunk], axis=0)
        gated = cot.astype(F32) * out_gate
        d_update = gated.astype(BF16)
        d_gates = (gated * update * (1.0 - out_gate)).astype(BF16)
        d_norm = dot(d_update, out_weight[...], TRANSPOSED)
        d_tris = norm_back(d_norm, gain, hat, inverse).astype(BF16)
        for t, place in enumerate(places):
            part = slice(t * cells, (t + 1) * cells)
            d_gate[place, :] = d_gates[part]
            d_tri[place, :] = d_tris[part]
            tri_norm_out[place, :] = tri_norm[part]
            d_update_out[place, :] = d_update[part]


def contract(rows, cols, count, unroll, start, source, row_at, operand, operand_at):
    tiles = cols // 8

    def step(term, sums):
        new = list(sums)
        loaded = [operand[tile(operand_at(term) + t * 8), :] for t in range(tiles)]
        for a in range(rows):
            row = source[pl.ds(row_at(a, term), 1), :]
            for t in range(tiles):
                new[a * tiles + t] += row * loaded[t]
        return tuple(new)

    return lax.fori_loop(0, count, step, start, unroll=unroll)


def early_kernel(
    sizes,
    d_tri_ref,
    d_gate,
    tri_norm,
    d_update,
    *refs,
):
    rows, cols, groups = sizes
    left, right, normed, d_left, d_right, small_grads, source = refs[6:]
    cells = rows * cols
    hidden = left.shape[-1]
    channels = normed.shape[-1]
    half = lax.axis_index("col")
    zeros = (jnp.zeros((8, hidden), F32),) * (rows * cols // 8)
    source[...] = d_tri_ref[...].astype(F32)
    for n, s, p in slots(groups):
        place, part = at(p, cells), slice(s * cells, (s + 1) * cells)
        normed[place, :] = refs[n][part, :]
        left[place, :] = refs[2 + n][part, :]
        right[place, :] = refs[4 + n][part, :]

    def left_block(p, carry):
        sums = contract(
            rows,
            cols,
            cols,
            8,
            zeros,
            source,
            lambda a, j: (p * rows + a) * cols + j,
            right,
            lambda j: (half * cols + j) * cols,
        )
        for t, value in enumerate(sums):
            d_left[tile(p * cells + t * 8), :] = value
        return carry

    lax.fori_loop(0, groups, left_block, 0)

    def right_block(p, carry):
        sums = contract(
            rows,
            cols,
            rows * groups,
            8,
            zeros,
            source,
            lambda a, i: i * cols + p * rows + a,
            left,
            lambda i: i * cols,
        )
        for t, value in enumerate(sums):
            d_right[tile(p * cells + t * 8), :] = value
        return carry

    lax.fori_loop(0, cols // rows, right_block, 0)
    scale = 1.0 / (rows * groups)
    small_grads[:, :channels] = dot(normed[...], d_gate[...], BY_ROWS) * scale
    small_grads[:, channels:] = dot(tri_norm[...], d_update[...], BY_ROWS) * scale


def late_kernel(
    sizes,
    d_tri_ref,
    left,
    right,
    normed,
    d_left,
    d_right,
    *refs,
):
    rows, cols, groups = sizes
    left_gate, left_value, right_gate, right_value = refs[:2], refs[2:4], refs[4:6], refs[6:8]
    proj_grad, d_proj, source, d_right_s = refs[8:]
    cells = rows * cols
    hidden = left.shape[-1]
    half = lax.axis_index("col")
    zeros = (jnp.zeros((8, hidden), F32),) * (rows * cols // 8)
    source[...] = d_tri_ref[...].astype(F32)
    d_right_s[at(half, cols * cols), :] = d_right[...]

    def right_block(p, carry):
        sums = contract(
            rows,
            cols,
            rows * groups,
            8,
            zeros,
            source,
            lambda a, i: i * cols + p * rows + a,
            left,
            lambda i: i * cols,
        )
        start = (1 - half) * cols * cols + p * cells
        for t, value in enumerate(sums):
            d_right_s[tile(start + t * 8), :] = value
        return carry

    lax.fori_loop(0, cols // rows, right_block, 0)

    for n, s, p in slots(groups):
        start = p * cells
        sums = contract(
            rows,
            cols,
            cols,
            8,
            tuple(d_left[tile(start + t * 8), :] for t in range(cells // 8)),
            source,
            lambda a, j, p=p: (p * rows + a) * cols + j,
            right,
            lambda j: ((1 - half) * cols + j) * cols,
        )
        part, place = slice(s * cells, (s + 1) * cells), at(p, cells)
        grads = jnp.concatenate(sums, axis=0)
        d_proj[place, :hidden] = (grads * left_value[n][part, :]).astype(BF16)
        d_proj[place, hidden : 2 * hidden] = (grads * left_gate[n][part, :]).astype(BF16)
        grads = d_right_s[place, :]
        d_proj[place, 2 * hidden : 3 * hidden] = (grads * right_value[n][part, :]).astype(BF16)
        d_proj[place, 3 * hidden :] = (grads * right_gate[n][part, :]).astype(BF16)

    scale = 1.0 / (rows * groups)
    proj_grad[...] = dot(normed[...], d_proj[...], BY_ROWS) * scale


def outputs_kernel(
    sizes,
    params,
    pair,
    d_proj,
    d_gate,
    proj_weight,
    gate_weight,
    block_in,
    small_own,
    small_mate,
    block_out,
    pair_grad,
    gate_grad,
    out_grad,
):
    rows, cols, _ = sizes
    cells = rows * cols
    own = at(lax.axis_index("row"), cells)
    d_normed = dot(d_proj[own, :], proj_weight[...], TRANSPOSED) + dot(
        d_gate[own, :], gate_weight[...], TRANSPOSED
    )
    gain = params[0:1, :]
    _, hat, inverse = layer_norm(pair[...].astype(F32), gain, params[1:2, :])
    pair_grad[...] = norm_back(d_normed, gain, hat, inverse)
    block_out[...] = block_in[...]
    channels = gate_grad.shape[1]
    small = small_own[...] + small_mate[...]
    gate_grad[...] = small[:, :channels]
    out_grad[...] = small[:, channels:]


def replicated(
    pair_rep,
    cotangent,
    norm_gain,
    norm_bias,
    proj_weight,
    gate_weight,
    tri_gain,
    tri_bias,
    out_weight,
):
    rows, cols, channels = pair_rep.shape
    hidden = tri_gain.shape[0]
    groups = lax.axis_size("row")
    cells = rows * cols
    every = cells * groups
    sizes = (rows, cols, groups)

    def call(kernel, outs, *args, scratch=(), micros=1, name, **more):
        cost = pl.CostEstimate(flops=micros * 10**9, bytes_accessed=0, transcendentals=0)
        return pl.pallas_call(
            functools.partial(kernel, sizes),
            out_shape=[jax.ShapeDtypeStruct(*out) for out in outs],
            scratch_shapes=[pltpu.VMEM(*one) if isinstance(one, tuple) else one for one in scratch],
            **more,
            compiler_params=pltpu.CompilerParams(vmem_limit_bytes=VMEM_BUDGET),
            cost_estimate=cost,
            name=name,
        )(*args)

    def across(value, mask):
        return lax.ppermute(value, "row", [(i, i ^ mask) for i in range(groups)])

    def over(value):
        return lax.ppermute(value, "col", SWAP)

    def along(value):
        got = []
        for distance in reversed(range(1, groups // 2)):
            arrived = across(value, 2 * distance)
            got.append(after(arrived, got[-1]) if got else arrived)
        return got[::-1]

    def join(*values):
        return jnp.concatenate(values, axis=0)

    def after(value, *others):
        return lax.optimization_barrier((value, *others))[0]

    full = (every, hidden)

    def own_edges(*blocks):
        count = sum(block.shape[0] for block in blocks)
        outs = [((count, channels), BF16)] + [((count, hidden), F32)] * 6
        return call(own_edges_kernel, outs, params, proj_weight, *blocks, name="own_edges")

    def mate_edges(*blocks):
        outs = [((sum(block.shape[0] for block in blocks), hidden), F32)] * 2
        return call(mate_edges_kernel, outs, params, proj_weight, *blocks, name="mate_edges")

    def fetch(kernel, outs, given, name):
        given = [pltpu.with_memory_space_constraint(v, pltpu.HBM) for v in given]
        return call(
            kernel,
            outs,
            *given,
            scratch=[pltpu.SemaphoreType.DMA((len(given),))],
            in_specs=[pl.BlockSpec(memory_space=pltpu.HBM)] * len(given),
            name=name,
        )

    given = [pair_rep.reshape(cells, channels), cotangent.reshape(cells, channels)]
    (both,) = fetch(fetch_inputs_kernel, [((2 * cells, channels), BF16)], given, "fetch_inputs")
    got = along(both)
    given = [v[None] for v in (norm_gain, norm_bias, tri_gain, tri_bias)]
    given += [proj_weight, gate_weight, out_weight]
    outs = [((4, channels), F32)] + [(a.shape, BF16) for a in given[4:]]
    held = fetch(fetch_weights_kernel, outs, given, "fetch_weights")
    params, proj_weight, gate_weight, out_weight = held
    both_far = across(both, 1)
    near_b = after(join(*(block[:cells] for block in got)), params)
    far_b = across(near_b, 1)
    cot_b = join(*(block[cells:] for block in got))
    cot_far_b = across(cot_b, 1)
    pair, pair_far = both[:cells], both_far[:cells]
    mate_near = over(join(pair, near_b))
    cots = (both[cells:], cot_b, both_far[cells:], cot_far_b)
    own_0 = own_edges(pair, near_b)
    mate_0 = mate_edges(mate_near)
    far_all = join(pair_far, after(far_b, mate_0[0]))
    own_1 = own_edges(far_all)
    mate_1 = mate_edges(over(far_all))
    own, mate = (own_0, own_1), (mate_0, mate_1)
    normed = [o[0] for o in own]
    left, left_gate, left_value = ([o[n] for o in own] for n in (1, 2, 3))
    right, right_gate, right_value = ([o[n] for o in own] for n in (4, 5, 6))
    def triangle(lefts, rights, *more):
        outs, scratch = [(full, F32)], [((cols * cols, hidden), F32)]
        args = (*lefts, *rights, *more)
        return call(triangle_kernel, outs, *args, scratch=scratch, name="triangle")

    tri = triangle(left, right)
    (tri,) = triangle([m[0] for m in mate], [m[1] for m in mate], *tri)
    block_out, d_tri, d_gate, tri_norm, d_update = call(
        cells_kernel,
        [((cells, channels), BF16)] + [(full, BF16)] * 4,
        params,
        tri,
        gate_weight,
        out_weight,
        *normed,
        *cots,
        micros=2,
        name="cells",
    )
    d_tri_mate = over(d_tri)
    left_all, right_all, normed_all, d_left, d_right, small_grads = call(
        early_kernel,
        [
            (full, F32),
            (full, F32),
            ((every, channels), BF16),
            (full, F32),
            ((cols * cols, hidden), F32),
            ((channels, 2 * channels), F32),
        ],
        d_tri,
        d_gate,
        tri_norm,
        d_update,
        *normed,
        *left,
        *right,
        scratch=[(full, F32)],
        micros=30,
        name="early",
    )
    small_mate = over(small_grads)
    proj_grad, d_proj = call(
        late_kernel,
        [((channels, 4 * hidden), F32), ((every, 4 * hidden), BF16)],
        d_tri_mate,
        left_all,
        right_all,
        normed_all,
        d_left,
        d_right,
        *left_gate,
        *left_value,
        *right_gate,
        *right_value,
        scratch=[(full, F32), (full, F32)],
        micros=40,
        name="late",
    )
    proj_mate = over(proj_grad)
    square = ((channels, channels), F32)
    block_out, pair_grad, gate_grad, out_grad = call(
        outputs_kernel,
        [((cells, channels), BF16), ((cells, channels), F32), square, square],
        params,
        pair,
        d_proj,
        d_gate,
        proj_weight,
        gate_weight,
        block_out,
        small_grads,
        small_mate,
        micros=10,
        name="outputs",
    )
    return (
        block_out.reshape(pair_rep.shape),
        pair_grad.reshape(pair_rep.shape),
        proj_grad + proj_mate,
        gate_grad,
        out_grad,
    )


def sharded(
    pair_rep,
    cotangent,
    norm_gain,
    norm_bias,
    proj_weight,
    gate_weight,
    tri_gain,
    tri_bias,
    out_weight,
):
    f32 = jnp.float32
    bf16 = jnp.bfloat16
    hidden = tri_gain.shape[0]
    channels = norm_gain.shape[0]
    row_count = pair_rep.shape[0]
    col_count = pair_rep.shape[1]
    crop_len = row_count * lax.axis_size("row")
    normed_f, pair_hat, pair_inv = layer_norm(pair_rep.astype(f32), norm_gain, norm_bias)
    normed = normed_f.astype(bf16)
    projected = jnp.einsum("ijc,cd->ijd", normed, proj_weight, preferred_element_type=f32)
    sig_left = jax.nn.sigmoid(projected[..., 0:hidden])
    val_left = projected[..., hidden : 2 * hidden]
    sig_right = jax.nn.sigmoid(projected[..., 2 * hidden : 3 * hidden])
    val_right = projected[..., 3 * hidden : 4 * hidden]
    left_edge = (sig_left * val_left).astype(bf16)
    right_edge = (sig_right * val_right).astype(bf16)
    out_gate = jax.nn.sigmoid(
        jnp.einsum("ijc,cd->ijd", normed, gate_weight, preferred_element_type=f32)
    )
    right_all = lax.all_gather(right_edge, "row", axis=0, tiled=True)
    block = right_all
    triangle = lax.psum_scatter(
        jnp.einsum("ikc,jkc->jic", left_edge, block, preferred_element_type=f32),
        "col",
        scatter_dimension=0,
        tiled=True,
    ).transpose(1, 0, 2)
    tri_f, tri_hat, tri_inv = layer_norm(triangle, tri_gain, tri_bias)
    tri_norm = tri_f.astype(bf16)
    update = jnp.einsum("ijh,hc->ijc", tri_norm, out_weight, preferred_element_type=f32)
    block_out = (out_gate * update).astype(bf16)
    cot = cotangent.astype(f32)
    d_update = (cot * out_gate).astype(bf16)
    d_gate = (cot * update * out_gate * (1.0 - out_gate)).astype(bf16)
    d_norm = jnp.einsum("ijc,hc->ijh", d_update, out_weight, preferred_element_type=f32)
    d_triangle = norm_back(d_norm, tri_gain, tri_hat, tri_inv).astype(bf16)
    tri_rows = lax.all_gather(d_triangle, "col", axis=1, tiled=True)
    d_left = jnp.einsum("ijc,jkc->ikc", tri_rows, right_all, preferred_element_type=f32)
    tri_cols = lax.all_to_all(tri_rows, "row", split_axis=1, concat_axis=0, tiled=True)
    block = tri_cols
    d_right = jnp.einsum(
        "ijc,ikc->jkc",
        block,
        lax.all_gather(left_edge, "row", axis=0, tiled=True),
        preferred_element_type=f32,
    )
    d_proj = jnp.concatenate(
        [
            d_left * val_left * sig_left * (1.0 - sig_left),
            d_left * sig_left,
            d_right * val_right * sig_right * (1.0 - sig_right),
            d_right * sig_right,
        ],
        axis=-1,
    ).astype(bf16)
    d_normed = jnp.einsum(
        "ijd,cd->ijc", d_proj, proj_weight, preferred_element_type=f32
    ) + jnp.einsum("ijd,cd->ijc", d_gate, gate_weight, preferred_element_type=f32)
    pair_grad = norm_back(d_normed, norm_gain, pair_hat, pair_inv)
    cells = row_count * col_count
    flat_norm = normed.reshape(cells, channels)
    local_proj = (
        jnp.dot(flat_norm.T, d_proj.reshape(cells, 4 * hidden), preferred_element_type=f32)
        / crop_len
    )
    local_gate = (
        jnp.dot(flat_norm.T, d_gate.reshape(cells, channels), preferred_element_type=f32) / crop_len
    )
    local_out = (
        jnp.dot(
            tri_norm.reshape(cells, hidden).T,
            d_update.reshape(cells, channels),
            preferred_element_type=f32,
        )
        / crop_len
    )
    proj_grad, gate_grad, out_grad = lax.psum((local_proj, local_gate, local_out), ("row", "col"))
    return (block_out, pair_grad, proj_grad, gate_grad, out_grad)


def local(pair_rep, *others):
    rows, cols, channels = pair_rep.shape
    hidden = others[7].shape[0]
    groups = lax.axis_size("row")
    every = rows * groups * cols
    fits = 24 * every * channels * 4 <= VMEM_BUDGET and hidden == channels
    paired = lax.axis_size("col") == 2 and groups & (groups - 1) == 0 and groups >= 8
    whole_tiles = cols % 8 == 0 and cols % (2 * rows) == 0 and rows * cols % 16 == 0
    plan = replicated if fits and paired and whole_tiles else sharded
    return plan(pair_rep, *others)


def solution(mesh):
    return jax.shard_map(
        local,
        mesh=mesh,
        in_specs=(
            P(("crop", "row"), "col", None),
            P(("crop", "row"), "col", None),
            P(),
            P(),
            P(),
            P(),
            P(),
            P(),
            P(),
        ),
        out_specs=(
            P(("crop", "row"), "col", None),
            P(("crop", "row"), "col", None),
            P("crop", None),
            P("crop", None),
            P("crop", None),
        ),
        check_vma=False,
    )
```

```python
import functools

import jax
import jax.numpy as jnp
from jax import lax
from jax.experimental import pallas as pl
from jax.experimental.pallas import tpu as pltpu
from jax.sharding import PartitionSpec as P

F32 = jnp.float32
BF16 = jnp.bfloat16
VMEM_BUDGET = 24 * 2**20
SWAP = ((0, 1), (1, 0))
NATIVE = ((1,), (0,))
BY_ROWS = ((0,), (0,))
TRANSPOSED = ((1,), (1,))


def layer_norm(values, gain, bias):
    centred = values - jnp.mean(values, axis=-1, keepdims=True)
    inverse = lax.rsqrt(jnp.mean(centred * centred, axis=-1, keepdims=True) + 1e-05)
    scaled = centred * inverse
    return (scaled * gain + bias, scaled, inverse)


def norm_back(grads, gain, scaled, inverse):
    weighted = grads * gain
    first = jnp.mean(weighted, axis=-1, keepdims=True)
    second = jnp.mean(weighted * scaled, axis=-1, keepdims=True)
    return inverse * (weighted - first - scaled * second)


def sigmoid(values):
    return 0.5 * jnp.tanh(0.5 * values) + 0.5


def dot(a, b, contract=NATIVE):
    return lax.dot_general(a, b, (contract, ((), ())), preferred_element_type=F32)


def at(index, size):
    return pl.ds(pl.multiple_of(index * size, size), size)


def tile(start):
    return pl.ds(pl.multiple_of(start, 8), 8)


def parts(groups):
    distances = tuple(range(groups // 2))
    return ((0, distances), (1, distances))


def row_block(side, distance):
    me = lax.axis_index("row")
    return lax.bitwise_xor(me, 2 * distance + side)


def slots(groups):
    found = []
    for n, (side, distances) in enumerate(parts(groups)):
        found += [(n, s, row_block(side, d)) for s, d in enumerate(distances)]
    return found


def edges(blocks, params, proj_weight):
    hidden = proj_weight.shape[1] // 4
    values = jnp.concatenate([block[...] for block in blocks], axis=0).astype(F32)
    normed = layer_norm(values, params[0:1, :], params[1:2, :])[0].astype(BF16)
    projected = dot(normed, proj_weight[...])
    sides = []
    for start in (0, 2 * hidden):
        gate = sigmoid(projected[:, start : start + hidden])
        edge = gate * projected[:, start + hidden : start + 2 * hidden]
        sides.append((edge.astype(BF16).astype(F32), gate, edge * (1.0 - gate)))
    return normed, sides


def fetch_inputs_kernel(sizes, pair, cot, both, sems):
    cells = sizes[0] * sizes[1]
    copies = [
        pltpu.make_async_copy(pair, both.at[:cells], sems.at[0]),
        pltpu.make_async_copy(cot, both.at[cells:], sems.at[1]),
    ]
    for copy in copies:
        copy.start()
    for copy in copies:
        copy.wait()


def fetch_weights_kernel(sizes, *refs):
    given, (params, *held), sems = refs[:7], refs[7:11], refs[11]
    moves = [(v, params.at[n : n + 1]) for n, v in enumerate(given[:4])]
    moves += list(zip(given[4:], held, strict=True))
    copies = [pltpu.make_async_copy(a, b, sems.at[n]) for n, (a, b) in enumerate(moves)]
    for copy in copies:
        copy.start()
    for copy in copies:
        copy.wait()


def own_edges_kernel(sizes, params, weight, *refs):
    blocks, sent, normed_out, outs = refs[:-8], refs[-8], refs[-7], refs[-6:]
    normed, sides = edges(blocks, params, weight)
    normed_out[...] = normed
    count = normed.shape[0]
    sent[:count, :] = sides[0][0].astype(BF16)
    sent[count:, :] = sides[1][0].astype(BF16)
    for out, value in zip(outs, sides[0] + sides[1], strict=True):
        out[...] = value


def triangle_half(sizes, lefts, right_of, more, tri, picked):
    rows, cols, groups = sizes
    cells = rows * cols
    hidden = tri.shape[-1]
    half = lax.axis_index("col")
    count = cols // 8
    blocks = cols // rows
    for n, s, p in slots(groups):

        @pl.when(p // blocks == half)
        def _(n=n, s=s, p=p):
            picked[at(p - half * blocks, cells), :] = right_of(n, slice(s * cells, (s + 1) * cells))

    for n, s, p in slots(groups):

        if more is None:
            first = (jnp.zeros((8, hidden), F32),) * (rows * count)
        else:
            first = tuple(more[tile(p * cells + t * 8), :] for t in range(rows * count))
        sums = list(first)
        for k in range(cols):
            tiles = [picked[pl.ds(t * 8 * cols + k, 8, stride=cols), :] for t in range(count)]
            for a in range(rows):
                row = lefts[n][pl.ds((s * rows + a) * cols + k, 1), :]
                for t in range(count):
                    sums[a * count + t] += row * tiles[t]
        for t, value in enumerate(sums):
            tri[tile(p * cells + t * 8), :] = value


def own_triangle_kernel(sizes, left_0, left_1, right_0, right_1, tri, picked):
    rights = (right_0, right_1)
    triangle_half(
        sizes, (left_0, left_1), lambda n, part: rights[n][part, :], None, tri, picked
    )


def mate_triangle_kernel(sizes, edges_0, edges_1, more, tri, picked, left_0, left_1):
    got = (edges_0, edges_1)
    lefts = (left_0, left_1)
    count = left_0.shape[0]
    for edge, left in zip(got, lefts, strict=True):
        left[...] = edge[:count, :].astype(F32)

    def right_of(n, part):
        return got[n][count + part.start : count + part.stop, :].astype(F32)

    triangle_half(sizes, lefts, right_of, more, tri, picked)


def cells_kernel(
    sizes,
    params,
    tri,
    gate_weight,
    out_weight,
    *refs,
):
    rows, cols, groups = sizes
    cells = rows * cols
    normed, cots, (block_out, d_tri, d_gate, tri_norm_out, d_update_out) = (
        refs[:2],
        refs[2:6],
        refs[6:],
    )
    gain, bias = params[2:3, :], params[3:4, :]
    every = slots(groups)
    for first in range(0, groups, 4):
        chunk = every[first : first + 4]
        places = [at(p, cells) for _, _, p in chunk]
        here = jnp.concatenate([tri[place, :] for place in places], axis=0)
        tri_f, hat, inverse = layer_norm(here, gain, bias)
        tri_norm = tri_f.astype(BF16)
        update = dot(tri_norm, out_weight[...])
        n, s, _ = chunk[0]
        out_gate = sigmoid(dot(normed[n][s * cells : (s + 4) * cells, :], gate_weight[...]))
        if first == 0:
            block_out[...] = (out_gate[:cells] * update[:cells]).astype(BF16)
        cot = jnp.concatenate([cots[2 * n + min(s, 1)][max(s - 1, 0) * cells : max(s, 1) * cells, :] for n, s, _ in chunk], axis=0)
        gated = cot.astype(F32) * out_gate
        d_update = gated.astype(BF16)
        d_gates = (gated * update * (1.0 - out_gate)).astype(BF16)
        d_norm = dot(d_update, out_weight[...], TRANSPOSED)
        d_tris = norm_back(d_norm, gain, hat, inverse).astype(BF16)
        for t, place in enumerate(places):
            part = slice(t * cells, (t + 1) * cells)
            d_gate[place, :] = d_gates[part]
            d_tri[place, :] = d_tris[part]
            tri_norm_out[place, :] = tri_norm[part]
            d_update_out[place, :] = d_update[part]


def contract(rows, cols, count, unroll, start, source, row_at, operand, operand_at):
    tiles = cols // 8

    def step(term, sums):
        new = list(sums)
        loaded = [operand[tile(operand_at(term) + t * 8), :] for t in range(tiles)]
        for a in range(rows):
            row = source[pl.ds(row_at(a, term), 1), :]
            for t in range(tiles):
                new[a * tiles + t] += row * loaded[t]
        return tuple(new)

    return lax.fori_loop(0, count, step, start, unroll=unroll)


def contract_all(rows, cols, count, start, source, row_at, operand, operand_at):
    tiles = cols // 8
    sums = list(start)
    for term in range(count):
        loaded = [operand[tile(operand_at(term) + t * 8), :] for t in range(tiles)]
        for a in range(rows):
            row = source[pl.ds(row_at(a, term), 1), :]
            for t in range(tiles):
                sums[a * tiles + t] += row * loaded[t]
    return sums


def early_kernel(
    sizes,
    d_tri_ref,
    d_gate,
    tri_norm,
    d_update,
    *refs,
):
    rows, cols, groups = sizes
    left, right, normed, d_left, d_right, small_grads, source = refs[6:]
    cells = rows * cols
    hidden = left.shape[-1]
    channels = normed.shape[-1]
    half = lax.axis_index("col")
    zeros = (jnp.zeros((8, hidden), F32),) * (rows * cols // 8)
    source[...] = d_tri_ref[...].astype(F32)
    for n, s, p in slots(groups):
        place, part = at(p, cells), slice(s * cells, (s + 1) * cells)
        normed[place, :] = refs[n][part, :]
        left[place, :] = refs[2 + n][part, :]
        right[place, :] = refs[4 + n][part, :]

    scale = 1.0 / (rows * groups)
    small_grads[:, :channels] = dot(normed[...], d_gate[...], BY_ROWS) * scale
    small_grads[:, channels:] = dot(tri_norm[...], d_update[...], BY_ROWS) * scale
    for p in range(groups):
        sums = contract_all(
            rows,
            cols,
            cols,
            zeros,
            source,
            lambda a, j, p=p: (p * rows + a) * cols + j,
            right,
            lambda j: (half * cols + j) * cols,
        )
        for t, value in enumerate(sums):
            d_left[tile(p * cells + t * 8), :] = value

    for p in range(cols // rows):
        sums = contract_all(
            rows,
            cols,
            rows * groups,
            zeros,
            source,
            lambda a, i, p=p: i * cols + p * rows + a,
            left,
            lambda i: i * cols,
        )
        for t, value in enumerate(sums):
            d_right[tile(p * cells + t * 8), :] = value


def late_kernel(
    sizes,
    d_tri_ref,
    left,
    right,
    normed,
    d_left,
    d_right,
    *refs,
):
    rows, cols, groups = sizes
    left_gate, left_value, right_gate, right_value = refs[:2], refs[2:4], refs[4:6], refs[6:8]
    proj_grad, d_proj, source, d_right_s = refs[8:]
    cells = rows * cols
    hidden = left.shape[-1]
    half = lax.axis_index("col")
    zeros = (jnp.zeros((8, hidden), F32),) * (rows * cols // 8)
    source[...] = d_tri_ref[...].astype(F32)
    d_right_s[at(half, cols * cols), :] = d_right[...]

    def right_block(p, carry):
        sums = contract(
            rows,
            cols,
            rows * groups,
            8,
            zeros,
            source,
            lambda a, i: i * cols + p * rows + a,
            left,
            lambda i: i * cols,
        )
        start = (1 - half) * cols * cols + p * cells
        for t, value in enumerate(sums):
            d_right_s[tile(start + t * 8), :] = value
        return carry

    lax.fori_loop(0, cols // rows, right_block, 0)

    scale = 1.0 / (rows * groups)
    for n, s, p in slots(groups):
        part, place = slice(s * cells, (s + 1) * cells), at(p, cells)
        grads = d_right_s[place, :]
        d_proj[place, 2 * hidden : 3 * hidden] = (grads * right_value[n][part, :]).astype(BF16)
        d_proj[place, 3 * hidden :] = (grads * right_gate[n][part, :]).astype(BF16)
    proj_grad[:, 2 * hidden :] = dot(normed[...], d_proj[:, 2 * hidden :], BY_ROWS) * scale
    for n, s, p in slots(groups):
        start = p * cells
        sums = contract_all(
            rows,
            cols,
            cols,
            [d_left[tile(start + t * 8), :] for t in range(cells // 8)],
            source,
            lambda a, j, p=p: (p * rows + a) * cols + j,
            right,
            lambda j: ((1 - half) * cols + j) * cols,
        )
        part, place = slice(s * cells, (s + 1) * cells), at(p, cells)
        grads = jnp.concatenate(sums, axis=0)
        d_proj[place, :hidden] = (grads * left_value[n][part, :]).astype(BF16)
        d_proj[place, hidden : 2 * hidden] = (grads * left_gate[n][part, :]).astype(BF16)
    proj_grad[:, : 2 * hidden] = dot(normed[...], d_proj[:, : 2 * hidden], BY_ROWS) * scale


def outputs_kernel(
    sizes,
    params,
    pair,
    d_proj,
    d_gate,
    proj_weight,
    gate_weight,
    block_in,
    small_own,
    small_mate,
    block_out,
    pair_grad,
    gate_grad,
    out_grad,
):
    rows, cols, _ = sizes
    cells = rows * cols
    own = at(lax.axis_index("row"), cells)
    d_normed = dot(d_proj[own, :], proj_weight[...], TRANSPOSED) + dot(
        d_gate[own, :], gate_weight[...], TRANSPOSED
    )
    gain = params[0:1, :]
    _, hat, inverse = layer_norm(pair[...].astype(F32), gain, params[1:2, :])
    pair_grad[...] = norm_back(d_normed, gain, hat, inverse)
    block_out[...] = block_in[...]
    channels = gate_grad.shape[1]
    small = small_own[...] + small_mate[...]
    gate_grad[...] = small[:, :channels]
    out_grad[...] = small[:, channels:]


def replicated(
    pair_rep,
    cotangent,
    norm_gain,
    norm_bias,
    proj_weight,
    gate_weight,
    tri_gain,
    tri_bias,
    out_weight,
):
    rows, cols, channels = pair_rep.shape
    hidden = tri_gain.shape[0]
    groups = lax.axis_size("row")
    cells = rows * cols
    every = cells * groups
    sizes = (rows, cols, groups)

    def call(kernel, outs, *args, scratch=(), micros=1, name, **more):
        cost = pl.CostEstimate(flops=micros * 10**9, bytes_accessed=0, transcendentals=0)
        return pl.pallas_call(
            functools.partial(kernel, sizes),
            out_shape=[jax.ShapeDtypeStruct(*out) for out in outs],
            scratch_shapes=[pltpu.VMEM(*one) if isinstance(one, tuple) else one for one in scratch],
            **more,
            compiler_params=pltpu.CompilerParams(vmem_limit_bytes=VMEM_BUDGET),
            cost_estimate=cost,
            name=name,
        )(*args)

    def across(value, mask):
        return lax.ppermute(value, "row", [(i, i ^ mask) for i in range(groups)])

    def over(value):
        return lax.ppermute(value, "col", SWAP)

    def along(value):
        got = []
        for distance in reversed(range(1, groups // 2)):
            arrived = across(value, 2 * distance)
            got.append(after(arrived, got[-1]) if got else arrived)
        return got[::-1]

    def join(*values):
        return jnp.concatenate(values, axis=0)

    def after(value, *others):
        return lax.optimization_barrier((value, *others))[0]

    full = (every, hidden)

    def own_edges(*blocks):
        count = sum(block.shape[0] for block in blocks)
        outs = [((2 * count, hidden), BF16), ((count, channels), BF16)]
        outs += [((count, hidden), F32)] * 6
        return call(own_edges_kernel, outs, params, proj_weight, *blocks, micros=10, name="own_edges")

    def fetch(kernel, outs, given, name):
        given = [pltpu.with_memory_space_constraint(v, pltpu.HBM) for v in given]
        return call(
            kernel,
            outs,
            *given,
            scratch=[pltpu.SemaphoreType.DMA((len(given),))],
            in_specs=[pl.BlockSpec(memory_space=pltpu.HBM)] * len(given),
            name=name,
        )

    given = [pair_rep.reshape(cells, channels), cotangent.reshape(cells, channels)]
    (both,) = fetch(fetch_inputs_kernel, [((2 * cells, channels), BF16)], given, "fetch_inputs")
    got = along(both)
    given = [v[None] for v in (norm_gain, norm_bias, tri_gain, tri_bias)]
    given += [proj_weight, gate_weight, out_weight]
    outs = [((4, channels), F32)] + [(a.shape, BF16) for a in given[4:]]
    held = fetch(fetch_weights_kernel, outs, given, "fetch_weights")
    params, proj_weight, gate_weight, out_weight = held
    both_far = across(both, 1)
    near_b = after(join(*(block[:cells] for block in got)), params)
    far_b = across(near_b, 1)
    cot_b = join(*(block[cells:] for block in got))
    pair, pair_far = both[:cells], both_far[:cells]
    own_0 = own_edges(pair, near_b)
    mate_0 = over(own_0[0])
    cot_far_b = across(after(cot_b, own_0[0]), 1)
    cots = (both[cells:], cot_b, both_far[cells:], cot_far_b)
    own_1 = own_edges(pair_far, far_b)
    mate_1 = over(own_1[0])
    own = [o[1:] for o in (own_0, own_1)]
    normed = [o[0] for o in own]
    left, left_gate, left_value = ([o[n] for o in own] for n in (1, 2, 3))
    right, right_gate, right_value = ([o[n] for o in own] for n in (4, 5, 6))
    outs, picked, half_left = [(full, F32)], ((cols * cols, hidden), F32), ((every // 2, hidden), F32)
    tri = call(own_triangle_kernel, outs, *left, *right, scratch=[picked], micros=10, name="own_triangle")
    scratch = [picked, half_left, half_left]

    args = (mate_0, mate_1, *tri)
    (tri,) = call(mate_triangle_kernel, outs, *args, scratch=scratch, name="mate_triangle")
    block_out, d_tri, d_gate, tri_norm, d_update = call(
        cells_kernel,
        [((cells, channels), BF16)] + [(full, BF16)] * 4,
        params,
        tri,
        gate_weight,
        out_weight,
        *normed,
        *cots,
        micros=2,
        name="cells",
    )
    d_tri_mate = over(d_tri)
    left_all, right_all, normed_all, d_left, d_right, small_grads = call(
        early_kernel,
        [
            (full, F32),
            (full, F32),
            ((every, channels), BF16),
            (full, F32),
            ((cols * cols, hidden), F32),
            ((channels, 2 * channels), F32),
        ],
        d_tri,
        d_gate,
        tri_norm,
        d_update,
        *normed,
        *left,
        *right,
        scratch=[(full, F32)],
        micros=30,
        name="early",
    )
    small_mate = over(small_grads)
    proj_grad, d_proj = call(
        late_kernel,
        [((channels, 4 * hidden), F32), ((every, 4 * hidden), BF16)],
        d_tri_mate,
        left_all,
        right_all,
        normed_all,
        d_left,
        d_right,
        *left_gate,
        *left_value,
        *right_gate,
        *right_value,
        scratch=[(full, F32), (full, F32)],
        micros=40,
        name="late",
    )
    proj_mate = over(proj_grad)
    square = ((channels, channels), F32)
    block_out, pair_grad, gate_grad, out_grad = call(
        outputs_kernel,
        [((cells, channels), BF16), ((cells, channels), F32), square, square],
        params,
        pair,
        d_proj,
        d_gate,
        proj_weight,
        gate_weight,
        block_out,
        small_grads,
        small_mate,
        micros=10,
        name="outputs",
    )
    return (
        block_out.reshape(pair_rep.shape),
        pair_grad.reshape(pair_rep.shape),
        proj_grad + proj_mate,
        gate_grad,
        out_grad,
    )


def sharded(
    pair_rep,
    cotangent,
    norm_gain,
    norm_bias,
    proj_weight,
    gate_weight,
    tri_gain,
    tri_bias,
    out_weight,
):
    f32 = jnp.float32
    bf16 = jnp.bfloat16
    hidden = tri_gain.shape[0]
    channels = norm_gain.shape[0]
    row_count = pair_rep.shape[0]
    col_count = pair_rep.shape[1]
    crop_len = row_count * lax.axis_size("row")
    normed_f, pair_hat, pair_inv = layer_norm(pair_rep.astype(f32), norm_gain, norm_bias)
    normed = normed_f.astype(bf16)
    projected = jnp.einsum("ijc,cd->ijd", normed, proj_weight, preferred_element_type=f32)
    sig_left = jax.nn.sigmoid(projected[..., 0:hidden])
    val_left = projected[..., hidden : 2 * hidden]
    sig_right = jax.nn.sigmoid(projected[..., 2 * hidden : 3 * hidden])
    val_right = projected[..., 3 * hidden : 4 * hidden]
    left_edge = (sig_left * val_left).astype(bf16)
    right_edge = (sig_right * val_right).astype(bf16)
    out_gate = jax.nn.sigmoid(
        jnp.einsum("ijc,cd->ijd", normed, gate_weight, preferred_element_type=f32)
    )
    right_all = lax.all_gather(right_edge, "row", axis=0, tiled=True)
    block = right_all
    triangle = lax.psum_scatter(
        jnp.einsum("ikc,jkc->jic", left_edge, block, preferred_element_type=f32),
        "col",
        scatter_dimension=0,
        tiled=True,
    ).transpose(1, 0, 2)
    tri_f, tri_hat, tri_inv = layer_norm(triangle, tri_gain, tri_bias)
    tri_norm = tri_f.astype(bf16)
    update = jnp.einsum("ijh,hc->ijc", tri_norm, out_weight, preferred_element_type=f32)
    block_out = (out_gate * update).astype(bf16)
    cot = cotangent.astype(f32)
    d_update = (cot * out_gate).astype(bf16)
    d_gate = (cot * update * out_gate * (1.0 - out_gate)).astype(bf16)
    d_norm = jnp.einsum("ijc,hc->ijh", d_update, out_weight, preferred_element_type=f32)
    d_triangle = norm_back(d_norm, tri_gain, tri_hat, tri_inv).astype(bf16)
    tri_rows = lax.all_gather(d_triangle, "col", axis=1, tiled=True)
    d_left = jnp.einsum("ijc,jkc->ikc", tri_rows, right_all, preferred_element_type=f32)
    tri_cols = lax.all_to_all(tri_rows, "row", split_axis=1, concat_axis=0, tiled=True)
    block = tri_cols
    d_right = jnp.einsum(
        "ijc,ikc->jkc",
        block,
        lax.all_gather(left_edge, "row", axis=0, tiled=True),
        preferred_element_type=f32,
    )
    d_proj = jnp.concatenate(
        [
            d_left * val_left * sig_left * (1.0 - sig_left),
            d_left * sig_left,
            d_right * val_right * sig_right * (1.0 - sig_right),
            d_right * sig_right,
        ],
        axis=-1,
    ).astype(bf16)
    d_normed = jnp.einsum(
        "ijd,cd->ijc", d_proj, proj_weight, preferred_element_type=f32
    ) + jnp.einsum("ijd,cd->ijc", d_gate, gate_weight, preferred_element_type=f32)
    pair_grad = norm_back(d_normed, norm_gain, pair_hat, pair_inv)
    cells = row_count * col_count
    flat_norm = normed.reshape(cells, channels)
    local_proj = (
        jnp.dot(flat_norm.T, d_proj.reshape(cells, 4 * hidden), preferred_element_type=f32)
        / crop_len
    )
    local_gate = (
        jnp.dot(flat_norm.T, d_gate.reshape(cells, channels), preferred_element_type=f32) / crop_len
    )
    local_out = (
        jnp.dot(
            tri_norm.reshape(cells, hidden).T,
            d_update.reshape(cells, channels),
            preferred_element_type=f32,
        )
        / crop_len
    )
    proj_grad, gate_grad, out_grad = lax.psum((local_proj, local_gate, local_out), ("row", "col"))
    return (block_out, pair_grad, proj_grad, gate_grad, out_grad)


def local(pair_rep, *others):
    rows, cols, channels = pair_rep.shape
    hidden = others[7].shape[0]
    groups = lax.axis_size("row")
    every = rows * groups * cols
    fits = 24 * every * channels * 4 <= VMEM_BUDGET and hidden == channels
    paired = lax.axis_size("col") == 2 and groups & (groups - 1) == 0 and groups >= 8
    whole_tiles = cols % 8 == 0 and cols % (2 * rows) == 0 and rows * cols % 16 == 0
    plan = replicated if fits and paired and whole_tiles else sharded
    return plan(pair_rep, *others)


def solution(mesh):
    return jax.shard_map(
        local,
        mesh=mesh,
        in_specs=(
            P(("crop", "row"), "col", None),
            P(("crop", "row"), "col", None),
            P(),
            P(),
            P(),
            P(),
            P(),
            P(),
            P(),
        ),
        out_specs=(
            P(("crop", "row"), "col", None),
            P(("crop", "row"), "col", None),
            P("crop", None),
            P("crop", None),
            P("crop", None),
        ),
        check_vma=False,
    )
```

```python
import functools

import jax
import jax.numpy as jnp
from jax import lax
from jax.experimental import pallas as pl
from jax.experimental.pallas import tpu as pltpu
from jax.sharding import PartitionSpec as P

F32 = jnp.float32
BF16 = jnp.bfloat16
VMEM_BUDGET = 24 * 2**20
SWAP = ((0, 1), (1, 0))
NATIVE = ((1,), (0,))
BY_ROWS = ((0,), (0,))
TRANSPOSED = ((1,), (1,))


def layer_norm(values, gain, bias):
    centred = values - jnp.mean(values, axis=-1, keepdims=True)
    inverse = lax.rsqrt(jnp.mean(centred * centred, axis=-1, keepdims=True) + 1e-05)
    scaled = centred * inverse
    return (scaled * gain + bias, scaled, inverse)


def norm_back(grads, gain, scaled, inverse):
    weighted = grads * gain
    first = jnp.mean(weighted, axis=-1, keepdims=True)
    second = jnp.mean(weighted * scaled, axis=-1, keepdims=True)
    return inverse * (weighted - first - scaled * second)


def sigmoid(values):
    return 0.5 * jnp.tanh(0.5 * values) + 0.5


def dot(a, b, contract=NATIVE):
    return lax.dot_general(a, b, (contract, ((), ())), preferred_element_type=F32)


def at(index, size):
    return pl.ds(pl.multiple_of(index * size, size), size)


def tile(start):
    return pl.ds(pl.multiple_of(start, 8), 8)


def parts(groups):
    distances = tuple(range(groups // 2))
    return ((0, distances), (1, distances))


def row_block(side, distance):
    me = lax.axis_index("row")
    return lax.bitwise_xor(me, 2 * distance + side)


def slots(groups):
    found = []
    for n, (side, distances) in enumerate(parts(groups)):
        found += [(n, s, row_block(side, d)) for s, d in enumerate(distances)]
    return found


def edges(blocks, params, proj_weight):
    hidden = proj_weight.shape[1] // 4
    values = jnp.concatenate([block[...] for block in blocks], axis=0).astype(F32)
    normed = layer_norm(values, params[0:1, :], params[1:2, :])[0].astype(BF16)
    projected = dot(normed, proj_weight[...])
    sides = []
    for start in (0, 2 * hidden):
        gate = sigmoid(projected[:, start : start + hidden])
        edge = gate * projected[:, start + hidden : start + 2 * hidden]
        sides.append((edge.astype(BF16).astype(F32), gate, edge * (1.0 - gate)))
    return normed, sides


def fetch_inputs_kernel(sizes, pair, cot, both, sems):
    cells = sizes[0] * sizes[1]
    copies = [
        pltpu.make_async_copy(pair, both.at[:cells], sems.at[0]),
        pltpu.make_async_copy(cot, both.at[cells:], sems.at[1]),
    ]
    for copy in copies:
        copy.start()
    for copy in copies:
        copy.wait()


def fetch_weights_kernel(sizes, *refs):
    given, (params, *held), sems = refs[:7], refs[7:11], refs[11]
    moves = [(v, params.at[n : n + 1]) for n, v in enumerate(given[:4])]
    moves += list(zip(given[4:], held, strict=True))
    copies = [pltpu.make_async_copy(a, b, sems.at[n]) for n, (a, b) in enumerate(moves)]
    for copy in copies:
        copy.start()
    for copy in copies:
        copy.wait()


def own_edges_kernel(sizes, params, weight, *refs):
    blocks, sent, normed_out, outs = refs[:-8], refs[-8], refs[-7], refs[-6:]
    normed, sides = edges(blocks, params, weight)
    normed_out[...] = normed
    count = normed.shape[0]
    sent[:count, :] = sides[0][0].astype(BF16)
    sent[count:, :] = sides[1][0].astype(BF16)
    for out, value in zip(outs, sides[0] + sides[1], strict=True):
        out[...] = value


def triangle_half(sizes, lefts, right_of, more, tri, picked):
    rows, cols, groups = sizes
    cells = rows * cols
    hidden = tri.shape[-1]
    half = lax.axis_index("col")
    count = cols // 8
    blocks = cols // rows
    for n, s, p in slots(groups):

        @pl.when(p // blocks == half)
        def _(n=n, s=s, p=p):
            picked[at(p - half * blocks, cells), :] = right_of(n, slice(s * cells, (s + 1) * cells))

    for n, s, p in slots(groups):

        if more is None:
            first = (jnp.zeros((8, hidden), F32),) * (rows * count)
        else:
            first = tuple(more[tile(p * cells + t * 8), :] for t in range(rows * count))
        sums = list(first)
        for k in range(cols):
            tiles = [picked[pl.ds(t * 8 * cols + k, 8, stride=cols), :] for t in range(count)]
            for a in range(rows):
                row = lefts[n][pl.ds((s * rows + a) * cols + k, 1), :]
                for t in range(count):
                    sums[a * count + t] += row * tiles[t]
        for t, value in enumerate(sums):
            tri[tile(p * cells + t * 8), :] = value


def own_triangle_kernel(sizes, left_0, left_1, right_0, right_1, tri, picked):
    rights = (right_0, right_1)
    triangle_half(
        sizes, (left_0, left_1), lambda n, part: rights[n][part, :], None, tri, picked
    )


def mate_triangle_kernel(sizes, edges_0, edges_1, more, tri, picked, left_0, left_1):
    got = (edges_0, edges_1)
    lefts = (left_0, left_1)
    count = left_0.shape[0]
    for edge, left in zip(got, lefts, strict=True):
        left[...] = edge[:count, :].astype(F32)

    def right_of(n, part):
        return got[n][count + part.start : count + part.stop, :].astype(F32)

    triangle_half(sizes, lefts, right_of, more, tri, picked)


def cells_kernel(
    sizes,
    params,
    tri,
    gate_weight,
    out_weight,
    *refs,
):
    rows, cols, groups = sizes
    cells = rows * cols
    normed, cots, (block_out, d_tri, d_gate, tri_norm_out, d_update_out) = (
        refs[:2],
        refs[2:6],
        refs[6:],
    )
    gain, bias = params[2:3, :], params[3:4, :]
    every = slots(groups)
    for first in range(0, groups, 4):
        chunk = every[first : first + 4]
        places = [at(p, cells) for _, _, p in chunk]
        here = jnp.concatenate([tri[place, :] for place in places], axis=0)
        tri_f, hat, inverse = layer_norm(here, gain, bias)
        tri_norm = tri_f.astype(BF16)
        update = dot(tri_norm, out_weight[...])
        n, s, _ = chunk[0]
        out_gate = sigmoid(dot(normed[n][s * cells : (s + 4) * cells, :], gate_weight[...]))
        if first == 0:
            block_out[...] = (out_gate[:cells] * update[:cells]).astype(BF16)
        cot = jnp.concatenate([cots[2 * n + min(s, 1)][max(s - 1, 0) * cells : max(s, 1) * cells, :] for n, s, _ in chunk], axis=0)
        gated = cot.astype(F32) * out_gate
        d_update = gated.astype(BF16)
        d_gates = (gated * update * (1.0 - out_gate)).astype(BF16)
        d_norm = dot(d_update, out_weight[...], TRANSPOSED)
        d_tris = norm_back(d_norm, gain, hat, inverse).astype(BF16)
        for t, place in enumerate(places):
            part = slice(t * cells, (t + 1) * cells)
            d_gate[place, :] = d_gates[part]
            d_tri[place, :] = d_tris[part]
            tri_norm_out[place, :] = tri_norm[part]
            d_update_out[place, :] = d_update[part]


def contract(rows, cols, count, unroll, start, source, row_at, operand, operand_at):
    tiles = cols // 8

    def step(term, sums):
        new = list(sums)
        loaded = [operand[tile(operand_at(term) + t * 8), :] for t in range(tiles)]
        for a in range(rows):
            row = source[pl.ds(row_at(a, term), 1), :]
            for t in range(tiles):
                new[a * tiles + t] += row * loaded[t]
        return tuple(new)

    return lax.fori_loop(0, count, step, start, unroll=unroll)


def contract_all(rows, cols, count, start, source, row_at, operand, operand_at):
    tiles = cols // 8
    sums = list(start)
    for term in range(count):
        loaded = [operand[tile(operand_at(term) + t * 8), :] for t in range(tiles)]
        for a in range(rows):
            row = source[pl.ds(row_at(a, term), 1), :]
            for t in range(tiles):
                sums[a * tiles + t] += row * loaded[t]
    return sums


def early_kernel(
    sizes,
    d_tri_ref,
    d_gate,
    tri_norm,
    d_update,
    *refs,
):
    rows, cols, groups = sizes
    left, right, normed, d_left, d_right, small_grads, source = refs[6:]
    cells = rows * cols
    hidden = left.shape[-1]
    channels = normed.shape[-1]
    half = lax.axis_index("col")
    zeros = (jnp.zeros((8, hidden), F32),) * (rows * cols // 8)
    source[...] = d_tri_ref[...].astype(F32)
    for n, s, p in slots(groups):
        place, part = at(p, cells), slice(s * cells, (s + 1) * cells)
        normed[place, :] = refs[n][part, :]
        left[place, :] = refs[2 + n][part, :]
        right[place, :] = refs[4 + n][part, :]

    scale = 1.0 / (rows * groups)
    small_grads[:, :channels] = dot(normed[...], d_gate[...], BY_ROWS) * scale
    small_grads[:, channels:] = dot(tri_norm[...], d_update[...], BY_ROWS) * scale
    for p in range(groups):
        sums = contract_all(
            rows,
            cols,
            cols,
            zeros,
            source,
            lambda a, j, p=p: (p * rows + a) * cols + j,
            right,
            lambda j: (half * cols + j) * cols,
        )
        for t, value in enumerate(sums):
            d_left[tile(p * cells + t * 8), :] = value

    for p in range(cols // rows):
        sums = contract_all(
            rows,
            cols,
            rows * groups,
            zeros,
            source,
            lambda a, i, p=p: i * cols + p * rows + a,
            left,
            lambda i: i * cols,
        )
        for t, value in enumerate(sums):
            d_right[tile(p * cells + t * 8), :] = value


def late_kernel(
    sizes,
    d_tri_ref,
    left,
    right,
    normed,
    d_left,
    d_right,
    *refs,
):
    rows, cols, groups = sizes
    left_gate, left_value, right_gate, right_value = refs[:2], refs[2:4], refs[4:6], refs[6:8]
    proj_grad, d_proj, source, d_right_s = refs[8:]
    cells = rows * cols
    hidden = left.shape[-1]
    half = lax.axis_index("col")
    zeros = (jnp.zeros((8, hidden), F32),) * (rows * cols // 8)
    source[...] = d_tri_ref[...].astype(F32)
    d_right_s[at(half, cols * cols), :] = d_right[...]

    def right_block(p, carry):
        sums = contract(
            rows,
            cols,
            rows * groups,
            8,
            zeros,
            source,
            lambda a, i: i * cols + p * rows + a,
            left,
            lambda i: i * cols,
        )
        start = (1 - half) * cols * cols + p * cells
        for t, value in enumerate(sums):
            d_right_s[tile(start + t * 8), :] = value
        return carry

    lax.fori_loop(0, cols // rows, right_block, 0)

    scale = 1.0 / (rows * groups)
    for n, s, p in slots(groups):
        part, place = slice(s * cells, (s + 1) * cells), at(p, cells)
        grads = d_right_s[place, :]
        d_proj[place, 2 * hidden : 3 * hidden] = (grads * right_value[n][part, :]).astype(BF16)
        d_proj[place, 3 * hidden :] = (grads * right_gate[n][part, :]).astype(BF16)
    proj_grad[:, 2 * hidden :] = dot(normed[...], d_proj[:, 2 * hidden :], BY_ROWS) * scale
    for n, s, p in slots(groups):
        start = p * cells
        sums = contract_all(
            rows,
            cols,
            cols,
            [d_left[tile(start + t * 8), :] for t in range(cells // 8)],
            source,
            lambda a, j, p=p: (p * rows + a) * cols + j,
            right,
            lambda j: ((1 - half) * cols + j) * cols,
        )
        part, place = slice(s * cells, (s + 1) * cells), at(p, cells)
        grads = jnp.concatenate(sums, axis=0)
        d_proj[place, :hidden] = (grads * left_value[n][part, :]).astype(BF16)
        d_proj[place, hidden : 2 * hidden] = (grads * left_gate[n][part, :]).astype(BF16)
    proj_grad[:, : 2 * hidden] = dot(normed[...], d_proj[:, : 2 * hidden], BY_ROWS) * scale


def outputs_kernel(
    sizes,
    params,
    pair,
    d_proj,
    d_gate,
    proj_weight,
    gate_weight,
    block_in,
    small_own,
    small_mate,
    block_out,
    pair_grad,
    gate_grad,
    out_grad,
):
    rows, cols, _ = sizes
    cells = rows * cols
    own = at(lax.axis_index("row"), cells)
    d_normed = dot(d_proj[own, :], proj_weight[...], TRANSPOSED) + dot(
        d_gate[own, :], gate_weight[...], TRANSPOSED
    )
    gain = params[0:1, :]
    _, hat, inverse = layer_norm(pair[...].astype(F32), gain, params[1:2, :])
    pair_grad[...] = norm_back(d_normed, gain, hat, inverse)
    block_out[...] = block_in[...]
    channels = gate_grad.shape[1]
    small = small_own[...] + small_mate[...]
    gate_grad[...] = small[:, :channels]
    out_grad[...] = small[:, channels:]


def replicated(
    pair_rep,
    cotangent,
    norm_gain,
    norm_bias,
    proj_weight,
    gate_weight,
    tri_gain,
    tri_bias,
    out_weight,
):
    rows, cols, channels = pair_rep.shape
    hidden = tri_gain.shape[0]
    groups = lax.axis_size("row")
    cells = rows * cols
    every = cells * groups
    sizes = (rows, cols, groups)

    def call(kernel, outs, *args, scratch=(), micros=1, name, **more):
        cost = pl.CostEstimate(flops=micros * 10**9, bytes_accessed=0, transcendentals=0)
        return pl.pallas_call(
            functools.partial(kernel, sizes),
            out_shape=[jax.ShapeDtypeStruct(*out) for out in outs],
            scratch_shapes=[pltpu.VMEM(*one) if isinstance(one, tuple) else one for one in scratch],
            **more,
            compiler_params=pltpu.CompilerParams(vmem_limit_bytes=VMEM_BUDGET),
            cost_estimate=cost,
            name=name,
        )(*args)

    def across(value, mask):
        return lax.ppermute(value, "row", [(i, i ^ mask) for i in range(groups)])

    def over(value):
        return lax.ppermute(value, "col", SWAP)

    def along(value):
        got, before = {}, None
        middle = groups // 4
        rest = [d for d in reversed(range(1, groups // 2)) if d != middle]
        for distance in (middle, *rest):
            arrived = across(value, 2 * distance)
            before = arrived if before is None else after(arrived, before)
            got[distance] = before
        return [got[d] for d in range(1, groups // 2)]

    def join(*values):
        return jnp.concatenate(values, axis=0)

    def after(value, *others):
        return lax.optimization_barrier((value, *others))[0]

    full = (every, hidden)

    def own_edges(*blocks):
        count = sum(block.shape[0] for block in blocks)
        outs = [((2 * count, hidden), BF16), ((count, channels), BF16)]
        outs += [((count, hidden), F32)] * 6
        return call(own_edges_kernel, outs, params, proj_weight, *blocks, micros=10, name="own_edges")

    def fetch(kernel, outs, given, name):
        given = [pltpu.with_memory_space_constraint(v, pltpu.HBM) for v in given]
        return call(
            kernel,
            outs,
            *given,
            scratch=[pltpu.SemaphoreType.DMA((len(given),))],
            in_specs=[pl.BlockSpec(memory_space=pltpu.HBM)] * len(given),
            name=name,
        )

    given = [pair_rep.reshape(cells, channels), cotangent.reshape(cells, channels)]
    (both,) = fetch(fetch_inputs_kernel, [((2 * cells, channels), BF16)], given, "fetch_inputs")
    got = along(both)
    given = [v[None] for v in (norm_gain, norm_bias, tri_gain, tri_bias)]
    given += [proj_weight, gate_weight, out_weight]
    outs = [((4, channels), F32)] + [(a.shape, BF16) for a in given[4:]]
    held = fetch(fetch_weights_kernel, outs, given, "fetch_weights")
    params, proj_weight, gate_weight, out_weight = held
    both_far = across(both, 1)
    near_b = after(join(*(block[:cells] for block in got)), params)
    far_b = across(near_b, 1)
    cot_b = join(*(block[cells:] for block in got))
    pair, pair_far = both[:cells], both_far[:cells]
    own_0 = own_edges(pair, near_b)
    mate_0 = over(own_0[0])
    cot_far_b = across(after(cot_b, own_0[0]), 1)
    cots = (both[cells:], cot_b, both_far[cells:], cot_far_b)
    own_1 = own_edges(pair_far, far_b)
    mate_1 = over(own_1[0])
    own = [o[1:] for o in (own_0, own_1)]
    normed = [o[0] for o in own]
    left, left_gate, left_value = ([o[n] for o in own] for n in (1, 2, 3))
    right, right_gate, right_value = ([o[n] for o in own] for n in (4, 5, 6))
    outs, picked, half_left = [(full, F32)], ((cols * cols, hidden), F32), ((every // 2, hidden), F32)
    tri = call(own_triangle_kernel, outs, *left, *right, scratch=[picked], micros=10, name="own_triangle")
    scratch = [picked, half_left, half_left]

    args = (mate_0, mate_1, *tri)
    (tri,) = call(mate_triangle_kernel, outs, *args, scratch=scratch, name="mate_triangle")
    block_out, d_tri, d_gate, tri_norm, d_update = call(
        cells_kernel,
        [((cells, channels), BF16)] + [(full, BF16)] * 4,
        params,
        tri,
        gate_weight,
        out_weight,
        *normed,
        *cots,
        micros=2,
        name="cells",
    )
    d_tri_mate = over(d_tri)
    left_all, right_all, normed_all, d_left, d_right, small_grads = call(
        early_kernel,
        [
            (full, F32),
            (full, F32),
            ((every, channels), BF16),
            (full, F32),
            ((cols * cols, hidden), F32),
            ((channels, 2 * channels), F32),
        ],
        d_tri,
        d_gate,
        tri_norm,
        d_update,
        *normed,
        *left,
        *right,
        scratch=[(full, F32)],
        micros=30,
        name="early",
    )
    small_mate = over(small_grads)
    proj_grad, d_proj = call(
        late_kernel,
        [((channels, 4 * hidden), F32), ((every, 4 * hidden), BF16)],
        d_tri_mate,
        left_all,
        right_all,
        normed_all,
        d_left,
        d_right,
        *left_gate,
        *left_value,
        *right_gate,
        *right_value,
        scratch=[(full, F32), (full, F32)],
        micros=40,
        name="late",
    )
    proj_mate = over(proj_grad)
    square = ((channels, channels), F32)
    block_out, pair_grad, gate_grad, out_grad = call(
        outputs_kernel,
        [((cells, channels), BF16), ((cells, channels), F32), square, square],
        params,
        pair,
        d_proj,
        d_gate,
        proj_weight,
        gate_weight,
        block_out,
        small_grads,
        small_mate,
        micros=10,
        name="outputs",
    )
    return (
        block_out.reshape(pair_rep.shape),
        pair_grad.reshape(pair_rep.shape),
        proj_grad + proj_mate,
        gate_grad,
        out_grad,
    )


def sharded(
    pair_rep,
    cotangent,
    norm_gain,
    norm_bias,
    proj_weight,
    gate_weight,
    tri_gain,
    tri_bias,
    out_weight,
):
    f32 = jnp.float32
    bf16 = jnp.bfloat16
    hidden = tri_gain.shape[0]
    channels = norm_gain.shape[0]
    row_count = pair_rep.shape[0]
    col_count = pair_rep.shape[1]
    crop_len = row_count * lax.axis_size("row")
    normed_f, pair_hat, pair_inv = layer_norm(pair_rep.astype(f32), norm_gain, norm_bias)
    normed = normed_f.astype(bf16)
    projected = jnp.einsum("ijc,cd->ijd", normed, proj_weight, preferred_element_type=f32)
    sig_left = jax.nn.sigmoid(projected[..., 0:hidden])
    val_left = projected[..., hidden : 2 * hidden]
    sig_right = jax.nn.sigmoid(projected[..., 2 * hidden : 3 * hidden])
    val_right = projected[..., 3 * hidden : 4 * hidden]
    left_edge = (sig_left * val_left).astype(bf16)
    right_edge = (sig_right * val_right).astype(bf16)
    out_gate = jax.nn.sigmoid(
        jnp.einsum("ijc,cd->ijd", normed, gate_weight, preferred_element_type=f32)
    )
    right_all = lax.all_gather(right_edge, "row", axis=0, tiled=True)
    block = right_all
    triangle = lax.psum_scatter(
        jnp.einsum("ikc,jkc->jic", left_edge, block, preferred_element_type=f32),
        "col",
        scatter_dimension=0,
        tiled=True,
    ).transpose(1, 0, 2)
    tri_f, tri_hat, tri_inv = layer_norm(triangle, tri_gain, tri_bias)
    tri_norm = tri_f.astype(bf16)
    update = jnp.einsum("ijh,hc->ijc", tri_norm, out_weight, preferred_element_type=f32)
    block_out = (out_gate * update).astype(bf16)
    cot = cotangent.astype(f32)
    d_update = (cot * out_gate).astype(bf16)
    d_gate = (cot * update * out_gate * (1.0 - out_gate)).astype(bf16)
    d_norm = jnp.einsum("ijc,hc->ijh", d_update, out_weight, preferred_element_type=f32)
    d_triangle = norm_back(d_norm, tri_gain, tri_hat, tri_inv).astype(bf16)
    tri_rows = lax.all_gather(d_triangle, "col", axis=1, tiled=True)
    d_left = jnp.einsum("ijc,jkc->ikc", tri_rows, right_all, preferred_element_type=f32)
    tri_cols = lax.all_to_all(tri_rows, "row", split_axis=1, concat_axis=0, tiled=True)
    block = tri_cols
    d_right = jnp.einsum(
        "ijc,ikc->jkc",
        block,
        lax.all_gather(left_edge, "row", axis=0, tiled=True),
        preferred_element_type=f32,
    )
    d_proj = jnp.concatenate(
        [
            d_left * val_left * sig_left * (1.0 - sig_left),
            d_left * sig_left,
            d_right * val_right * sig_right * (1.0 - sig_right),
            d_right * sig_right,
        ],
        axis=-1,
    ).astype(bf16)
    d_normed = jnp.einsum(
        "ijd,cd->ijc", d_proj, proj_weight, preferred_element_type=f32
    ) + jnp.einsum("ijd,cd->ijc", d_gate, gate_weight, preferred_element_type=f32)
    pair_grad = norm_back(d_normed, norm_gain, pair_hat, pair_inv)
    cells = row_count * col_count
    flat_norm = normed.reshape(cells, channels)
    local_proj = (
        jnp.dot(flat_norm.T, d_proj.reshape(cells, 4 * hidden), preferred_element_type=f32)
        / crop_len
    )
    local_gate = (
        jnp.dot(flat_norm.T, d_gate.reshape(cells, channels), preferred_element_type=f32) / crop_len
    )
    local_out = (
        jnp.dot(
            tri_norm.reshape(cells, hidden).T,
            d_update.reshape(cells, channels),
            preferred_element_type=f32,
        )
        / crop_len
    )
    proj_grad, gate_grad, out_grad = lax.psum((local_proj, local_gate, local_out), ("row", "col"))
    return (block_out, pair_grad, proj_grad, gate_grad, out_grad)


def local(pair_rep, *others):
    rows, cols, channels = pair_rep.shape
    hidden = others[7].shape[0]
    groups = lax.axis_size("row")
    every = rows * groups * cols
    fits = 24 * every * channels * 4 <= VMEM_BUDGET and hidden == channels
    paired = lax.axis_size("col") == 2 and groups & (groups - 1) == 0 and groups >= 8
    whole_tiles = cols % 8 == 0 and cols % (2 * rows) == 0 and rows * cols % 16 == 0
    plan = replicated if fits and paired and whole_tiles else sharded
    return plan(pair_rep, *others)


def solution(mesh):
    return jax.shard_map(
        local,
        mesh=mesh,
        in_specs=(
            P(("crop", "row"), "col", None),
            P(("crop", "row"), "col", None),
            P(),
            P(),
            P(),
            P(),
            P(),
            P(),
            P(),
        ),
        out_specs=(
            P(("crop", "row"), "col", None),
            P(("crop", "row"), "col", None),
            P("crop", None),
            P("crop", None),
            P("crop", None),
        ),
        check_vma=False,
    )
```

```python
import functools

import jax
import jax.numpy as jnp
from jax import lax
from jax.experimental import pallas as pl
from jax.experimental.pallas import tpu as pltpu
from jax.sharding import PartitionSpec as P

F32 = jnp.float32
BF16 = jnp.bfloat16
VMEM_BUDGET = 24 * 2**20
SWAP = ((0, 1), (1, 0))
NATIVE = ((1,), (0,))
BY_ROWS = ((0,), (0,))
TRANSPOSED = ((1,), (1,))


def layer_norm(values, gain, bias):
    centred = values - jnp.mean(values, axis=-1, keepdims=True)
    inverse = lax.rsqrt(jnp.mean(centred * centred, axis=-1, keepdims=True) + 1e-05)
    scaled = centred * inverse
    return (scaled * gain + bias, scaled, inverse)


def norm_back(grads, gain, scaled, inverse):
    weighted = grads * gain
    first = jnp.mean(weighted, axis=-1, keepdims=True)
    second = jnp.mean(weighted * scaled, axis=-1, keepdims=True)
    return inverse * (weighted - first - scaled * second)


def sigmoid(values):
    return 0.5 * jnp.tanh(0.5 * values) + 0.5


def dot(a, b, contract=NATIVE):
    return lax.dot_general(a, b, (contract, ((), ())), preferred_element_type=F32)


def at(index, size):
    return pl.ds(pl.multiple_of(index * size, size), size)


def tile(start):
    return pl.ds(pl.multiple_of(start, 8), 8)


def parts(groups):
    distances = tuple(range(groups // 2))
    return ((0, distances), (1, distances))


def row_block(side, distance):
    me = lax.axis_index("row")
    return lax.bitwise_xor(me, 2 * distance + side)


def slots(groups):
    found = []
    for n, (side, distances) in enumerate(parts(groups)):
        found += [(n, s, row_block(side, d)) for s, d in enumerate(distances)]
    return found


def named_slots(sizes, side, half):
    rows, cols, _ = sizes
    me = lax.axis_index("row")
    blocks = cols // rows
    found = []
    for n in range(blocks // 2):
        place = 2 * n + lax.rem(me + side, 2)
        found.append((place, lax.bitwise_xor((half * blocks + place) // 2, me // 2)))
    return found


def edges(blocks, params, proj_weight):
    hidden = proj_weight.shape[1] // 4
    values = jnp.concatenate([block[...] for block in blocks], axis=0).astype(F32)
    normed = layer_norm(values, params[0:1, :], params[1:2, :])[0].astype(BF16)
    projected = dot(normed, proj_weight[...])
    sides = []
    for start in (0, 2 * hidden):
        gate = sigmoid(projected[:, start : start + hidden])
        edge = gate * projected[:, start + hidden : start + 2 * hidden]
        sides.append((edge.astype(BF16).astype(F32), gate, edge * (1.0 - gate)))
    return normed, sides


def fetch_inputs_kernel(sizes, pair, cot, both, sems):
    cells = sizes[0] * sizes[1]
    copies = [
        pltpu.make_async_copy(pair, both.at[:cells], sems.at[0]),
        pltpu.make_async_copy(cot, both.at[cells:], sems.at[1]),
    ]
    for copy in copies:
        copy.start()
    for copy in copies:
        copy.wait()


def fetch_weights_kernel(sizes, *refs):
    given, (params, *held), sems = refs[:7], refs[7:11], refs[11]
    moves = [(v, params.at[n : n + 1]) for n, v in enumerate(given[:4])]
    moves += list(zip(given[4:], held, strict=True))
    copies = [pltpu.make_async_copy(a, b, sems.at[n]) for n, (a, b) in enumerate(moves)]
    for copy in copies:
        copy.start()
    for copy in copies:
        copy.wait()


def own_edges_kernel(side, sizes, params, weight, *refs):
    blocks, sent, normed_out, outs = refs[:-8], refs[-8], refs[-7], refs[-6:]
    normed, sides = edges(blocks, params, weight)
    normed_out[...] = normed
    for out, value in zip(outs, sides[0] + sides[1], strict=True):
        out[...] = value
    rows, cols, groups = sizes
    cells = rows * cols
    count = normed.shape[0]
    sent[:count, :] = sides[0][0].astype(BF16)
    other = 1 - lax.axis_index("col")
    for n, (_, slot) in enumerate(named_slots(sizes, side, other)):
        place = slice(count + n * cells, count + (n + 1) * cells)
        sent[place, :] = outs[3][at(slot, cells), :].astype(BF16)


def triangle_half(sizes, lefts, right_of, more, tri, picked):
    rows, cols, groups = sizes
    cells = rows * cols
    hidden = tri.shape[-1]
    half = lax.axis_index("col")
    count = cols // 8
    for n in range(2):
        for m, (place, slot) in enumerate(named_slots(sizes, n, half)):
            picked[at(place, cells), :] = right_of(n, m, slot)

    for n, s, p in slots(groups):

        if more is None:
            first = (jnp.zeros((8, hidden), F32),) * (rows * count)
        else:
            first = tuple(more[tile(p * cells + t * 8), :] for t in range(rows * count))
        sums = list(first)
        for k in range(cols):
            tiles = [picked[pl.ds(t * 8 * cols + k, 8, stride=cols), :] for t in range(count)]
            for a in range(rows):
                row = lefts[n][pl.ds((s * rows + a) * cols + k, 1), :]
                for t in range(count):
                    sums[a * count + t] += row * tiles[t]
        for t, value in enumerate(sums):
            tri[tile(p * cells + t * 8), :] = value


def own_triangle_kernel(sizes, left_0, left_1, right_0, right_1, tri, picked):
    rights = (right_0, right_1)
    triangle_half(
        sizes,
        (left_0, left_1),
        lambda n, m, slot: rights[n][at(slot, sizes[0] * sizes[1]), :],
        None,
        tri,
        picked,
    )


def mate_triangle_kernel(sizes, edges_0, edges_1, more, tri, picked, left_0, left_1):
    got = (edges_0, edges_1)
    lefts = (left_0, left_1)
    count = left_0.shape[0]
    for edge, left in zip(got, lefts, strict=True):
        left[...] = edge[:count, :].astype(F32)

    cells = sizes[0] * sizes[1]

    def right_of(n, m, slot):
        return got[n][count + m * cells : count + (m + 1) * cells, :].astype(F32)

    triangle_half(sizes, lefts, right_of, more, tri, picked)


def cells_kernel(
    sizes,
    params,
    tri,
    gate_weight,
    out_weight,
    *refs,
):
    rows, cols, groups = sizes
    cells = rows * cols
    normed, cots, (block_out, d_tri, d_gate, tri_norm_out, d_update_out) = (
        refs[:2],
        refs[2:6],
        refs[6:],
    )
    gain, bias = params[2:3, :], params[3:4, :]
    every = slots(groups)
    for first in range(0, groups, 4):
        chunk = every[first : first + 4]
        places = [at(p, cells) for _, _, p in chunk]
        here = jnp.concatenate([tri[place, :] for place in places], axis=0)
        tri_f, hat, inverse = layer_norm(here, gain, bias)
        tri_norm = tri_f.astype(BF16)
        update = dot(tri_norm, out_weight[...])
        n, s, _ = chunk[0]
        out_gate = sigmoid(dot(normed[n][s * cells : (s + 4) * cells, :], gate_weight[...]))
        if first == 0:
            block_out[...] = (out_gate[:cells] * update[:cells]).astype(BF16)
        cot = jnp.concatenate([cots[2 * n + min(s, 1)][max(s - 1, 0) * cells : max(s, 1) * cells, :] for n, s, _ in chunk], axis=0)
        gated = cot.astype(F32) * out_gate
        d_update = gated.astype(BF16)
        d_gates = (gated * update * (1.0 - out_gate)).astype(BF16)
        d_norm = dot(d_update, out_weight[...], TRANSPOSED)
        d_tris = norm_back(d_norm, gain, hat, inverse).astype(BF16)
        for t, place in enumerate(places):
            part = slice(t * cells, (t + 1) * cells)
            d_gate[place, :] = d_gates[part]
            d_tri[place, :] = d_tris[part]
            tri_norm_out[place, :] = tri_norm[part]
            d_update_out[place, :] = d_update[part]


def contract(rows, cols, count, unroll, start, source, row_at, operand, operand_at):
    tiles = cols // 8

    def step(term, sums):
        new = list(sums)
        loaded = [operand[tile(operand_at(term) + t * 8), :] for t in range(tiles)]
        for a in range(rows):
            row = source[pl.ds(row_at(a, term), 1), :]
            for t in range(tiles):
                new[a * tiles + t] += row * loaded[t]
        return tuple(new)

    return lax.fori_loop(0, count, step, start, unroll=unroll)


def contract_all(rows, cols, count, start, source, row_at, operand, operand_at):
    tiles = cols // 8
    sums = list(start)
    for term in range(count):
        loaded = [operand[tile(operand_at(term) + t * 8), :] for t in range(tiles)]
        for a in range(rows):
            row = source[pl.ds(row_at(a, term), 1), :]
            for t in range(tiles):
                sums[a * tiles + t] += row * loaded[t]
    return sums


def early_kernel(
    sizes,
    d_tri_ref,
    d_gate,
    tri_norm,
    d_update,
    *refs,
):
    rows, cols, groups = sizes
    left, right, normed, d_left, d_right, small_grads, source = refs[6:]
    cells = rows * cols
    hidden = left.shape[-1]
    channels = normed.shape[-1]
    half = lax.axis_index("col")
    zeros = (jnp.zeros((8, hidden), F32),) * (rows * cols // 8)
    source[...] = d_tri_ref[...].astype(F32)
    for n, s, p in slots(groups):
        place, part = at(p, cells), slice(s * cells, (s + 1) * cells)
        normed[place, :] = refs[n][part, :]
        left[place, :] = refs[2 + n][part, :]
        right[place, :] = refs[4 + n][part, :]

    scale = 1.0 / (rows * groups)
    small_grads[:, :channels] = dot(normed[...], d_gate[...], BY_ROWS) * scale
    small_grads[:, channels:] = dot(tri_norm[...], d_update[...], BY_ROWS) * scale
    for p in range(groups):
        sums = contract_all(
            rows,
            cols,
            cols,
            zeros,
            source,
            lambda a, j, p=p: (p * rows + a) * cols + j,
            right,
            lambda j: (half * cols + j) * cols,
        )
        for t, value in enumerate(sums):
            d_left[tile(p * cells + t * 8), :] = value

    for p in range(cols // rows):
        sums = contract_all(
            rows,
            cols,
            rows * groups,
            zeros,
            source,
            lambda a, i, p=p: i * cols + p * rows + a,
            left,
            lambda i: i * cols,
        )
        for t, value in enumerate(sums):
            d_right[tile(p * cells + t * 8), :] = value


def late_kernel(
    sizes,
    d_tri_ref,
    left,
    right,
    normed,
    d_left,
    d_right,
    *refs,
):
    rows, cols, groups = sizes
    left_gate, left_value, right_gate, right_value = refs[:2], refs[2:4], refs[4:6], refs[6:8]
    proj_grad, d_proj, source, d_right_s = refs[8:]
    cells = rows * cols
    hidden = left.shape[-1]
    half = lax.axis_index("col")
    zeros = (jnp.zeros((8, hidden), F32),) * (rows * cols // 8)
    source[...] = d_tri_ref[...].astype(F32)
    d_right_s[at(half, cols * cols), :] = d_right[...]

    def right_block(p, carry):
        sums = contract(
            rows,
            cols,
            rows * groups,
            24,
            zeros,
            source,
            lambda a, i: i * cols + p * rows + a,
            left,
            lambda i: i * cols,
        )
        start = (1 - half) * cols * cols + p * cells
        for t, value in enumerate(sums):
            d_right_s[tile(start + t * 8), :] = value
        return carry

    lax.fori_loop(0, cols // rows, right_block, 0)

    scale = 1.0 / (rows * groups)
    for n, s, p in slots(groups):
        part, place = slice(s * cells, (s + 1) * cells), at(p, cells)
        grads = d_right_s[place, :]
        d_proj[place, 2 * hidden : 3 * hidden] = (grads * right_value[n][part, :]).astype(BF16)
        d_proj[place, 3 * hidden :] = (grads * right_gate[n][part, :]).astype(BF16)
    proj_grad[:, 2 * hidden :] = dot(normed[...], d_proj[:, 2 * hidden :], BY_ROWS) * scale
    for n, s, p in slots(groups):
        start = p * cells
        sums = contract_all(
            rows,
            cols,
            cols,
            [d_left[tile(start + t * 8), :] for t in range(cells // 8)],
            source,
            lambda a, j, p=p: (p * rows + a) * cols + j,
            right,
            lambda j: ((1 - half) * cols + j) * cols,
        )
        part, place = slice(s * cells, (s + 1) * cells), at(p, cells)
        grads = jnp.concatenate(sums, axis=0)
        d_proj[place, :hidden] = (grads * left_value[n][part, :]).astype(BF16)
        d_proj[place, hidden : 2 * hidden] = (grads * left_gate[n][part, :]).astype(BF16)
    proj_grad[:, : 2 * hidden] = dot(normed[...], d_proj[:, : 2 * hidden], BY_ROWS) * scale


def outputs_kernel(
    sizes,
    params,
    pair,
    d_proj,
    d_gate,
    proj_weight,
    gate_weight,
    block_in,
    small_own,
    small_mate,
    block_out,
    pair_grad,
    gate_grad,
    out_grad,
):
    rows, cols, _ = sizes
    cells = rows * cols
    own = at(lax.axis_index("row"), cells)
    d_normed = dot(d_proj[own, :], proj_weight[...], TRANSPOSED) + dot(
        d_gate[own, :], gate_weight[...], TRANSPOSED
    )
    gain = params[0:1, :]
    _, hat, inverse = layer_norm(pair[...].astype(F32), gain, params[1:2, :])
    pair_grad[...] = norm_back(d_normed, gain, hat, inverse)
    block_out[...] = block_in[...]
    channels = gate_grad.shape[1]
    small = small_own[...] + small_mate[...]
    gate_grad[...] = small[:, :channels]
    out_grad[...] = small[:, channels:]


def replicated(
    pair_rep,
    cotangent,
    norm_gain,
    norm_bias,
    proj_weight,
    gate_weight,
    tri_gain,
    tri_bias,
    out_weight,
):
    rows, cols, channels = pair_rep.shape
    hidden = tri_gain.shape[0]
    groups = lax.axis_size("row")
    cells = rows * cols
    every = cells * groups
    sizes = (rows, cols, groups)

    def call(kernel, outs, *args, scratch=(), micros=1, name, **more):
        cost = pl.CostEstimate(flops=micros * 10**9, bytes_accessed=0, transcendentals=0)
        return pl.pallas_call(
            functools.partial(kernel, sizes),
            out_shape=[jax.ShapeDtypeStruct(*out) for out in outs],
            scratch_shapes=[pltpu.VMEM(*one) if isinstance(one, tuple) else one for one in scratch],
            **more,
            compiler_params=pltpu.CompilerParams(vmem_limit_bytes=VMEM_BUDGET),
            cost_estimate=cost,
            name=name,
        )(*args)

    def across(value, mask):
        return lax.ppermute(value, "row", [(i, i ^ mask) for i in range(groups)])

    def over(value):
        return lax.ppermute(value, "col", SWAP)

    def along(value):
        got, before = {}, None
        middle = groups // 4
        rest = [d for d in reversed(range(1, groups // 2)) if d != middle]
        for distance in (middle, *rest):
            arrived = across(value, 2 * distance)
            before = arrived if before is None else after(arrived, before)
            got[distance] = before
        return [got[d] for d in range(1, groups // 2)]

    def join(*values):
        return jnp.concatenate(values, axis=0)

    def after(value, *others):
        return lax.optimization_barrier((value, *others))[0]

    full = (every, hidden)

    def own_edges(side, *blocks):
        count = sum(block.shape[0] for block in blocks)
        outs = [((count + count // 2, hidden), BF16), ((count, channels), BF16)]
        outs += [((count, hidden), F32)] * 6
        kernel = functools.partial(own_edges_kernel, side)
        return call(kernel, outs, params, proj_weight, *blocks, micros=10, name="own_edges")

    def fetch(kernel, outs, given, name):
        given = [pltpu.with_memory_space_constraint(v, pltpu.HBM) for v in given]
        return call(
            kernel,
            outs,
            *given,
            scratch=[pltpu.SemaphoreType.DMA((len(given),))],
            in_specs=[pl.BlockSpec(memory_space=pltpu.HBM)] * len(given),
            name=name,
        )

    given = [pair_rep.reshape(cells, channels), cotangent.reshape(cells, channels)]
    (both,) = fetch(fetch_inputs_kernel, [((2 * cells, channels), BF16)], given, "fetch_inputs")
    got = along(both)
    given = [v[None] for v in (norm_gain, norm_bias, tri_gain, tri_bias)]
    given += [proj_weight, gate_weight, out_weight]
    outs = [((4, channels), F32)] + [(a.shape, BF16) for a in given[4:]]
    held = fetch(fetch_weights_kernel, outs, given, "fetch_weights")
    params, proj_weight, gate_weight, out_weight = held
    both_far = across(both, 1)
    near_b = after(join(*(block[:cells] for block in got)), params)
    far_b = across(near_b, 1)
    cot_b = join(*(block[cells:] for block in got))
    pair, pair_far = both[:cells], both_far[:cells]
    own_0 = own_edges(0, pair, near_b)
    mate_0 = over(own_0[0])
    cot_far_b = across(after(cot_b, own_0[0]), 1)
    cots = (both[cells:], cot_b, both_far[cells:], cot_far_b)
    own_1 = own_edges(1, pair_far, far_b)
    mate_1 = over(own_1[0])
    own = [o[1:] for o in (own_0, own_1)]
    normed = [o[0] for o in own]
    left, left_gate, left_value = ([o[n] for o in own] for n in (1, 2, 3))
    right, right_gate, right_value = ([o[n] for o in own] for n in (4, 5, 6))
    outs, picked, half_left = [(full, F32)], ((cols * cols, hidden), F32), ((every // 2, hidden), F32)
    tri = call(own_triangle_kernel, outs, *left, *right, scratch=[picked], micros=10, name="own_triangle")
    scratch = [picked, half_left, half_left]

    args = (mate_0, mate_1, *tri)
    (tri,) = call(mate_triangle_kernel, outs, *args, scratch=scratch, name="mate_triangle")
    block_out, d_tri, d_gate, tri_norm, d_update = call(
        cells_kernel,
        [((cells, channels), BF16)] + [(full, BF16)] * 4,
        params,
        tri,
        gate_weight,
        out_weight,
        *normed,
        *cots,
        micros=2,
        name="cells",
    )
    d_tri_mate = over(d_tri)
    left_all, right_all, normed_all, d_left, d_right, small_grads = call(
        early_kernel,
        [
            (full, F32),
            (full, F32),
            ((every, channels), BF16),
            (full, F32),
            ((cols * cols, hidden), F32),
            ((channels, 2 * channels), F32),
        ],
        d_tri,
        d_gate,
        tri_norm,
        d_update,
        *normed,
        *left,
        *right,
        scratch=[(full, F32)],
        micros=30,
        name="early",
    )
    small_mate = over(small_grads)
    proj_grad, d_proj = call(
        late_kernel,
        [((channels, 4 * hidden), F32), ((every, 4 * hidden), BF16)],
        d_tri_mate,
        left_all,
        right_all,
        normed_all,
        d_left,
        d_right,
        *left_gate,
        *left_value,
        *right_gate,
        *right_value,
        scratch=[(full, F32), (full, F32)],
        micros=40,
        name="late",
    )
    proj_mate = over(proj_grad)
    square = ((channels, channels), F32)
    block_out, pair_grad, gate_grad, out_grad = call(
        outputs_kernel,
        [((cells, channels), BF16), ((cells, channels), F32), square, square],
        params,
        pair,
        d_proj,
        d_gate,
        proj_weight,
        gate_weight,
        block_out,
        small_grads,
        small_mate,
        micros=10,
        name="outputs",
    )
    return (
        block_out.reshape(pair_rep.shape),
        pair_grad.reshape(pair_rep.shape),
        proj_grad + proj_mate,
        gate_grad,
        out_grad,
    )


def sharded(
    pair_rep,
    cotangent,
    norm_gain,
    norm_bias,
    proj_weight,
    gate_weight,
    tri_gain,
    tri_bias,
    out_weight,
):
    f32 = jnp.float32
    bf16 = jnp.bfloat16
    hidden = tri_gain.shape[0]
    channels = norm_gain.shape[0]
    row_count = pair_rep.shape[0]
    col_count = pair_rep.shape[1]
    crop_len = row_count * lax.axis_size("row")
    normed_f, pair_hat, pair_inv = layer_norm(pair_rep.astype(f32), norm_gain, norm_bias)
    normed = normed_f.astype(bf16)
    projected = jnp.einsum("ijc,cd->ijd", normed, proj_weight, preferred_element_type=f32)
    sig_left = jax.nn.sigmoid(projected[..., 0:hidden])
    val_left = projected[..., hidden : 2 * hidden]
    sig_right = jax.nn.sigmoid(projected[..., 2 * hidden : 3 * hidden])
    val_right = projected[..., 3 * hidden : 4 * hidden]
    left_edge = (sig_left * val_left).astype(bf16)
    right_edge = (sig_right * val_right).astype(bf16)
    out_gate = jax.nn.sigmoid(
        jnp.einsum("ijc,cd->ijd", normed, gate_weight, preferred_element_type=f32)
    )
    right_all = lax.all_gather(right_edge, "row", axis=0, tiled=True)
    block = right_all
    triangle = lax.psum_scatter(
        jnp.einsum("ikc,jkc->jic", left_edge, block, preferred_element_type=f32),
        "col",
        scatter_dimension=0,
        tiled=True,
    ).transpose(1, 0, 2)
    tri_f, tri_hat, tri_inv = layer_norm(triangle, tri_gain, tri_bias)
    tri_norm = tri_f.astype(bf16)
    update = jnp.einsum("ijh,hc->ijc", tri_norm, out_weight, preferred_element_type=f32)
    block_out = (out_gate * update).astype(bf16)
    cot = cotangent.astype(f32)
    d_update = (cot * out_gate).astype(bf16)
    d_gate = (cot * update * out_gate * (1.0 - out_gate)).astype(bf16)
    d_norm = jnp.einsum("ijc,hc->ijh", d_update, out_weight, preferred_element_type=f32)
    d_triangle = norm_back(d_norm, tri_gain, tri_hat, tri_inv).astype(bf16)
    tri_rows = lax.all_gather(d_triangle, "col", axis=1, tiled=True)
    d_left = jnp.einsum("ijc,jkc->ikc", tri_rows, right_all, preferred_element_type=f32)
    tri_cols = lax.all_to_all(tri_rows, "row", split_axis=1, concat_axis=0, tiled=True)
    block = tri_cols
    d_right = jnp.einsum(
        "ijc,ikc->jkc",
        block,
        lax.all_gather(left_edge, "row", axis=0, tiled=True),
        preferred_element_type=f32,
    )
    d_proj = jnp.concatenate(
        [
            d_left * val_left * sig_left * (1.0 - sig_left),
            d_left * sig_left,
            d_right * val_right * sig_right * (1.0 - sig_right),
            d_right * sig_right,
        ],
        axis=-1,
    ).astype(bf16)
    d_normed = jnp.einsum(
        "ijd,cd->ijc", d_proj, proj_weight, preferred_element_type=f32
    ) + jnp.einsum("ijd,cd->ijc", d_gate, gate_weight, preferred_element_type=f32)
    pair_grad = norm_back(d_normed, norm_gain, pair_hat, pair_inv)
    cells = row_count * col_count
    flat_norm = normed.reshape(cells, channels)
    local_proj = (
        jnp.dot(flat_norm.T, d_proj.reshape(cells, 4 * hidden), preferred_element_type=f32)
        / crop_len
    )
    local_gate = (
        jnp.dot(flat_norm.T, d_gate.reshape(cells, channels), preferred_element_type=f32) / crop_len
    )
    local_out = (
        jnp.dot(
            tri_norm.reshape(cells, hidden).T,
            d_update.reshape(cells, channels),
            preferred_element_type=f32,
        )
        / crop_len
    )
    proj_grad, gate_grad, out_grad = lax.psum((local_proj, local_gate, local_out), ("row", "col"))
    return (block_out, pair_grad, proj_grad, gate_grad, out_grad)


def local(pair_rep, *others):
    rows, cols, channels = pair_rep.shape
    hidden = others[7].shape[0]
    groups = lax.axis_size("row")
    every = rows * groups * cols
    fits = 24 * every * channels * 4 <= VMEM_BUDGET and hidden == channels
    paired = lax.axis_size("col") == 2 and groups & (groups - 1) == 0 and groups >= 8
    whole_tiles = cols % 8 == 0 and cols % (2 * rows) == 0 and rows * cols % 16 == 0
    plan = replicated if fits and paired and whole_tiles else sharded
    return plan(pair_rep, *others)


def solution(mesh):
    return jax.shard_map(
        local,
        mesh=mesh,
        in_specs=(
            P(("crop", "row"), "col", None),
            P(("crop", "row"), "col", None),
            P(),
            P(),
            P(),
            P(),
            P(),
            P(),
            P(),
        ),
        out_specs=(
            P(("crop", "row"), "col", None),
            P(("crop", "row"), "col", None),
            P("crop", None),
            P("crop", None),
            P("crop", None),
        ),
        check_vma=False,
    )
```

```python
import functools

import jax
import jax.numpy as jnp
from jax import lax
from jax.experimental import pallas as pl
from jax.experimental.pallas import tpu as pltpu
from jax.sharding import PartitionSpec as P

F32 = jnp.float32
BF16 = jnp.bfloat16
VMEM_BUDGET = 24 * 2**20
SWAP = ((0, 1), (1, 0))
NATIVE = ((1,), (0,))
BY_ROWS = ((0,), (0,))
TRANSPOSED = ((1,), (1,))


def layer_norm(values, gain, bias):
    centred = values - jnp.mean(values, axis=-1, keepdims=True)
    inverse = lax.rsqrt(jnp.mean(centred * centred, axis=-1, keepdims=True) + 1e-05)
    scaled = centred * inverse
    return (scaled * gain + bias, scaled, inverse)


def norm_back(grads, gain, scaled, inverse):
    weighted = grads * gain
    first = jnp.mean(weighted, axis=-1, keepdims=True)
    second = jnp.mean(weighted * scaled, axis=-1, keepdims=True)
    return inverse * (weighted - first - scaled * second)


def sigmoid(values):
    return 0.5 * jnp.tanh(0.5 * values) + 0.5


def dot(a, b, contract=NATIVE):
    return lax.dot_general(a, b, (contract, ((), ())), preferred_element_type=F32)


def at(index, size):
    return pl.ds(pl.multiple_of(index * size, size), size)


def tile(start):
    return pl.ds(pl.multiple_of(start, 8), 8)


def parts(groups):
    distances = tuple(range(groups // 2))
    return ((0, distances), (1, distances))


def row_block(side, distance):
    me = lax.axis_index("row")
    return lax.bitwise_xor(me, 2 * distance + side)


def slots(groups):
    found = []
    for n, (side, distances) in enumerate(parts(groups)):
        found += [(n, s, row_block(side, d)) for s, d in enumerate(distances)]
    return found


def named_slots(sizes, side, half):
    rows, cols, _ = sizes
    me = lax.axis_index("row")
    blocks = cols // rows
    found = []
    for n in range(blocks // 2):
        place = 2 * n + lax.rem(me + side, 2)
        found.append((place, lax.bitwise_xor((half * blocks + place) // 2, me // 2)))
    return found


def edges(blocks, params, proj_weight):
    hidden = proj_weight.shape[1] // 4
    values = jnp.concatenate([block[...] for block in blocks], axis=0).astype(F32)
    normed = layer_norm(values, params[0:1, :], params[1:2, :])[0].astype(BF16)
    projected = dot(normed, proj_weight[...])
    sides = []
    for start in (0, 2 * hidden):
        gate = sigmoid(projected[:, start : start + hidden])
        edge = gate * projected[:, start + hidden : start + 2 * hidden]
        sides.append((edge.astype(BF16).astype(F32), gate, edge * (1.0 - gate)))
    return normed, sides


def fetch_inputs_kernel(sizes, pair, cot, both, sems):
    cells = sizes[0] * sizes[1]
    copies = [
        pltpu.make_async_copy(pair, both.at[:cells], sems.at[0]),
        pltpu.make_async_copy(cot, both.at[cells:], sems.at[1]),
    ]
    for copy in copies:
        copy.start()
    for copy in copies:
        copy.wait()


def fetch_weights_kernel(sizes, *refs):
    given, (params, *held), sems = refs[:7], refs[7:11], refs[11]
    moves = [(v, params.at[n : n + 1]) for n, v in enumerate(given[:4])]
    moves += list(zip(given[4:], held, strict=True))
    copies = [pltpu.make_async_copy(a, b, sems.at[n]) for n, (a, b) in enumerate(moves)]
    for copy in copies:
        copy.start()
    for copy in copies:
        copy.wait()


def own_edges_kernel(side, sizes, params, weight, *refs):
    blocks, sent, normed_out, outs = refs[:-8], refs[-8], refs[-7], refs[-6:]
    normed, sides = edges(blocks, params, weight)
    normed_out[...] = normed
    for out, value in zip(outs, sides[0] + sides[1], strict=True):
        out[...] = value
    rows, cols, groups = sizes
    cells = rows * cols
    count = normed.shape[0]
    sent[:count, :] = sides[0][0].astype(BF16)
    other = 1 - lax.axis_index("col")
    for n, (_, slot) in enumerate(named_slots(sizes, side, other)):
        place = slice(count + n * cells, count + (n + 1) * cells)
        sent[place, :] = outs[3][at(slot, cells), :].astype(BF16)


def triangle_half(sizes, lefts, right_of, more, tri, picked):
    rows, cols, groups = sizes
    cells = rows * cols
    hidden = tri.shape[-1]
    half = lax.axis_index("col")
    count = cols // 8
    for n in range(2):
        for m, (place, slot) in enumerate(named_slots(sizes, n, half)):
            picked[at(place, cells), :] = right_of(n, m, slot)

    for n, s, p in slots(groups):

        if more is None:
            first = (jnp.zeros((8, hidden), F32),) * (rows * count)
        else:
            first = tuple(more[tile(p * cells + t * 8), :] for t in range(rows * count))
        sums = list(first)
        for k in range(cols):
            tiles = [picked[pl.ds(t * 8 * cols + k, 8, stride=cols), :] for t in range(count)]
            for a in range(rows):
                row = lefts[n][pl.ds((s * rows + a) * cols + k, 1), :]
                for t in range(count):
                    sums[a * count + t] += row * tiles[t]
        for t, value in enumerate(sums):
            tri[tile(p * cells + t * 8), :] = value


def own_triangle_kernel(sizes, left_0, left_1, right_0, right_1, tri, picked):
    rights = (right_0, right_1)
    triangle_half(
        sizes,
        (left_0, left_1),
        lambda n, m, slot: rights[n][at(slot, sizes[0] * sizes[1]), :],
        None,
        tri,
        picked,
    )


def mate_triangle_kernel(sizes, edges_0, edges_1, more, tri, picked, left_0, left_1):
    got = (edges_0, edges_1)
    lefts = (left_0, left_1)
    count = left_0.shape[0]
    for edge, left in zip(got, lefts, strict=True):
        left[...] = edge[:count, :].astype(F32)

    cells = sizes[0] * sizes[1]

    def right_of(n, m, slot):
        return got[n][count + m * cells : count + (m + 1) * cells, :].astype(F32)

    triangle_half(sizes, lefts, right_of, more, tri, picked)


def cells_kernel(
    sizes,
    params,
    tri,
    gate_weight,
    out_weight,
    *refs,
):
    rows, cols, groups = sizes
    cells = rows * cols
    normed, cots, (block_out, d_tri, d_gate, tri_norm_out, d_update_out) = (
        refs[:2],
        refs[2:6],
        refs[6:],
    )
    gain, bias = params[2:3, :], params[3:4, :]
    every = slots(groups)
    for first in range(0, groups, 4):
        chunk = every[first : first + 4]
        places = [at(p, cells) for _, _, p in chunk]
        here = jnp.concatenate([tri[place, :] for place in places], axis=0)
        tri_f, hat, inverse = layer_norm(here, gain, bias)
        tri_norm = tri_f.astype(BF16)
        update = dot(tri_norm, out_weight[...])
        n, s, _ = chunk[0]
        out_gate = sigmoid(dot(normed[n][s * cells : (s + 4) * cells, :], gate_weight[...]))
        if first == 0:
            block_out[...] = (out_gate[:cells] * update[:cells]).astype(BF16)
        cot = jnp.concatenate([cots[2 * n + min(s, 1)][max(s - 1, 0) * cells : max(s, 1) * cells, :] for n, s, _ in chunk], axis=0)
        gated = cot.astype(F32) * out_gate
        d_update = gated.astype(BF16)
        d_gates = (gated * update * (1.0 - out_gate)).astype(BF16)
        d_norm = dot(d_update, out_weight[...], TRANSPOSED)
        d_tris = norm_back(d_norm, gain, hat, inverse).astype(BF16)
        for t, place in enumerate(places):
            part = slice(t * cells, (t + 1) * cells)
            d_gate[place, :] = d_gates[part]
            d_tri[place, :] = d_tris[part]
            tri_norm_out[place, :] = tri_norm[part]
            d_update_out[place, :] = d_update[part]


def contract(rows, cols, count, unroll, start, source, row_at, operand, operand_at):
    tiles = cols // 8

    def step(term, sums):
        new = list(sums)
        loaded = [operand[tile(operand_at(term) + t * 8), :] for t in range(tiles)]
        for a in range(rows):
            row = source[pl.ds(row_at(a, term), 1), :]
            for t in range(tiles):
                new[a * tiles + t] += row * loaded[t]
        return tuple(new)

    return lax.fori_loop(0, count, step, start, unroll=unroll)


def contract_all(rows, cols, count, start, source, row_at, operand, operand_at):
    tiles = cols // 8
    sums = list(start)
    for term in range(count):
        loaded = [operand[tile(operand_at(term) + t * 8), :] for t in range(tiles)]
        for a in range(rows):
            row = source[pl.ds(row_at(a, term), 1), :]
            for t in range(tiles):
                sums[a * tiles + t] += row * loaded[t]
    return sums


def early_kernel(
    sizes,
    d_tri_ref,
    d_gate,
    tri_norm,
    d_update,
    *refs,
):
    rows, cols, groups = sizes
    left, right, normed, d_left, d_right, small_grads, source = refs[6:]
    cells = rows * cols
    hidden = left.shape[-1]
    channels = normed.shape[-1]
    half = lax.axis_index("col")
    zeros = (jnp.zeros((8, hidden), F32),) * (rows * cols // 8)
    source[...] = d_tri_ref[...].astype(F32)
    for n, s, p in slots(groups):
        place, part = at(p, cells), slice(s * cells, (s + 1) * cells)
        normed[place, :] = refs[n][part, :]
        left[place, :] = refs[2 + n][part, :]
        right[place, :] = refs[4 + n][part, :]

    scale = 1.0 / (rows * groups)
    small_grads[:, :channels] = dot(normed[...], d_gate[...], BY_ROWS) * scale
    small_grads[:, channels:] = dot(tri_norm[...], d_update[...], BY_ROWS) * scale
    for p in range(groups):
        sums = contract_all(
            rows,
            cols,
            cols,
            zeros,
            source,
            lambda a, j, p=p: (p * rows + a) * cols + j,
            right,
            lambda j: (half * cols + j) * cols,
        )
        for t, value in enumerate(sums):
            d_left[tile(p * cells + t * 8), :] = value

    for p in range(cols // rows):
        sums = contract_all(
            rows,
            cols,
            rows * groups,
            zeros,
            source,
            lambda a, i, p=p: i * cols + p * rows + a,
            left,
            lambda i: i * cols,
        )
        for t, value in enumerate(sums):
            d_right[tile(p * cells + t * 8), :] = value


def late_kernel(
    sizes,
    d_tri_ref,
    left,
    right,
    normed,
    d_left,
    d_right,
    *refs,
):
    rows, cols, groups = sizes
    left_gate, left_value, right_gate, right_value = refs[:2], refs[2:4], refs[4:6], refs[6:8]
    proj_grad, d_proj, source, d_right_s = refs[8:]
    cells = rows * cols
    hidden = left.shape[-1]
    half = lax.axis_index("col")
    zeros = (jnp.zeros((8, hidden), F32),) * (rows * cols // 8)
    source[...] = d_tri_ref[...].astype(F32)
    d_right_s[at(half, cols * cols), :] = d_right[...]

    def right_block(p, carry):
        sums = contract(
            rows,
            cols,
            rows * groups,
            24,
            zeros,
            source,
            lambda a, i: i * cols + p * rows + a,
            left,
            lambda i: i * cols,
        )
        start = (1 - half) * cols * cols + p * cells
        for t, value in enumerate(sums):
            d_right_s[tile(start + t * 8), :] = value
        return carry

    lax.fori_loop(0, cols // rows, right_block, 0)

    scale = 1.0 / (rows * groups)
    for n, s, p in slots(groups):
        part, place = slice(s * cells, (s + 1) * cells), at(p, cells)
        grads = d_right_s[place, :]
        d_proj[place, 2 * hidden : 3 * hidden] = (grads * right_value[n][part, :]).astype(BF16)
        d_proj[place, 3 * hidden :] = (grads * right_gate[n][part, :]).astype(BF16)
    proj_grad[:, 2 * hidden :] = dot(normed[...], d_proj[:, 2 * hidden :], BY_ROWS) * scale
    for n, s, p in slots(groups):
        start = p * cells
        sums = contract_all(
            rows,
            cols,
            cols,
            [d_left[tile(start + t * 8), :] for t in range(cells // 8)],
            source,
            lambda a, j, p=p: (p * rows + a) * cols + j,
            right,
            lambda j: ((1 - half) * cols + j) * cols,
        )
        part, place = slice(s * cells, (s + 1) * cells), at(p, cells)
        grads = jnp.concatenate(sums, axis=0)
        d_proj[place, :hidden] = (grads * left_value[n][part, :]).astype(BF16)
        d_proj[place, hidden : 2 * hidden] = (grads * left_gate[n][part, :]).astype(BF16)
    proj_grad[:, : 2 * hidden] = dot(normed[...], d_proj[:, : 2 * hidden], BY_ROWS) * scale


def outputs_kernel(
    sizes,
    params,
    pair,
    d_proj,
    d_gate,
    proj_weight,
    gate_weight,
    block_in,
    block_out,
    pair_grad,
):
    rows, cols, _ = sizes
    cells = rows * cols
    own = at(lax.axis_index("row"), cells)
    d_normed = dot(d_proj[own, :], proj_weight[...], TRANSPOSED) + dot(
        d_gate[own, :], gate_weight[...], TRANSPOSED
    )
    gain = params[0:1, :]
    _, hat, inverse = layer_norm(pair[...].astype(F32), gain, params[1:2, :])
    pair_grad[...] = norm_back(d_normed, gain, hat, inverse)
    block_out[...] = block_in[...]


def sums_kernel(
    sizes, proj_own, proj_mate, small_own, small_mate, proj_grad, gate_grad, out_grad
):
    channels = gate_grad.shape[1]
    proj_grad[...] = proj_own[...] + proj_mate[...]
    gate_grad[...] = small_own[:, :channels] + small_mate[:, :channels]
    out_grad[...] = small_own[:, channels:] + small_mate[:, channels:]


def replicated(
    pair_rep,
    cotangent,
    norm_gain,
    norm_bias,
    proj_weight,
    gate_weight,
    tri_gain,
    tri_bias,
    out_weight,
):
    rows, cols, channels = pair_rep.shape
    hidden = tri_gain.shape[0]
    groups = lax.axis_size("row")
    cells = rows * cols
    every = cells * groups
    sizes = (rows, cols, groups)

    def call(kernel, outs, *args, scratch=(), micros=1, name, **more):
        cost = pl.CostEstimate(flops=micros * 10**9, bytes_accessed=0, transcendentals=0)
        return pl.pallas_call(
            functools.partial(kernel, sizes),
            out_shape=[jax.ShapeDtypeStruct(*out) for out in outs],
            scratch_shapes=[pltpu.VMEM(*one) if isinstance(one, tuple) else one for one in scratch],
            **more,
            compiler_params=pltpu.CompilerParams(vmem_limit_bytes=VMEM_BUDGET),
            cost_estimate=cost,
            name=name,
        )(*args)

    def across(value, mask):
        return lax.ppermute(value, "row", [(i, i ^ mask) for i in range(groups)])

    def over(value):
        return lax.ppermute(value, "col", SWAP)

    def along(value):
        got, before = {}, None
        middle = groups // 4
        rest = [d for d in reversed(range(1, groups // 2)) if d != middle]
        for distance in (middle, *rest):
            arrived = across(value, 2 * distance)
            before = arrived if before is None else after(arrived, before)
            got[distance] = before
        return [got[d] for d in range(1, groups // 2)]

    def join(*values):
        return jnp.concatenate(values, axis=0)

    def after(value, *others):
        return lax.optimization_barrier((value, *others))[0]

    full = (every, hidden)

    def own_edges(side, *blocks):
        count = sum(block.shape[0] for block in blocks)
        outs = [((count + count // 2, hidden), BF16), ((count, channels), BF16)]
        outs += [((count, hidden), F32)] * 6
        kernel = functools.partial(own_edges_kernel, side)
        return call(kernel, outs, params, proj_weight, *blocks, micros=10, name="own_edges")

    def fetch(kernel, outs, given, name):
        given = [pltpu.with_memory_space_constraint(v, pltpu.HBM) for v in given]
        return call(
            kernel,
            outs,
            *given,
            scratch=[pltpu.SemaphoreType.DMA((len(given),))],
            in_specs=[pl.BlockSpec(memory_space=pltpu.HBM)] * len(given),
            name=name,
        )

    given = [pair_rep.reshape(cells, channels), cotangent.reshape(cells, channels)]
    (both,) = fetch(fetch_inputs_kernel, [((2 * cells, channels), BF16)], given, "fetch_inputs")
    got = along(both)
    given = [v[None] for v in (norm_gain, norm_bias, tri_gain, tri_bias)]
    given += [proj_weight, gate_weight, out_weight]
    outs = [((4, channels), F32)] + [(a.shape, BF16) for a in given[4:]]
    held = fetch(fetch_weights_kernel, outs, given, "fetch_weights")
    params, proj_weight, gate_weight, out_weight = held
    both_far = across(both, 1)
    near_b = after(join(*(block[:cells] for block in got)), params)
    far_b = across(near_b, 1)
    cot_b = join(*(block[cells:] for block in got))
    pair, pair_far = both[:cells], both_far[:cells]
    own_0 = own_edges(0, pair, near_b)
    mate_0 = over(own_0[0])
    cot_far_b = across(after(cot_b, own_0[0]), 1)
    cots = (both[cells:], cot_b, both_far[cells:], cot_far_b)
    own_1 = own_edges(1, pair_far, far_b)
    mate_1 = over(own_1[0])
    own = [o[1:] for o in (own_0, own_1)]
    normed = [o[0] for o in own]
    left, left_gate, left_value = ([o[n] for o in own] for n in (1, 2, 3))
    right, right_gate, right_value = ([o[n] for o in own] for n in (4, 5, 6))
    outs, picked, half_left = [(full, F32)], ((cols * cols, hidden), F32), ((every // 2, hidden), F32)
    tri = call(own_triangle_kernel, outs, *left, *right, scratch=[picked], micros=10, name="own_triangle")
    scratch = [picked, half_left, half_left]

    args = (mate_0, mate_1, *tri)
    (tri,) = call(mate_triangle_kernel, outs, *args, scratch=scratch, name="mate_triangle")
    block_out, d_tri, d_gate, tri_norm, d_update = call(
        cells_kernel,
        [((cells, channels), BF16)] + [(full, BF16)] * 4,
        params,
        tri,
        gate_weight,
        out_weight,
        *normed,
        *cots,
        micros=2,
        name="cells",
    )
    d_tri_mate = over(d_tri)
    left_all, right_all, normed_all, d_left, d_right, small_grads = call(
        early_kernel,
        [
            (full, F32),
            (full, F32),
            ((every, channels), BF16),
            (full, F32),
            ((cols * cols, hidden), F32),
            ((channels, 2 * channels), F32),
        ],
        d_tri,
        d_gate,
        tri_norm,
        d_update,
        *normed,
        *left,
        *right,
        scratch=[(full, F32)],
        micros=30,
        name="early",
    )
    proj_grad, d_proj = call(
        late_kernel,
        [((channels, 4 * hidden), F32), ((every, 4 * hidden), BF16)],
        d_tri_mate,
        left_all,
        right_all,
        normed_all,
        d_left,
        d_right,
        *left_gate,
        *left_value,
        *right_gate,
        *right_value,
        scratch=[(full, F32), (full, F32)],
        micros=40,
        name="late",
    )
    proj_mate = over(proj_grad)
    small_mate = over(after(small_grads, proj_grad))
    block_out, pair_grad = call(
        outputs_kernel,
        [((cells, channels), BF16), ((cells, channels), F32)],
        params,
        pair,
        d_proj,
        d_gate,
        proj_weight,
        gate_weight,
        block_out,
        micros=10,
        name="outputs",
    )
    square = ((channels, channels), F32)
    proj_grad, gate_grad, out_grad = call(
        sums_kernel,
        [((channels, 4 * hidden), F32), square, square],
        proj_grad,
        proj_mate,
        small_grads,
        small_mate,
        name="sums",
    )
    return (
        block_out.reshape(pair_rep.shape),
        pair_grad.reshape(pair_rep.shape),
        proj_grad,
        gate_grad,
        out_grad,
    )


def sharded(
    pair_rep,
    cotangent,
    norm_gain,
    norm_bias,
    proj_weight,
    gate_weight,
    tri_gain,
    tri_bias,
    out_weight,
):
    f32 = jnp.float32
    bf16 = jnp.bfloat16
    hidden = tri_gain.shape[0]
    channels = norm_gain.shape[0]
    row_count = pair_rep.shape[0]
    col_count = pair_rep.shape[1]
    crop_len = row_count * lax.axis_size("row")
    normed_f, pair_hat, pair_inv = layer_norm(pair_rep.astype(f32), norm_gain, norm_bias)
    normed = normed_f.astype(bf16)
    projected = jnp.einsum("ijc,cd->ijd", normed, proj_weight, preferred_element_type=f32)
    sig_left = jax.nn.sigmoid(projected[..., 0:hidden])
    val_left = projected[..., hidden : 2 * hidden]
    sig_right = jax.nn.sigmoid(projected[..., 2 * hidden : 3 * hidden])
    val_right = projected[..., 3 * hidden : 4 * hidden]
    left_edge = (sig_left * val_left).astype(bf16)
    right_edge = (sig_right * val_right).astype(bf16)
    out_gate = jax.nn.sigmoid(
        jnp.einsum("ijc,cd->ijd", normed, gate_weight, preferred_element_type=f32)
    )
    right_all = lax.all_gather(right_edge, "row", axis=0, tiled=True)
    block = right_all
    triangle = lax.psum_scatter(
        jnp.einsum("ikc,jkc->jic", left_edge, block, preferred_element_type=f32),
        "col",
        scatter_dimension=0,
        tiled=True,
    ).transpose(1, 0, 2)
    tri_f, tri_hat, tri_inv = layer_norm(triangle, tri_gain, tri_bias)
    tri_norm = tri_f.astype(bf16)
    update = jnp.einsum("ijh,hc->ijc", tri_norm, out_weight, preferred_element_type=f32)
    block_out = (out_gate * update).astype(bf16)
    cot = cotangent.astype(f32)
    d_update = (cot * out_gate).astype(bf16)
    d_gate = (cot * update * out_gate * (1.0 - out_gate)).astype(bf16)
    d_norm = jnp.einsum("ijc,hc->ijh", d_update, out_weight, preferred_element_type=f32)
    d_triangle = norm_back(d_norm, tri_gain, tri_hat, tri_inv).astype(bf16)
    tri_rows = lax.all_gather(d_triangle, "col", axis=1, tiled=True)
    d_left = jnp.einsum("ijc,jkc->ikc", tri_rows, right_all, preferred_element_type=f32)
    tri_cols = lax.all_to_all(tri_rows, "row", split_axis=1, concat_axis=0, tiled=True)
    block = tri_cols
    d_right = jnp.einsum(
        "ijc,ikc->jkc",
        block,
        lax.all_gather(left_edge, "row", axis=0, tiled=True),
        preferred_element_type=f32,
    )
    d_proj = jnp.concatenate(
        [
            d_left * val_left * sig_left * (1.0 - sig_left),
            d_left * sig_left,
            d_right * val_right * sig_right * (1.0 - sig_right),
            d_right * sig_right,
        ],
        axis=-1,
    ).astype(bf16)
    d_normed = jnp.einsum(
        "ijd,cd->ijc", d_proj, proj_weight, preferred_element_type=f32
    ) + jnp.einsum("ijd,cd->ijc", d_gate, gate_weight, preferred_element_type=f32)
    pair_grad = norm_back(d_normed, norm_gain, pair_hat, pair_inv)
    cells = row_count * col_count
    flat_norm = normed.reshape(cells, channels)
    local_proj = (
        jnp.dot(flat_norm.T, d_proj.reshape(cells, 4 * hidden), preferred_element_type=f32)
        / crop_len
    )
    local_gate = (
        jnp.dot(flat_norm.T, d_gate.reshape(cells, channels), preferred_element_type=f32) / crop_len
    )
    local_out = (
        jnp.dot(
            tri_norm.reshape(cells, hidden).T,
            d_update.reshape(cells, channels),
            preferred_element_type=f32,
        )
        / crop_len
    )
    proj_grad, gate_grad, out_grad = lax.psum((local_proj, local_gate, local_out), ("row", "col"))
    return (block_out, pair_grad, proj_grad, gate_grad, out_grad)


def local(pair_rep, *others):
    rows, cols, channels = pair_rep.shape
    hidden = others[7].shape[0]
    groups = lax.axis_size("row")
    every = rows * groups * cols
    fits = 24 * every * channels * 4 <= VMEM_BUDGET and hidden == channels
    paired = lax.axis_size("col") == 2 and groups & (groups - 1) == 0 and groups >= 8
    whole_tiles = cols % 8 == 0 and cols % (2 * rows) == 0 and rows * cols % 16 == 0
    plan = replicated if fits and paired and whole_tiles else sharded
    return plan(pair_rep, *others)


def solution(mesh):
    return jax.shard_map(
        local,
        mesh=mesh,
        in_specs=(
            P(("crop", "row"), "col", None),
            P(("crop", "row"), "col", None),
            P(),
            P(),
            P(),
            P(),
            P(),
            P(),
            P(),
        ),
        out_specs=(
            P(("crop", "row"), "col", None),
            P(("crop", "row"), "col", None),
            P("crop", None),
            P("crop", None),
            P("crop", None),
        ),
        check_vma=False,
    )
```

```python
import functools

import jax
import jax.numpy as jnp
from jax import lax
from jax.experimental import pallas as pl
from jax.experimental.pallas import tpu as pltpu
from jax.sharding import PartitionSpec as P

F32 = jnp.float32
BF16 = jnp.bfloat16
VMEM_BUDGET = 24 * 2**20
SWAP = ((0, 1), (1, 0))
NATIVE = ((1,), (0,))
BY_ROWS = ((0,), (0,))
TRANSPOSED = ((1,), (1,))


def layer_norm(values, gain, bias):
    centred = values - jnp.mean(values, axis=-1, keepdims=True)
    inverse = lax.rsqrt(jnp.mean(centred * centred, axis=-1, keepdims=True) + 1e-05)
    scaled = centred * inverse
    return (scaled * gain + bias, scaled, inverse)


def norm_back(grads, gain, scaled, inverse):
    weighted = grads * gain
    first = jnp.mean(weighted, axis=-1, keepdims=True)
    second = jnp.mean(weighted * scaled, axis=-1, keepdims=True)
    return inverse * (weighted - first - scaled * second)


def sigmoid(values):
    return 0.5 * jnp.tanh(0.5 * values) + 0.5


def dot(a, b, contract=NATIVE):
    return lax.dot_general(a, b, (contract, ((), ())), preferred_element_type=F32)


def at(index, size):
    return pl.ds(pl.multiple_of(index * size, size), size)


def tile(start):
    return pl.ds(pl.multiple_of(start, 8), 8)


def parts(groups):
    distances = tuple(range(groups // 2))
    return ((0, distances), (1, distances))


def row_block(side, distance):
    me = lax.axis_index("row")
    return lax.bitwise_xor(me, 2 * distance + side)


def slots(groups):
    found = []
    for n, (side, distances) in enumerate(parts(groups)):
        found += [(n, s, row_block(side, d)) for s, d in enumerate(distances)]
    return found


def named_slots(sizes, side, half):
    rows, cols, _ = sizes
    me = lax.axis_index("row")
    blocks = cols // rows
    found = []
    for n in range(blocks // 2):
        place = 2 * n + lax.rem(me + side, 2)
        found.append((place, lax.bitwise_xor((half * blocks + place) // 2, me // 2)))
    return found


def edges(blocks, params, proj_weight):
    hidden = proj_weight.shape[1] // 4
    values = jnp.concatenate([block[...] for block in blocks], axis=0).astype(F32)
    normed = layer_norm(values, params[0:1, :], params[1:2, :])[0].astype(BF16)
    projected = dot(normed, proj_weight[...])
    sides = []
    for start in (0, 2 * hidden):
        gate = sigmoid(projected[:, start : start + hidden])
        edge = gate * projected[:, start + hidden : start + 2 * hidden]
        sides.append((edge.astype(BF16).astype(F32), gate, edge * (1.0 - gate)))
    return normed, sides


def fetch_inputs_kernel(sizes, pair, cot, both, sems):
    cells = sizes[0] * sizes[1]
    copies = [
        pltpu.make_async_copy(pair, both.at[:cells], sems.at[0]),
        pltpu.make_async_copy(cot, both.at[cells:], sems.at[1]),
    ]
    for copy in copies:
        copy.start()
    for copy in copies:
        copy.wait()


def fetch_weights_kernel(sizes, *refs):
    given, (params, *held), sems = refs[:7], refs[7:11], refs[11]
    moves = [(v, params.at[n : n + 1]) for n, v in enumerate(given[:4])]
    moves += list(zip(given[4:], held, strict=True))
    copies = [pltpu.make_async_copy(a, b, sems.at[n]) for n, (a, b) in enumerate(moves)]
    for copy in copies:
        copy.start()
    for copy in copies:
        copy.wait()


def own_edges_kernel(side, sizes, params, weight, *refs):
    blocks, sent, normed_out, outs = refs[:-8], refs[-8], refs[-7], refs[-6:]
    normed, sides = edges(blocks, params, weight)
    normed_out[...] = normed
    for out, value in zip(outs, sides[0] + sides[1], strict=True):
        out[...] = value
    rows, cols, groups = sizes
    cells = rows * cols
    count = normed.shape[0]
    sent[:count, :] = sides[0][0].astype(BF16)
    other = 1 - lax.axis_index("col")
    for n, (_, slot) in enumerate(named_slots(sizes, side, other)):
        place = slice(count + n * cells, count + (n + 1) * cells)
        sent[place, :] = outs[3][at(slot, cells), :].astype(BF16)


def triangle_half(sizes, lefts, right_of, more, tri, picked):
    rows, cols, groups = sizes
    cells = rows * cols
    hidden = tri.shape[-1]
    half = lax.axis_index("col")
    count = cols // 8
    for n in range(2):
        for m, (place, slot) in enumerate(named_slots(sizes, n, half)):
            picked[at(place, cells), :] = right_of(n, m, slot)

    for n, s, p in slots(groups):

        if more is None:
            first = (jnp.zeros((8, hidden), F32),) * (rows * count)
        else:
            first = tuple(more[tile(p * cells + t * 8), :] for t in range(rows * count))
        sums = list(first)
        for k in range(cols):
            tiles = [picked[pl.ds(t * 8 * cols + k, 8, stride=cols), :] for t in range(count)]
            for a in range(rows):
                row = lefts[n][pl.ds((s * rows + a) * cols + k, 1), :]
                for t in range(count):
                    sums[a * count + t] += row * tiles[t]
        for t, value in enumerate(sums):
            tri[tile(p * cells + t * 8), :] = value


def own_triangle_kernel(
    sizes,
    left_0,
    left_1,
    right_0,
    right_1,
    normed_0,
    normed_1,
    gate_weight,
    tri,
    gate_0,
    gate_1,
    picked,
):
    gate_0[...] = sigmoid(dot(normed_0[...], gate_weight[...]))
    gate_1[...] = sigmoid(dot(normed_1[...], gate_weight[...]))
    rights = (right_0, right_1)
    triangle_half(
        sizes,
        (left_0, left_1),
        lambda n, m, slot: rights[n][at(slot, sizes[0] * sizes[1]), :],
        None,
        tri,
        picked,
    )


def mate_triangle_kernel(sizes, edges_0, edges_1, more, tri, picked, left_0, left_1):
    got = (edges_0, edges_1)
    lefts = (left_0, left_1)
    count = left_0.shape[0]
    for edge, left in zip(got, lefts, strict=True):
        left[...] = edge[:count, :].astype(F32)

    cells = sizes[0] * sizes[1]

    def right_of(n, m, slot):
        return got[n][count + m * cells : count + (m + 1) * cells, :].astype(F32)

    triangle_half(sizes, lefts, right_of, more, tri, picked)


def cells_kernel(
    sizes,
    params,
    tri,
    out_weight,
    *refs,
):
    rows, cols, groups = sizes
    cells = rows * cols
    gates, cots, (block_out, d_tri, d_gate, tri_norm_out, d_update_out) = (
        refs[:2],
        refs[2:6],
        refs[6:],
    )
    gain, bias = params[2:3, :], params[3:4, :]
    every = slots(groups)
    for first in range(0, groups, 4):
        chunk = every[first : first + 4]
        places = [at(p, cells) for _, _, p in chunk]
        here = jnp.concatenate([tri[place, :] for place in places], axis=0)
        tri_f, hat, inverse = layer_norm(here, gain, bias)
        tri_norm = tri_f.astype(BF16)
        update = dot(tri_norm, out_weight[...])
        n, s, _ = chunk[0]
        out_gate = gates[n][s * cells : (s + 4) * cells, :]
        if first == 0:
            block_out[...] = (out_gate[:cells] * update[:cells]).astype(BF16)
        cot = jnp.concatenate([cots[2 * n + min(s, 1)][max(s - 1, 0) * cells : max(s, 1) * cells, :] for n, s, _ in chunk], axis=0)
        gated = cot.astype(F32) * out_gate
        d_update = gated.astype(BF16)
        d_gates = (gated * update * (1.0 - out_gate)).astype(BF16)
        d_norm = dot(d_update, out_weight[...], TRANSPOSED)
        d_tris = norm_back(d_norm, gain, hat, inverse).astype(BF16)
        for t, place in enumerate(places):
            part = slice(t * cells, (t + 1) * cells)
            d_gate[place, :] = d_gates[part]
            d_tri[place, :] = d_tris[part]
            tri_norm_out[place, :] = tri_norm[part]
            d_update_out[place, :] = d_update[part]


def contract(rows, cols, count, unroll, start, source, row_at, operand, operand_at):
    tiles = cols // 8

    def step(term, sums):
        new = list(sums)
        loaded = [operand[tile(operand_at(term) + t * 8), :] for t in range(tiles)]
        for a in range(rows):
            row = source[pl.ds(row_at(a, term), 1), :]
            for t in range(tiles):
                new[a * tiles + t] += row * loaded[t]
        return tuple(new)

    return lax.fori_loop(0, count, step, start, unroll=unroll)


def contract_all(rows, cols, count, start, source, row_at, operand, operand_at):
    tiles = cols // 8
    sums = list(start)
    for term in range(count):
        loaded = [operand[tile(operand_at(term) + t * 8), :] for t in range(tiles)]
        for a in range(rows):
            row = source[pl.ds(row_at(a, term), 1), :]
            for t in range(tiles):
                sums[a * tiles + t] += row * loaded[t]
    return sums


def early_kernel(
    sizes,
    d_tri_ref,
    d_gate,
    tri_norm,
    d_update,
    *refs,
):
    rows, cols, groups = sizes
    left, right, normed, d_left, d_right, small_grads, source = refs[6:]
    cells = rows * cols
    hidden = left.shape[-1]
    channels = normed.shape[-1]
    half = lax.axis_index("col")
    zeros = (jnp.zeros((8, hidden), F32),) * (rows * cols // 8)
    source[...] = d_tri_ref[...].astype(F32)
    for n, s, p in slots(groups):
        place, part = at(p, cells), slice(s * cells, (s + 1) * cells)
        normed[place, :] = refs[n][part, :]
        left[place, :] = refs[2 + n][part, :]
        right[place, :] = refs[4 + n][part, :]

    scale = 1.0 / (rows * groups)
    small_grads[:, :channels] = dot(normed[...], d_gate[...], BY_ROWS) * scale
    small_grads[:, channels:] = dot(tri_norm[...], d_update[...], BY_ROWS) * scale
    for p in range(groups):
        sums = contract_all(
            rows,
            cols,
            cols,
            zeros,
            source,
            lambda a, j, p=p: (p * rows + a) * cols + j,
            right,
            lambda j: (half * cols + j) * cols,
        )
        for t, value in enumerate(sums):
            d_left[tile(p * cells + t * 8), :] = value

    for p in range(cols // rows):
        sums = contract_all(
            rows,
            cols,
            rows * groups,
            zeros,
            source,
            lambda a, i, p=p: i * cols + p * rows + a,
            left,
            lambda i: i * cols,
        )
        for t, value in enumerate(sums):
            d_right[tile(p * cells + t * 8), :] = value


def late_kernel(
    sizes,
    d_tri_ref,
    left,
    right,
    normed,
    d_left,
    d_right,
    *refs,
):
    rows, cols, groups = sizes
    left_gate, left_value, right_gate, right_value = refs[:2], refs[2:4], refs[4:6], refs[6:8]
    proj_grad, d_proj, source, d_right_s = refs[8:]
    cells = rows * cols
    hidden = left.shape[-1]
    half = lax.axis_index("col")
    zeros = (jnp.zeros((8, hidden), F32),) * (rows * cols // 8)
    source[...] = d_tri_ref[...].astype(F32)
    d_right_s[at(half, cols * cols), :] = d_right[...]

    def right_block(p, carry):
        sums = contract(
            rows,
            cols,
            rows * groups,
            24,
            zeros,
            source,
            lambda a, i: i * cols + p * rows + a,
            left,
            lambda i: i * cols,
        )
        start = (1 - half) * cols * cols + p * cells
        for t, value in enumerate(sums):
            d_right_s[tile(start + t * 8), :] = value
        return carry

    lax.fori_loop(0, cols // rows, right_block, 0)

    scale = 1.0 / (rows * groups)
    for n, s, p in slots(groups):
        part, place = slice(s * cells, (s + 1) * cells), at(p, cells)
        grads = d_right_s[place, :]
        d_proj[place, 2 * hidden : 3 * hidden] = (grads * right_value[n][part, :]).astype(BF16)
        d_proj[place, 3 * hidden :] = (grads * right_gate[n][part, :]).astype(BF16)
    proj_grad[:, 2 * hidden :] = dot(normed[...], d_proj[:, 2 * hidden :], BY_ROWS) * scale
    for n, s, p in slots(groups):
        start = p * cells
        sums = contract_all(
            rows,
            cols,
            cols,
            [d_left[tile(start + t * 8), :] for t in range(cells // 8)],
            source,
            lambda a, j, p=p: (p * rows + a) * cols + j,
            right,
            lambda j: ((1 - half) * cols + j) * cols,
        )
        part, place = slice(s * cells, (s + 1) * cells), at(p, cells)
        grads = jnp.concatenate(sums, axis=0)
        d_proj[place, :hidden] = (grads * left_value[n][part, :]).astype(BF16)
        d_proj[place, hidden : 2 * hidden] = (grads * left_gate[n][part, :]).astype(BF16)
    proj_grad[:, : 2 * hidden] = dot(normed[...], d_proj[:, : 2 * hidden], BY_ROWS) * scale


def outputs_kernel(
    sizes,
    params,
    pair,
    d_proj,
    d_gate,
    proj_weight,
    gate_weight,
    block_in,
    block_out,
    pair_grad,
):
    rows, cols, _ = sizes
    cells = rows * cols
    own = at(lax.axis_index("row"), cells)
    d_normed = dot(d_proj[own, :], proj_weight[...], TRANSPOSED) + dot(
        d_gate[own, :], gate_weight[...], TRANSPOSED
    )
    gain = params[0:1, :]
    _, hat, inverse = layer_norm(pair[...].astype(F32), gain, params[1:2, :])
    pair_grad[...] = norm_back(d_normed, gain, hat, inverse)
    block_out[...] = block_in[...]


def sums_kernel(
    sizes, proj_own, proj_mate, small_own, small_mate, proj_grad, gate_grad, out_grad
):
    channels = gate_grad.shape[1]
    proj_grad[...] = proj_own[...] + proj_mate[...]
    gate_grad[...] = small_own[:, :channels] + small_mate[:, :channels]
    out_grad[...] = small_own[:, channels:] + small_mate[:, channels:]


def replicated(
    pair_rep,
    cotangent,
    norm_gain,
    norm_bias,
    proj_weight,
    gate_weight,
    tri_gain,
    tri_bias,
    out_weight,
):
    rows, cols, channels = pair_rep.shape
    hidden = tri_gain.shape[0]
    groups = lax.axis_size("row")
    cells = rows * cols
    every = cells * groups
    sizes = (rows, cols, groups)

    def call(kernel, outs, *args, scratch=(), micros=1, name, **more):
        cost = pl.CostEstimate(flops=micros * 10**9, bytes_accessed=0, transcendentals=0)
        return pl.pallas_call(
            functools.partial(kernel, sizes),
            out_shape=[jax.ShapeDtypeStruct(*out) for out in outs],
            scratch_shapes=[pltpu.VMEM(*one) if isinstance(one, tuple) else one for one in scratch],
            **more,
            compiler_params=pltpu.CompilerParams(vmem_limit_bytes=VMEM_BUDGET),
            cost_estimate=cost,
            name=name,
        )(*args)

    def across(value, mask):
        return lax.ppermute(value, "row", [(i, i ^ mask) for i in range(groups)])

    def over(value):
        return lax.ppermute(value, "col", SWAP)

    def along(value):
        got, before = {}, None
        middle = groups // 4
        rest = [d for d in reversed(range(1, groups // 2)) if d != middle]
        for distance in (middle, *rest):
            arrived = across(value, 2 * distance)
            before = arrived if before is None else after(arrived, before)
            got[distance] = before
        return [got[d] for d in range(1, groups // 2)]

    def join(*values):
        return jnp.concatenate(values, axis=0)

    def after(value, *others):
        return lax.optimization_barrier((value, *others))[0]

    full = (every, hidden)

    def own_edges(side, *blocks):
        count = sum(block.shape[0] for block in blocks)
        outs = [((count + count // 2, hidden), BF16), ((count, channels), BF16)]
        outs += [((count, hidden), F32)] * 6
        kernel = functools.partial(own_edges_kernel, side)
        return call(kernel, outs, params, proj_weight, *blocks, micros=10, name="own_edges")

    def fetch(kernel, outs, given, name):
        given = [pltpu.with_memory_space_constraint(v, pltpu.HBM) for v in given]
        return call(
            kernel,
            outs,
            *given,
            scratch=[pltpu.SemaphoreType.DMA((len(given),))],
            in_specs=[pl.BlockSpec(memory_space=pltpu.HBM)] * len(given),
            name=name,
        )

    given = [pair_rep.reshape(cells, channels), cotangent.reshape(cells, channels)]
    (both,) = fetch(fetch_inputs_kernel, [((2 * cells, channels), BF16)], given, "fetch_inputs")
    got = along(both)
    given = [v[None] for v in (norm_gain, norm_bias, tri_gain, tri_bias)]
    given += [proj_weight, gate_weight, out_weight]
    outs = [((4, channels), F32)] + [(a.shape, BF16) for a in given[4:]]
    held = fetch(fetch_weights_kernel, outs, given, "fetch_weights")
    params, proj_weight, gate_weight, out_weight = held
    both_far = across(both, 1)
    near_b = after(join(*(block[:cells] for block in got)), params)
    far_b = across(near_b, 1)
    cot_b = join(*(block[cells:] for block in got))
    pair, pair_far = both[:cells], both_far[:cells]
    own_0 = own_edges(0, pair, near_b)
    mate_0 = over(own_0[0])
    cot_far_b = across(after(cot_b, own_0[0]), 1)
    cots = (both[cells:], cot_b, both_far[cells:], cot_far_b)
    own_1 = own_edges(1, pair_far, far_b)
    mate_1 = over(own_1[0])
    own = [o[1:] for o in (own_0, own_1)]
    normed = [o[0] for o in own]
    left, left_gate, left_value = ([o[n] for o in own] for n in (1, 2, 3))
    right, right_gate, right_value = ([o[n] for o in own] for n in (4, 5, 6))
    outs, picked, half_left = [(full, F32)], ((cols * cols, hidden), F32), ((every // 2, hidden), F32)
    tri, *gates = call(
        own_triangle_kernel,
        outs + [((every // 2, channels), F32)] * 2,
        *left,
        *right,
        *normed,
        gate_weight,
        scratch=[picked],
        micros=10,
        name="own_triangle",
    )
    scratch = [picked, half_left, half_left]

    args = (mate_0, mate_1, tri)
    (tri,) = call(mate_triangle_kernel, outs, *args, scratch=scratch, name="mate_triangle")
    block_out, d_tri, d_gate, tri_norm, d_update = call(
        cells_kernel,
        [((cells, channels), BF16)] + [(full, BF16)] * 4,
        params,
        tri,
        out_weight,
        *gates,
        *cots,
        micros=2,
        name="cells",
    )
    d_tri_mate = over(d_tri)
    left_all, right_all, normed_all, d_left, d_right, small_grads = call(
        early_kernel,
        [
            (full, F32),
            (full, F32),
            ((every, channels), BF16),
            (full, F32),
            ((cols * cols, hidden), F32),
            ((channels, 2 * channels), F32),
        ],
        d_tri,
        d_gate,
        tri_norm,
        d_update,
        *normed,
        *left,
        *right,
        scratch=[(full, F32)],
        micros=30,
        name="early",
    )
    proj_grad, d_proj = call(
        late_kernel,
        [((channels, 4 * hidden), F32), ((every, 4 * hidden), BF16)],
        d_tri_mate,
        left_all,
        right_all,
        normed_all,
        d_left,
        d_right,
        *left_gate,
        *left_value,
        *right_gate,
        *right_value,
        scratch=[(full, F32), (full, F32)],
        micros=40,
        name="late",
    )
    proj_mate = over(proj_grad)
    small_mate = over(after(small_grads, proj_grad))
    block_out, pair_grad = call(
        outputs_kernel,
        [((cells, channels), BF16), ((cells, channels), F32)],
        params,
        pair,
        d_proj,
        d_gate,
        proj_weight,
        gate_weight,
        block_out,
        micros=10,
        name="outputs",
    )
    square = ((channels, channels), F32)
    proj_grad, gate_grad, out_grad = call(
        sums_kernel,
        [((channels, 4 * hidden), F32), square, square],
        proj_grad,
        proj_mate,
        small_grads,
        small_mate,
        name="sums",
    )
    return (
        block_out.reshape(pair_rep.shape),
        pair_grad.reshape(pair_rep.shape),
        proj_grad,
        gate_grad,
        out_grad,
    )


def sharded(
    pair_rep,
    cotangent,
    norm_gain,
    norm_bias,
    proj_weight,
    gate_weight,
    tri_gain,
    tri_bias,
    out_weight,
):
    f32 = jnp.float32
    bf16 = jnp.bfloat16
    hidden = tri_gain.shape[0]
    channels = norm_gain.shape[0]
    row_count = pair_rep.shape[0]
    col_count = pair_rep.shape[1]
    crop_len = row_count * lax.axis_size("row")
    normed_f, pair_hat, pair_inv = layer_norm(pair_rep.astype(f32), norm_gain, norm_bias)
    normed = normed_f.astype(bf16)
    projected = jnp.einsum("ijc,cd->ijd", normed, proj_weight, preferred_element_type=f32)
    sig_left = jax.nn.sigmoid(projected[..., 0:hidden])
    val_left = projected[..., hidden : 2 * hidden]
    sig_right = jax.nn.sigmoid(projected[..., 2 * hidden : 3 * hidden])
    val_right = projected[..., 3 * hidden : 4 * hidden]
    left_edge = (sig_left * val_left).astype(bf16)
    right_edge = (sig_right * val_right).astype(bf16)
    out_gate = jax.nn.sigmoid(
        jnp.einsum("ijc,cd->ijd", normed, gate_weight, preferred_element_type=f32)
    )
    right_all = lax.all_gather(right_edge, "row", axis=0, tiled=True)
    block = right_all
    triangle = lax.psum_scatter(
        jnp.einsum("ikc,jkc->jic", left_edge, block, preferred_element_type=f32),
        "col",
        scatter_dimension=0,
        tiled=True,
    ).transpose(1, 0, 2)
    tri_f, tri_hat, tri_inv = layer_norm(triangle, tri_gain, tri_bias)
    tri_norm = tri_f.astype(bf16)
    update = jnp.einsum("ijh,hc->ijc", tri_norm, out_weight, preferred_element_type=f32)
    block_out = (out_gate * update).astype(bf16)
    cot = cotangent.astype(f32)
    d_update = (cot * out_gate).astype(bf16)
    d_gate = (cot * update * out_gate * (1.0 - out_gate)).astype(bf16)
    d_norm = jnp.einsum("ijc,hc->ijh", d_update, out_weight, preferred_element_type=f32)
    d_triangle = norm_back(d_norm, tri_gain, tri_hat, tri_inv).astype(bf16)
    tri_rows = lax.all_gather(d_triangle, "col", axis=1, tiled=True)
    d_left = jnp.einsum("ijc,jkc->ikc", tri_rows, right_all, preferred_element_type=f32)
    tri_cols = lax.all_to_all(tri_rows, "row", split_axis=1, concat_axis=0, tiled=True)
    block = tri_cols
    d_right = jnp.einsum(
        "ijc,ikc->jkc",
        block,
        lax.all_gather(left_edge, "row", axis=0, tiled=True),
        preferred_element_type=f32,
    )
    d_proj = jnp.concatenate(
        [
            d_left * val_left * sig_left * (1.0 - sig_left),
            d_left * sig_left,
            d_right * val_right * sig_right * (1.0 - sig_right),
            d_right * sig_right,
        ],
        axis=-1,
    ).astype(bf16)
    d_normed = jnp.einsum(
        "ijd,cd->ijc", d_proj, proj_weight, preferred_element_type=f32
    ) + jnp.einsum("ijd,cd->ijc", d_gate, gate_weight, preferred_element_type=f32)
    pair_grad = norm_back(d_normed, norm_gain, pair_hat, pair_inv)
    cells = row_count * col_count
    flat_norm = normed.reshape(cells, channels)
    local_proj = (
        jnp.dot(flat_norm.T, d_proj.reshape(cells, 4 * hidden), preferred_element_type=f32)
        / crop_len
    )
    local_gate = (
        jnp.dot(flat_norm.T, d_gate.reshape(cells, channels), preferred_element_type=f32) / crop_len
    )
    local_out = (
        jnp.dot(
            tri_norm.reshape(cells, hidden).T,
            d_update.reshape(cells, channels),
            preferred_element_type=f32,
        )
        / crop_len
    )
    proj_grad, gate_grad, out_grad = lax.psum((local_proj, local_gate, local_out), ("row", "col"))
    return (block_out, pair_grad, proj_grad, gate_grad, out_grad)


def local(pair_rep, *others):
    rows, cols, channels = pair_rep.shape
    hidden = others[7].shape[0]
    groups = lax.axis_size("row")
    every = rows * groups * cols
    fits = 24 * every * channels * 4 <= VMEM_BUDGET and hidden == channels
    paired = lax.axis_size("col") == 2 and groups & (groups - 1) == 0 and groups >= 8
    whole_tiles = cols % 8 == 0 and cols % (2 * rows) == 0 and rows * cols % 16 == 0
    plan = replicated if fits and paired and whole_tiles else sharded
    return plan(pair_rep, *others)


def solution(mesh):
    return jax.shard_map(
        local,
        mesh=mesh,
        in_specs=(
            P(("crop", "row"), "col", None),
            P(("crop", "row"), "col", None),
            P(),
            P(),
            P(),
            P(),
            P(),
            P(),
            P(),
        ),
        out_specs=(
            P(("crop", "row"), "col", None),
            P(("crop", "row"), "col", None),
            P("crop", None),
            P("crop", None),
            P("crop", None),
        ),
        check_vma=False,
    )
```
